32 devices in a mesh: region: 8 (over z, y), rep: 4 (over x, core).
Axes of the slice: x: 2, y: 2, z: 4, core: 2. Of those that a mesh axis runs over, the one named last changes fastest.
Arguments:
- unit_cost: float32 [16, 131072], P(None, ('region', 'rep')), may hold values from -6 to 6
- start_primal: float32 [16, 131072], P(None, ('region', 'rep')), may hold values from 0 to 0.125
- start_dual: float32 [65536], P('region'), may hold values from 0 to 1
- quota_bound: float32 [65536], P('region'), may hold values from 2 to 6
- person_slot: int32 [131072], P(('region', 'rep')), may hold values from 0 to 1023
- cell_lists: int32 [8, 8, 128], P('region'), may hold values from 0 to 511
Outputs:
- primal: float32 [16, 131072], P(None, ('region', 'rep'))
- dual: float32 [65536], P('region')
The draws below stay inside these ranges and needn't reach their ends.
Inputs may be any that keep to these rules, and one draw needn't show every extreme that they name: person_slot = d * 128 + j names slot j of the person's region's list toward owner block d.
All inputs are finite; a program needn't handle non-finite values.
Results may differ from the reference program's by a relative error of at most 0.0003.
Values sent between devices are 32-bit elements; how exact they have to be, the bound alone decides.
No kernel may reach another device: no remote copies, remote signals or barrier semaphores. Data moves between devices by JAX's collectives and lax.ppermute only.
A program may use at most 64 MiB of HBM per device.

```python
import jax
import jax.numpy as jnp
from jax import lax

OPT = 16
P_DEV = 4096
G_DEV = 512
LIST_G = 128
ITERS = 2
BISECT = 30
PERSONS = 131072
CELLS = 65536
N_REGION = 8
N_REP = 4


def plant(array, rng, least, high):
    extent = array.shape
    place = [jax.random.randint(jax.random.fold_in(rng, axis), (), 0, extent[axis]) for axis in range(len(extent))]
    array = array.at[tuple(place)].set(least)
    longest = extent.index(max(extent))
    place[longest] = (place[longest] + 1) % extent[longest]
    return array.at[tuple(place)].set(high)


def shard_levels(rng, extent, cuts, smallest, top_value):
    gain = 1.0
    for axis_at, blocks in cuts:
        draws = jax.random.uniform(jax.random.fold_in(jax.random.fold_in(rng, 6), axis_at), (blocks,), jnp.float32, smallest / len(cuts), top_value / len(cuts))
        gain = gain * jnp.repeat(jnp.exp(draws), extent[axis_at] // blocks).reshape((-1,) + (1,) * (len(extent) - 1 - axis_at))
    return gain


def normal_values(stream_key, extent, scale, limit, pieces=(), kind=jnp.bfloat16):
    factor_of = shard_levels(stream_key, extent, pieces, -0.22, 0.18) if pieces else 1.0
    values = jax.random.normal(stream_key, extent, jnp.float32) * scale * factor_of
    return jnp.minimum(jnp.maximum(values, -limit), limit).astype(kind)


def setup_inputs(seed: int = 0) -> dict:
    key_list = jax.random.split(jax.random.key(seed), 7)
    return {
        "unit_cost": normal_values(key_list[0], (OPT, PERSONS), 1.0, 6.0, ((1, 32),), jnp.float32),
        "start_primal": jnp.clip(0.125 * jax.random.uniform(key_list[1], (OPT, PERSONS), jnp.float32) ** shard_levels(key_list[1], (OPT, PERSONS), ((1, 32),), -0.2, 0.2), 0.0, 0.125),
        "start_dual": jnp.clip(1.0 * jax.random.uniform(key_list[2], (CELLS,), jnp.float32) ** shard_levels(key_list[2], (CELLS,), ((0, 8),), -0.2, 0.2), 0.0, 1.0),
        "quota_bound": jnp.clip(2.0 + 4.0 * jax.random.uniform(key_list[3], (CELLS,), jnp.float32) ** shard_levels(key_list[3], (CELLS,), ((0, 8),), -0.2, 0.2), 2.0, 6.0),
        "person_slot": plant(jax.random.randint(key_list[4], (PERSONS,), 0, N_REGION * LIST_G), jax.random.fold_in(key_list[4], 1), 0, (N_REGION * LIST_G) - 1).astype(jnp.int32),
        "cell_lists": plant(jax.random.randint(key_list[5], (N_REGION, N_REGION, LIST_G), 0, G_DEV), jax.random.fold_in(key_list[5], 1), 0, G_DEV - 1).astype(jnp.int32),
    }


PRIMAL_STEP = 0.5
DUAL_STEP = 0.25


def project_simplex(values):
    largest = jnp.max(values, axis=0)

    def bisect_once(repeat, bounds):
        low_end, high_end = bounds
        middle = 0.5 * (low_end + high_end)
        mass_sum = jnp.sum(jnp.maximum(values - middle, 0.0), axis=0)
        above = mass_sum > 1.0
        return (jnp.where(above, middle, low_end), jnp.where(above, high_end, middle))

    low_end, high_end = lax.fori_loop(0, BISECT, bisect_once, (largest - 1.0, largest))
    middle = 0.5 * (low_end + high_end)
    return jnp.maximum(values - middle, 0.0)


def reference(unit_cost, start_primal, start_dual, quota_bound, person_slot, cell_lists):
    persons = unit_cost.shape[1]
    region_of = (jnp.arange(persons, dtype=jnp.int32) // (P_DEV * N_REP)).astype(jnp.int32)
    owner = (person_slot // LIST_G).astype(jnp.int32)
    within = (person_slot % LIST_G).astype(jnp.int32)
    cell_row = (owner * G_DEV + cell_lists[owner, region_of, within]).astype(jnp.int32)
    cell_rows = N_REGION * G_DEV
    primal = start_primal
    dual = start_dual
    for repeat in range(ITERS):
        dual_rows = dual.reshape(cell_rows, OPT)
        adjoint = jnp.take(dual_rows, cell_row, axis=0).T
        fresh = project_simplex(primal - PRIMAL_STEP * (unit_cost + adjoint))
        extrapolated = 2.0 * fresh - primal
        applied = jax.ops.segment_sum(extrapolated.T, cell_row, num_segments=cell_rows).reshape(-1)
        dual = jnp.maximum(dual + DUAL_STEP * (applied - quota_bound), 0.0)
        primal = fresh
    return primal, dual
```

```python
import functools

import jax
import jax.numpy as jnp
from jax import lax
from jax.experimental import pallas as pl
from jax.experimental.pallas import tpu as pltpu
from jax.sharding import PartitionSpec as P

ITERS = 2
BISECT = 30
PRIMAL_STEP = 0.5
DUAL_STEP = 0.25
LANES = 128
SUBLANES = 8
CHUNK = 8


def sorting_network(count):
    pairs = []
    p = 1
    while p < count:
        k = p
        while k >= 1:
            for j in range(k % p, count - k, 2 * k):
                for i in range(min(k, count - j - k)):
                    if (i + j) // (2 * p) == (i + j + k) // (2 * p):
                        pairs.append((i + j, i + j + k))
            k //= 2
        p *= 2
    return pairs


def repeat_chunks(total, body, init):
    if total == 1:
        return body(0, init)
    return lax.fori_loop(0, total, body, init)


def simplex_theta(values):
    ranked = list(values)
    for a, b in sorting_network(len(values)):
        ranked[a], ranked[b] = jnp.maximum(ranked[a], ranked[b]), jnp.minimum(ranked[a], ranked[b])
    largest = ranked[0]
    total = jnp.zeros_like(largest)
    best = jnp.full_like(largest, -1.0)
    for k in range(1, len(values)):
        total = total + (ranked[k] - largest)
        best = jnp.maximum(best, (total - 1.0) * (1.0 / (k + 1)))
    cells = float(2**BISECT)
    step = jnp.maximum(jnp.ceil((best + 1.0) * cells), 1.0) - 0.5
    return (largest - 1.0) + step * (1.0 / cells)


def split_two(x):
    high = x.astype(jnp.bfloat16)
    low = (x - high.astype(jnp.float32)).astype(jnp.bfloat16)
    return high, low


def person_kernel(prices_ref, slot_ref, cost_ref, primal_ref, fresh_ref, sums_ref, x_ref, parts_ref, hot_ref):
    regions, options, _ = prices_ref.shape
    rep = sums_ref.shape[0] // regions
    rows = slot_ref.shape[0]
    halves = options // SUBLANES
    chunks = regions // CHUNK

    for g in range(rows // SUBLANES):
        slot = slot_ref[g * SUBLANES : (g + 1) * SUBLANES, :]
        owner = slot // LANES
        within = slot - owner * LANES

        def pick(chunk, found):
            found = list(found)
            for d in range(CHUNK):
                mine = owner == chunk * CHUNK + d
                for o in range(options):
                    table = jnp.broadcast_to(prices_ref[chunk * CHUNK + d, o : o + 1, :], (SUBLANES, LANES))
                    value = jnp.take_along_axis(table, within, axis=1)
                    found[o] = jnp.where(mine, value, found[o])
            return tuple(found)

        zero = jnp.zeros((SUBLANES, LANES), jnp.float32)
        adjoint = repeat_chunks(chunks, pick, (zero,) * options)
        places = []
        values = []
        for o in range(options):
            first = ((o // SUBLANES) * rows + g * SUBLANES) * SUBLANES + o % SUBLANES
            at = pl.ds(first, SUBLANES, stride=SUBLANES)
            places.append(at)
            values.append(primal_ref[at, :] - PRIMAL_STEP * (cost_ref[at, :] + adjoint[o]))
        theta = simplex_theta(values)
        for o in range(options):
            fresh = jnp.maximum(values[o] - theta, 0.0)
            fresh_ref[places[o], :] = fresh
            x_ref[places[o], :] = 2.0 * fresh - primal_ref[places[o], :]

    lane_rows = 2 * SUBLANES
    for c in range(rows):
        span = slice(c * LANES, (c + 1) * LANES)
        x = jnp.concatenate(
            [x_ref[(h * rows + c) * SUBLANES : (h * rows + c + 1) * SUBLANES, :] for h in range(halves)], axis=0
        )
        high, low = split_two(x)
        parts_ref[0:options, span] = high
        parts_ref[options : 2 * options, span] = low
        slot = jnp.broadcast_to(slot_ref[c : c + 1, :], (LANES, LANES))
        here = lax.broadcasted_iota(jnp.int32, (LANES, LANES), 0)
        hot_ref[:, span] = jnp.where((slot & (LANES - 1)) == here, 1.0, 0.0).astype(jnp.bfloat16)

    def add_up(chunk, carry):
        lines = []
        slot = jnp.concatenate([slot_ref[c : c + 1, :] for c in range(rows)], axis=1)
        owner = slot // LANES - chunk * CHUNK
        for part in range(2):
            x = parts_ref[part * options : (part + 1) * options, :]
            for d in range(CHUNK):
                mine = jnp.where(owner == d, 1.0, 0.0)
                mine = jnp.broadcast_to(mine, (options, rows * LANES)).astype(jnp.bfloat16)
                lines.append(x * mine)
        left = jnp.concatenate(lines, axis=0)
        total = lax.dot_general(
            left, hot_ref[...], (((1,), (1,)), ((), ())), preferred_element_type=jnp.float32
        )
        total = total[: CHUNK * options] + total[CHUNK * options :]
        for d in range(CHUNK):
            block = total[d * options : (d + 1) * options, :]
            for k in range(rep):
                sums_ref[(chunk * CHUNK + d) * rep + k] = block
        return carry

    repeat_chunks(chunks, add_up, 0)


def group_place(lists):
    return (lists & (SUBLANES - 1)), lists >> 3


def pick_rows(dual_blocks, lists_ref, picked_ref):
    regions = lists_ref.shape[0]
    options = picked_ref.shape[1]
    half = LANES // 2

    def one(r, carry):
        residue, column = group_place(lists_ref[pl.ds(r, 1), :])
        block = jnp.broadcast_to(residue >> 1, (options, LANES))
        lane = jnp.broadcast_to((residue & 1) * half + column, (options, LANES))
        found = jnp.zeros((options, LANES), jnp.float32)
        for b, table in enumerate(dual_blocks):
            found = jnp.where(block == b, jnp.take_along_axis(table, lane, axis=1), found)
        picked_ref[r] = found
        return carry

    if regions <= CHUNK:
        for r in range(regions):
            one(r, 0)
    else:
        lax.fori_loop(0, regions, one, 0)


def first_kernel(dual_ref, quota_ref, lists_ref, picked_ref, dual_rows_ref, quota_rows_ref):
    options = picked_ref.shape[1]
    half = LANES // 2
    both = jnp.concatenate([dual_ref[...], quota_ref[...]], axis=0).T
    left = lax.broadcasted_iota(jnp.int32, (options, LANES), 1) < half
    duals = []
    for b in range(SUBLANES // 2):
        even = both[2 * b * options : (2 * b + 1) * options, :]
        odd = both[(2 * b + 1) * options : (2 * b + 2) * options, :]
        dual = jnp.where(left, even, pltpu.roll(odd, half, 1))
        quota = jnp.where(left, pltpu.roll(even, half, 1), odd)
        dual_rows_ref[:, b * LANES : (b + 1) * LANES] = dual
        quota_rows_ref[:, b * LANES : (b + 1) * LANES] = quota
        duals.append(dual)
    pick_rows(duals, lists_ref, picked_ref)


def block_sums(arrived_ref, lists_ref, groups):
    regions = lists_ref.shape[0]
    rep = arrived_ref.shape[0] // regions
    options = arrived_ref.shape[1]
    half = groups // SUBLANES

    def add_up(chunk, total):
        highs, lows, hots = [], [], []
        here = lax.broadcasted_iota(jnp.int32, (groups, LANES), 0)
        for i in range(CHUNK):
            r = chunk * CHUNK + i
            x = arrived_ref[r * rep]
            for k in range(1, rep):
                x = x + arrived_ref[r * rep + k]
            high, low = split_two(x)
            highs.append(high)
            lows.append(low)
            residue, column = group_place(lists_ref[pl.ds(r, 1), :])
            place = jnp.broadcast_to(residue * half + column, (groups, LANES))
            hots.append(jnp.where(place == here, 1.0, 0.0).astype(jnp.bfloat16))
        left = jnp.concatenate([jnp.concatenate(highs, axis=1), jnp.concatenate(lows, axis=1)], axis=0)
        right = jnp.concatenate(hots, axis=1)
        product = lax.dot_general(left, right, (((1,), (1,)), ((), ())), preferred_element_type=jnp.float32)
        return total + product[:options] + product[options:]

    return repeat_chunks(regions // CHUNK, add_up, jnp.zeros((options, groups), jnp.float32))


def middle_kernel(arrived_ref, lists_ref, dual_rows_ref, quota_rows_ref, picked_ref, next_rows_ref):
    applied = block_sums(arrived_ref, lists_ref, dual_rows_ref.shape[1])
    dual = jnp.maximum(dual_rows_ref[...] + DUAL_STEP * (applied - quota_rows_ref[...]), 0.0)
    next_rows_ref[...] = dual
    pick_rows([dual[:, b * LANES : (b + 1) * LANES] for b in range(SUBLANES // 2)], lists_ref, picked_ref)


def last_kernel(arrived_ref, lists_ref, dual_rows_ref, quota_rows_ref, dual_ref):
    options = dual_rows_ref.shape[0]
    half = LANES // 2
    applied = block_sums(arrived_ref, lists_ref, dual_rows_ref.shape[1])
    dual = jnp.maximum(dual_rows_ref[...] + DUAL_STEP * (applied - quota_rows_ref[...]), 0.0)
    lines = []
    for b in range(SUBLANES // 2):
        block = dual[:, b * LANES : (b + 1) * LANES]
        lines.append(block)
        lines.append(pltpu.roll(block, half, 1))
    dual_ref[...] = jnp.concatenate(lines, axis=0).T[: dual_ref.shape[0], :]


def call(kernel, out_shape, scratch=()):
    return pl.pallas_call(
        kernel,
        out_shape=[jax.ShapeDtypeStruct(shape, jnp.float32) for shape in out_shape],
        scratch_shapes=list(scratch),
        compiler_params=pltpu.CompilerParams(vmem_limit_bytes=48 * 1024 * 1024),
    )


def local(unit_cost, start_primal, start_dual, quota_bound, person_slot, cell_lists):
    options, persons = unit_cost.shape
    regions = lax.axis_size("region")
    rep = lax.axis_size("rep")
    groups = quota_bound.shape[0] // options
    rows = persons // LANES
    halves = options // SUBLANES
    lists = cell_lists[0]
    slots = person_slot.reshape(rows, LANES)

    def to_tiles(x):
        x = x.reshape(halves, SUBLANES, rows, LANES).transpose(0, 2, 1, 3)
        return x.reshape(options * rows, LANES)

    def from_tiles(x):
        x = x.reshape(halves, rows, SUBLANES, LANES).transpose(0, 2, 1, 3)
        return x.reshape(options, persons)

    flat = (groups * options // LANES, LANES)
    row_shape = (options, groups)
    picked_shape = (regions, options, LANES)
    tile_shape = (options * rows, LANES)
    sums_shape = (regions * rep, options, LANES)
    scratch = (
        pltpu.VMEM(tile_shape, jnp.float32),
        pltpu.VMEM((2 * options, persons), jnp.bfloat16),
        pltpu.VMEM((LANES, persons), jnp.bfloat16),
    )
    persons_step = call(person_kernel, (tile_shape, sums_shape), scratch)

    picked, dual_rows, quota_rows = call(first_kernel, (picked_shape, row_shape, row_shape))(
        start_dual.reshape(flat), quota_bound.reshape(flat), lists
    )
    cost = to_tiles(unit_cost)
    primal = to_tiles(start_primal)
    for repeat in range(ITERS):
        prices = lax.all_to_all(picked, "region", split_axis=0, concat_axis=0, tiled=True)
        primal, sums = persons_step(prices, slots, cost, primal)
        arrived = lax.all_to_all(sums, ("region", "rep"), split_axis=0, concat_axis=0, tiled=True)
        if repeat + 1 < ITERS:
            picked, dual_rows = call(middle_kernel, (picked_shape, row_shape))(
                arrived, lists, dual_rows, quota_rows
            )
    (dual,) = call(last_kernel, (flat,))(arrived, lists, dual_rows, quota_rows)
    return (from_tiles(primal), dual.reshape(-1))


def solution(mesh):
    placed = (
        P(None, ("region", "rep")),
        P(None, ("region", "rep")),
        P("region"),
        P("region"),
        P(("region", "rep")),
        P("region", None, None),
    )
    return jax.shard_map(
        local,
        mesh=mesh,
        in_specs=placed,
        out_specs=(P(None, ("region", "rep")), P("region")),
        check_vma=False,
    )
```

```python
import functools

import jax
import jax.numpy as jnp
from jax import lax
from jax.experimental import pallas as pl
from jax.experimental.pallas import tpu as pltpu
from jax.sharding import PartitionSpec as P

ITERS = 2
BISECT = 30
PRIMAL_STEP = 0.5
DUAL_STEP = 0.25
LANES = 128
SUBLANES = 8
CHUNK = 8


def sorting_network(count):
    pairs = []
    p = 1
    while p < count:
        k = p
        while k >= 1:
            for j in range(k % p, count - k, 2 * k):
                for i in range(min(k, count - j - k)):
                    if (i + j) // (2 * p) == (i + j + k) // (2 * p):
                        pairs.append((i + j, i + j + k))
            k //= 2
        p *= 2
    return pairs


def repeat_chunks(total, body, init):
    if total == 1:
        return body(0, init)
    return lax.fori_loop(0, total, body, init)


def simplex_theta(values):
    ranked = list(values)
    for a, b in sorting_network(len(values)):
        ranked[a], ranked[b] = jnp.maximum(ranked[a], ranked[b]), jnp.minimum(ranked[a], ranked[b])
    largest = ranked[0]
    total = jnp.zeros_like(largest)
    best = jnp.full_like(largest, -1.0)
    for k in range(1, len(values)):
        total = total + (ranked[k] - largest)
        best = jnp.maximum(best, (total - 1.0) * (1.0 / (k + 1)))
    cells = float(2**BISECT)
    step = jnp.maximum(jnp.ceil((best + 1.0) * cells), 1.0) - 0.5
    return (largest - 1.0) + step * (1.0 / cells)


def split_two(x):
    high = x.astype(jnp.bfloat16)
    low = (x - high.astype(jnp.float32)).astype(jnp.bfloat16)
    return high, low


def person_kernel(options, rep, last, *refs):
    if last:
        prices_ref, share_ref, slot_ref, cost_ref, primal_ref, fresh_ref, sums_ref, x_ref, parts_ref, hot_ref = refs
        regions = share_ref.shape[0]
    else:
        prices_ref, slot_ref, cost_ref, primal_ref, fresh_ref, sums_ref, x_ref, parts_ref, hot_ref = refs
        regions = prices_ref.shape[0]
    quarter = options // rep
    rows = slot_ref.shape[0]
    halves = options // SUBLANES
    chunks = regions // CHUNK

    def price(d, o):
        if last:
            return prices_ref[d * rep + o // quarter, o % quarter : o % quarter + 1, :]
        return prices_ref[d, o : o + 1, :]

    for g in range(rows // SUBLANES):
        slot = slot_ref[g * SUBLANES : (g + 1) * SUBLANES, :]
        owner = slot // LANES
        within = slot - owner * LANES

        def pick(chunk, found):
            found = list(found)
            for d in range(CHUNK):
                mine = owner == chunk * CHUNK + d
                for o in range(options):
                    table = jnp.broadcast_to(price(chunk * CHUNK + d, o), (SUBLANES, LANES))
                    value = jnp.take_along_axis(table, within, axis=1)
                    found[o] = jnp.where(mine, value, found[o])
            return tuple(found)

        zero = jnp.zeros((SUBLANES, LANES), jnp.float32)
        adjoint = repeat_chunks(chunks, pick, (zero,) * options)
        places = []
        values = []
        for o in range(options):
            first = ((o // SUBLANES) * rows + g * SUBLANES) * SUBLANES + o % SUBLANES
            at = pl.ds(first, SUBLANES, stride=SUBLANES)
            places.append(at)
            values.append(primal_ref[at, :] - PRIMAL_STEP * (cost_ref[at, :] + adjoint[o]))
        theta = simplex_theta(values)
        for o in range(options):
            fresh = jnp.maximum(values[o] - theta, 0.0)
            fresh_ref[places[o], :] = fresh
            x_ref[places[o], :] = 2.0 * fresh - primal_ref[places[o], :]

    for c in range(rows):
        span = slice(c * LANES, (c + 1) * LANES)
        x = jnp.concatenate(
            [x_ref[(h * rows + c) * SUBLANES : (h * rows + c + 1) * SUBLANES, :] for h in range(halves)], axis=0
        )
        high, low = split_two(x)
        parts_ref[0:options, span] = high
        parts_ref[options : 2 * options, span] = low
        slot = jnp.broadcast_to(slot_ref[c : c + 1, :], (LANES, LANES))
        here = lax.broadcasted_iota(jnp.int32, (LANES, LANES), 0)
        hot_ref[:, span] = jnp.where((slot & (LANES - 1)) == here, 1.0, 0.0).astype(jnp.bfloat16)

    def add_up(chunk, carry):
        lines = []
        slot = jnp.concatenate([slot_ref[c : c + 1, :] for c in range(rows)], axis=1)
        owner = slot // LANES - chunk * CHUNK
        for part in range(2):
            x = parts_ref[part * options : (part + 1) * options, :]
            for d in range(CHUNK):
                mine = jnp.where(owner == d, 1.0, 0.0)
                mine = jnp.broadcast_to(mine, (options, rows * LANES)).astype(jnp.bfloat16)
                lines.append(x * mine)
        left = jnp.concatenate(lines, axis=0)
        total = lax.dot_general(
            left, hot_ref[...], (((1,), (1,)), ((), ())), preferred_element_type=jnp.float32
        )
        total = total[: CHUNK * options] + total[CHUNK * options :]
        for i in range(CHUNK):
            d = chunk * CHUNK + i
            block = total[i * options : (i + 1) * options, :]
            if last:
                share = jnp.where(lax.axis_index("rep") == 0, share_ref[d, options : options + SUBLANES, :], 0.0)
                held = jnp.concatenate([price(d, o) for o in range(options)], axis=0)
                block = DUAL_STEP * block + held * jnp.concatenate([share] * halves, axis=0)
            for k in range(rep):
                sums_ref[d * rep + k] = block if last else block[k * quarter : (k + 1) * quarter, :]
        return carry

    repeat_chunks(chunks, add_up, 0)


def group_place(lists):
    return (lists & (SUBLANES - 1)), lists >> 3


def each_region(regions, body):
    if regions <= CHUNK:
        for r in range(regions):
            body(r, 0)
    else:
        lax.fori_loop(0, regions, body, 0)


def pick_rows(blocks, lists_ref, r):
    lines = blocks[0].shape[0]
    residue, column = group_place(lists_ref[pl.ds(r, 1), :])
    block = jnp.broadcast_to(residue >> 1, (lines, LANES))
    lane = jnp.broadcast_to((residue & 1) * (LANES // 2) + column, (lines, LANES))
    found = jnp.zeros((lines, LANES), jnp.float32)
    for b, table in enumerate(blocks):
        found = jnp.where(block == b, jnp.take_along_axis(table, lane, axis=1), found)
    return found


def count_rows(lists_ref):
    here = lax.broadcasted_iota(jnp.int32, (SUBLANES, LANES), 0)
    there = lax.broadcasted_iota(jnp.int32, (LANES, LANES), 0)

    def add_up(chunk, total):
        lefts, rights = [], []
        for i in range(CHUNK):
            residue, column = group_place(lists_ref[pl.ds(chunk * CHUNK + i, 1), :])
            lefts.append(jnp.where(jnp.broadcast_to(residue, here.shape) == here, 1.0, 0.0).astype(jnp.bfloat16))
            rights.append(jnp.where(jnp.broadcast_to(column, there.shape) == there, 1.0, 0.0).astype(jnp.bfloat16))
        return total + lax.dot_general(
            jnp.concatenate(lefts, axis=1),
            jnp.concatenate(rights, axis=1),
            (((1,), (1,)), ((), ())),
            preferred_element_type=jnp.float32,
        )

    return repeat_chunks(lists_ref.shape[0] // CHUNK, add_up, jnp.zeros((SUBLANES, LANES), jnp.float32))


def first_kernel(options, *refs):
    sources, outs = refs[:6], refs[6:13]
    dual_ref, quota_ref, sems = refs[13:]
    picked_ref, shift_ref, base_ref, lists_ref, slot_ref, cost_ref, primal_ref = outs
    targets = (dual_ref, quota_ref, lists_ref, slot_ref, cost_ref, primal_ref)
    copies = [
        pltpu.make_async_copy(source, target, sems.at[i])
        for i, (source, target) in enumerate(zip(sources, targets))
    ]
    for copy in copies:
        copy.start()
    for copy in copies[:3]:
        copy.wait()
    half = LANES // 2
    quarter = shift_ref.shape[1]
    counts = count_rows(lists_ref)
    shares = 1.0 / jnp.maximum(counts, 1.0)
    both = jnp.concatenate([dual_ref[...], quota_ref[...]], axis=0).T
    left = lax.broadcasted_iota(jnp.int32, (options, LANES), 1) < half
    duals = []
    for b in range(SUBLANES // 2):
        span = slice(b * LANES, (b + 1) * LANES)
        even = both[2 * b * options : (2 * b + 1) * options, :]
        odd = both[(2 * b + 1) * options : (2 * b + 2) * options, :]
        dual = jnp.where(left, even, pltpu.roll(odd, half, 1))
        quota = jnp.where(left, pltpu.roll(even, half, 1), odd)
        count_even = jnp.broadcast_to(counts[2 * b : 2 * b + 1, :], (options, LANES))
        count_odd = jnp.broadcast_to(counts[2 * b + 1 : 2 * b + 2, :], (options, LANES))
        count = jnp.where(left, count_even, pltpu.roll(count_odd, half, 1))
        shift = dual - DUAL_STEP * quota
        for k in range(options // quarter):
            shift_ref[k, :, span] = shift[k * quarter : (k + 1) * quarter, :]
        alone = dual
        for _ in range(ITERS - 1):
            alone = jnp.maximum(alone - DUAL_STEP * quota, 0.0)
        base_ref[:, span] = jnp.where(count == 0.0, alone, 0.0) - DUAL_STEP * quota
        duals.append(dual)

    here = lax.broadcasted_iota(jnp.int32, (SUBLANES, LANES), 0)

    def one(r, carry):
        picked_ref[r, 0:options, :] = pick_rows(duals, lists_ref, r)
        residue, column = group_place(lists_ref[pl.ds(r, 1), :])
        share = jnp.take_along_axis(shares, jnp.broadcast_to(column, (SUBLANES, LANES)), axis=1)
        share = jnp.sum(jnp.where(residue == here, share, 0.0), axis=0, keepdims=True)
        picked_ref[r, options : options + SUBLANES, :] = jnp.broadcast_to(share, (SUBLANES, LANES))
        return carry

    each_region(lists_ref.shape[0], one)
    for copy in copies[3:]:
        copy.wait()


def block_sums(arrived_ref, lists_ref, groups):
    regions = lists_ref.shape[0]
    rep = arrived_ref.shape[0] // regions
    options = arrived_ref.shape[1]
    half = groups // SUBLANES

    def add_up(chunk, total):
        sums, hots = [], []
        here = lax.broadcasted_iota(jnp.int32, (groups, LANES), 0)
        for i in range(CHUNK):
            r = chunk * CHUNK + i
            x = arrived_ref[r * rep]
            for k in range(1, rep):
                x = x + arrived_ref[r * rep + k]
            sums.append(x)
            residue, column = group_place(lists_ref[pl.ds(r, 1), :])
            place = jnp.broadcast_to(residue * half + column, (groups, LANES))
            hots.append(jnp.where(place == here, 1.0, 0.0).astype(jnp.bfloat16))
        high, low = split_two(jnp.concatenate(sums, axis=1))
        right = jnp.concatenate(hots, axis=1)
        for part in (high, low):
            total = total + lax.dot_general(
                part, right, (((1,), (1,)), ((), ())), preferred_element_type=jnp.float32
            )
        return total

    return repeat_chunks(regions // CHUNK, add_up, jnp.zeros((options, groups), jnp.float32))


def middle_kernel(arrived_ref, lists_ref, shift_ref, picked_ref):
    regions = lists_ref.shape[0]
    rep = arrived_ref.shape[0] // regions
    applied = block_sums(arrived_ref, lists_ref, shift_ref.shape[2])
    dual = jnp.maximum(shift_ref[lax.axis_index("rep")] + DUAL_STEP * applied, 0.0)
    blocks = [dual[:, b * LANES : (b + 1) * LANES] for b in range(SUBLANES // 2)]

    def one(r, carry):
        found = pick_rows(blocks, lists_ref, r)
        for k in range(rep):
            picked_ref[r * rep + k] = found
        return carry

    each_region(regions, one)


def last_kernel(arrived_ref, lists_ref, base_ref, fresh_ref, dual_ref, primal_ref, sem):
    copy = pltpu.make_async_copy(fresh_ref, primal_ref, sem)
    copy.start()
    half = LANES // 2
    dual = jnp.maximum(base_ref[...] + block_sums(arrived_ref, lists_ref, base_ref.shape[1]), 0.0)
    lines = []
    for b in range(SUBLANES // 2):
        block = dual[:, b * LANES : (b + 1) * LANES]
        lines.append(block)
        lines.append(pltpu.roll(block, half, 1))
    dual_ref[...] = jnp.concatenate(lines, axis=0).T[: dual_ref.shape[0], :]
    copy.wait()


def call(kernel, outs, scratch=(), ins=None):
    vmem = pl.BlockSpec(memory_space=pltpu.VMEM)
    hbm = pl.BlockSpec(memory_space=pltpu.HBM)
    params = {} if ins is None else {"in_specs": [hbm if far else vmem for far in ins]}
    return pl.pallas_call(
        kernel,
        out_shape=[jax.ShapeDtypeStruct(shape, kind) for shape, kind, _ in outs],
        out_specs=[hbm if far else vmem for _, _, far in outs],
        scratch_shapes=list(scratch),
        compiler_params=pltpu.CompilerParams(vmem_limit_bytes=48 * 1024 * 1024),
        **params,
    )


def local(unit_cost, start_primal, start_dual, quota_bound, person_slot, cell_lists):
    options, persons = unit_cost.shape
    regions = lax.axis_size("region")
    rep = lax.axis_size("rep")
    quarter = options // rep
    groups = quota_bound.shape[0] // options
    rows = persons // LANES
    halves = options // SUBLANES

    def to_tiles(x):
        x = x.reshape(halves, SUBLANES, rows, LANES).transpose(0, 2, 1, 3)
        return x.reshape(options * rows, LANES)

    def from_tiles(x):
        x = x.reshape(halves, rows, SUBLANES, LANES).transpose(0, 2, 1, 3)
        return x.reshape(options, persons)

    def array(*shape, kind=jnp.float32, far=False):
        return (shape, kind, far)

    flat = (groups * options // LANES, LANES)
    tiles = array(options * rows, LANES)
    scratch = (
        pltpu.VMEM(tiles[0], jnp.float32),
        pltpu.VMEM((2 * options, persons), jnp.bfloat16),
        pltpu.VMEM((LANES, persons), jnp.bfloat16),
    )
    quarters = array(regions * rep, quarter, LANES)

    picked, shift, base, lists, slots, cost, primal = call(
        functools.partial(first_kernel, options),
        (
            array(regions, options + SUBLANES, LANES),
            array(rep, quarter, groups),
            array(options, groups),
            array(regions, LANES, kind=jnp.int32),
            array(rows, LANES, kind=jnp.int32),
            tiles,
            tiles,
        ),
        (pltpu.VMEM(flat, jnp.float32), pltpu.VMEM(flat, jnp.float32), pltpu.SemaphoreType.DMA((6,))),
        (True,) * 6,
    )(
        start_dual.reshape(flat),
        quota_bound.reshape(flat),
        cell_lists[0],
        person_slot.reshape(rows, LANES),
        to_tiles(unit_cost),
        to_tiles(start_primal),
    )
    first_prices = lax.all_to_all(picked, "region", split_axis=0, concat_axis=0, tiled=True)
    both = ("region", "rep")

    primal, sums = call(functools.partial(person_kernel, options, rep, False), (tiles, quarters), scratch)(
        first_prices, slots, cost, primal
    )
    arrived = lax.all_to_all(sums, both, split_axis=0, concat_axis=0, tiled=True)
    (picked,) = call(middle_kernel, (quarters,))(arrived, lists, shift)
    prices = lax.all_to_all(picked, both, split_axis=0, concat_axis=0, tiled=True)
    primal, sums = call(
        functools.partial(person_kernel, options, rep, True), (tiles, array(regions * rep, options, LANES)), scratch
    )(prices, first_prices, slots, cost, primal)
    arrived = lax.all_to_all(sums, both, split_axis=0, concat_axis=0, tiled=True)
    dual, primal = call(
        last_kernel,
        (array(*flat), array(options * rows, LANES, far=True)),
        (pltpu.SemaphoreType.DMA,),
    )(arrived, lists, base, primal)
    return (from_tiles(primal), dual.reshape(-1))


def solution(mesh):
    placed = (
        P(None, ("region", "rep")),
        P(None, ("region", "rep")),
        P("region"),
        P("region"),
        P(("region", "rep")),
        P("region", None, None),
    )
    return jax.shard_map(
        local,
        mesh=mesh,
        in_specs=placed,
        out_specs=(P(None, ("region", "rep")), P("region")),
        check_vma=False,
    )
```

```python
import functools

import jax
import jax.numpy as jnp
from jax import lax
from jax.experimental import pallas as pl
from jax.experimental.pallas import tpu as pltpu
from jax.sharding import PartitionSpec as P

ITERS = 2
BISECT = 30
PRIMAL_STEP = 0.5
DUAL_STEP = 0.25
LANES = 128
SUBLANES = 8
CHUNK = 8


def sorting_network(count):
    pairs = []
    p = 1
    while p < count:
        k = p
        while k >= 1:
            for j in range(k % p, count - k, 2 * k):
                for i in range(min(k, count - j - k)):
                    if (i + j) // (2 * p) == (i + j + k) // (2 * p):
                        pairs.append((i + j, i + j + k))
            k //= 2
        p *= 2
    return pairs


def repeat_chunks(total, body, init):
    if total == 1:
        return body(0, init)
    return lax.fori_loop(0, total, body, init)


def simplex_theta(values):
    ranked = list(values)
    for a, b in sorting_network(len(values)):
        ranked[a], ranked[b] = jnp.maximum(ranked[a], ranked[b]), jnp.minimum(ranked[a], ranked[b])
    largest = ranked[0]
    total = jnp.zeros_like(largest)
    best = jnp.full_like(largest, -1.0)
    for k in range(1, len(values)):
        total = total + (ranked[k] - largest)
        best = jnp.maximum(best, (total - 1.0) * (1.0 / (k + 1)))
    cells = float(2**BISECT)
    step = jnp.maximum(jnp.ceil((best + 1.0) * cells), 1.0) - 0.5
    return (largest - 1.0) + step * (1.0 / cells)


def split_two(x):
    high = x.astype(jnp.bfloat16)
    low = (x - high.astype(jnp.float32)).astype(jnp.bfloat16)
    return high, low


def person_kernel(options, rep, last, *refs):
    if last:
        prices_ref, share_ref, slot_ref, cost_ref, primal_ref, fresh_ref, sums_ref, x_ref, parts_ref, hot_ref = refs
        regions = share_ref.shape[0]
    else:
        prices_ref, slot_ref, cost_ref, primal_ref, fresh_ref, sums_ref, x_ref, parts_ref, hot_ref = refs
        regions = prices_ref.shape[0]
    quarter = options // rep
    rows = slot_ref.shape[0]
    halves = options // SUBLANES
    chunks = regions // CHUNK

    def price(d, o):
        if last:
            return prices_ref[d * rep + o // quarter, o % quarter : o % quarter + 1, :]
        return prices_ref[d, o : o + 1, :]

    for g in range(rows // SUBLANES):
        slot = slot_ref[g * SUBLANES : (g + 1) * SUBLANES, :]
        owner = slot // LANES
        within = slot - owner * LANES

        def pick(chunk, found):
            found = list(found)
            for d in range(CHUNK):
                mine = owner == chunk * CHUNK + d
                for o in range(options):
                    table = jnp.broadcast_to(price(chunk * CHUNK + d, o), (SUBLANES, LANES))
                    value = jnp.take_along_axis(table, within, axis=1)
                    found[o] = jnp.where(mine, value, found[o])
            return tuple(found)

        zero = jnp.zeros((SUBLANES, LANES), jnp.float32)
        adjoint = repeat_chunks(chunks, pick, (zero,) * options)
        places = []
        values = []
        for o in range(options):
            first = ((o // SUBLANES) * rows + g * SUBLANES) * SUBLANES + o % SUBLANES
            at = pl.ds(first, SUBLANES, stride=SUBLANES)
            places.append(at)
            values.append(primal_ref[at, :] - PRIMAL_STEP * (cost_ref[at, :] + adjoint[o]))
        theta = simplex_theta(values)
        for o in range(options):
            fresh = jnp.maximum(values[o] - theta, 0.0)
            fresh_ref[places[o], :] = fresh
            x_ref[places[o], :] = 2.0 * fresh - primal_ref[places[o], :]

    for c in range(rows):
        span = slice(c * LANES, (c + 1) * LANES)
        x = jnp.concatenate(
            [x_ref[(h * rows + c) * SUBLANES : (h * rows + c + 1) * SUBLANES, :] for h in range(halves)], axis=0
        )
        high, low = split_two(x)
        parts_ref[0:options, span] = high
        parts_ref[options : 2 * options, span] = low
        slot = jnp.broadcast_to(slot_ref[c : c + 1, :], (LANES, LANES))
        here = lax.broadcasted_iota(jnp.int32, (LANES, LANES), 0)
        hot_ref[:, span] = jnp.where((slot & (LANES - 1)) == here, 1.0, 0.0).astype(jnp.bfloat16)

    def add_up(chunk, carry):
        lines = []
        slot = jnp.concatenate([slot_ref[c : c + 1, :] for c in range(rows)], axis=1)
        owner = slot // LANES - chunk * CHUNK
        for part in range(2):
            x = parts_ref[part * options : (part + 1) * options, :]
            for d in range(CHUNK):
                mine = jnp.where(owner == d, 1.0, 0.0)
                mine = jnp.broadcast_to(mine, (options, rows * LANES)).astype(jnp.bfloat16)
                lines.append(x * mine)
        left = jnp.concatenate(lines, axis=0)
        total = lax.dot_general(
            left, hot_ref[...], (((1,), (1,)), ((), ())), preferred_element_type=jnp.float32
        )
        total = total[: CHUNK * options] + total[CHUNK * options :]
        for i in range(CHUNK):
            d = chunk * CHUNK + i
            block = total[i * options : (i + 1) * options, :]
            if last:
                share = jnp.where(lax.axis_index("rep") == 0, share_ref[d, options : options + SUBLANES, :], 0.0)
                held = jnp.concatenate([price(d, o) for o in range(options)], axis=0)
                block = DUAL_STEP * block + held * jnp.concatenate([share] * halves, axis=0)
            for k in range(rep):
                sums_ref[d * rep + k] = block if last else block[k * quarter : (k + 1) * quarter, :]
        return carry

    repeat_chunks(chunks, add_up, 0)


def group_place(lists):
    return (lists & (SUBLANES - 1)), lists >> 3


def each_region(regions, body):
    if regions <= CHUNK:
        for r in range(regions):
            body(r, 0)
    else:
        lax.fori_loop(0, regions, body, 0)


def pick_rows(blocks, lists_ref, r):
    lines = blocks[0].shape[0]
    residue, column = group_place(lists_ref[pl.ds(r, 1), :])
    block = jnp.broadcast_to(residue >> 1, (lines, LANES))
    lane = jnp.broadcast_to((residue & 1) * (LANES // 2) + column, (lines, LANES))
    found = jnp.zeros((lines, LANES), jnp.float32)
    for b, table in enumerate(blocks):
        found = jnp.where(block == b, jnp.take_along_axis(table, lane, axis=1), found)
    return found


def count_rows(lists_ref):
    here = lax.broadcasted_iota(jnp.int32, (SUBLANES, LANES), 0)
    there = lax.broadcasted_iota(jnp.int32, (LANES, LANES), 0)

    def add_up(chunk, total):
        lefts, rights = [], []
        for i in range(CHUNK):
            residue, column = group_place(lists_ref[pl.ds(chunk * CHUNK + i, 1), :])
            lefts.append(jnp.where(jnp.broadcast_to(residue, here.shape) == here, 1.0, 0.0).astype(jnp.bfloat16))
            rights.append(jnp.where(jnp.broadcast_to(column, there.shape) == there, 1.0, 0.0).astype(jnp.bfloat16))
        return total + lax.dot_general(
            jnp.concatenate(lefts, axis=1),
            jnp.concatenate(rights, axis=1),
            (((1,), (1,)), ((), ())),
            preferred_element_type=jnp.float32,
        )

    return repeat_chunks(lists_ref.shape[0] // CHUNK, add_up, jnp.zeros((SUBLANES, LANES), jnp.float32))


def first_kernel(options, *refs):
    sources, outs = refs[:6], refs[6:13]
    dual_ref, quota_ref, sems = refs[13:]
    picked_ref, shift_ref, base_ref, lists_ref, slot_ref, cost_ref, primal_ref = outs
    targets = (dual_ref, quota_ref, lists_ref, slot_ref, cost_ref, primal_ref)
    copies = [
        pltpu.make_async_copy(source, target, sems.at[i])
        for i, (source, target) in enumerate(zip(sources, targets))
    ]
    for copy in copies:
        copy.start()
    for copy in copies[:3]:
        copy.wait()
    half = LANES // 2
    quarter = shift_ref.shape[1]
    counts = count_rows(lists_ref)
    shares = 1.0 / jnp.maximum(counts, 1.0)
    both = jnp.concatenate([dual_ref[...], quota_ref[...]], axis=0).T
    left = lax.broadcasted_iota(jnp.int32, (options, LANES), 1) < half
    duals = []
    for b in range(SUBLANES // 2):
        span = slice(b * LANES, (b + 1) * LANES)
        even = both[2 * b * options : (2 * b + 1) * options, :]
        odd = both[(2 * b + 1) * options : (2 * b + 2) * options, :]
        dual = jnp.where(left, even, pltpu.roll(odd, half, 1))
        quota = jnp.where(left, pltpu.roll(even, half, 1), odd)
        count_even = jnp.broadcast_to(counts[2 * b : 2 * b + 1, :], (options, LANES))
        count_odd = jnp.broadcast_to(counts[2 * b + 1 : 2 * b + 2, :], (options, LANES))
        count = jnp.where(left, count_even, pltpu.roll(count_odd, half, 1))
        shift = dual - DUAL_STEP * quota
        for k in range(options // quarter):
            shift_ref[k, :, span] = shift[k * quarter : (k + 1) * quarter, :]
        alone = dual
        for _ in range(ITERS - 1):
            alone = jnp.maximum(alone - DUAL_STEP * quota, 0.0)
        base_ref[:, span] = jnp.where(count == 0.0, alone, 0.0) - DUAL_STEP * quota
        duals.append(dual)

    here = lax.broadcasted_iota(jnp.int32, (SUBLANES, LANES), 0)

    def one(r, carry):
        picked_ref[r, 0:options, :] = pick_rows(duals, lists_ref, r)
        residue, column = group_place(lists_ref[pl.ds(r, 1), :])
        share = jnp.take_along_axis(shares, jnp.broadcast_to(column, (SUBLANES, LANES)), axis=1)
        share = jnp.sum(jnp.where(residue == here, share, 0.0), axis=0, keepdims=True)
        picked_ref[r, options : options + SUBLANES, :] = jnp.broadcast_to(share, (SUBLANES, LANES))
        return carry

    each_region(lists_ref.shape[0], one)
    for copy in copies[3:]:
        copy.wait()


def block_sums(arrived_ref, lists_ref, groups):
    regions = lists_ref.shape[0]
    rep = arrived_ref.shape[0] // regions
    options = arrived_ref.shape[1]
    half = groups // SUBLANES

    def add_up(chunk, total):
        sums, hots = [], []
        here = lax.broadcasted_iota(jnp.int32, (groups, LANES), 0)
        for i in range(CHUNK):
            r = chunk * CHUNK + i
            x = arrived_ref[r * rep]
            for k in range(1, rep):
                x = x + arrived_ref[r * rep + k]
            sums.append(x)
            residue, column = group_place(lists_ref[pl.ds(r, 1), :])
            place = jnp.broadcast_to(residue * half + column, (groups, LANES))
            hots.append(jnp.where(place == here, 1.0, 0.0).astype(jnp.bfloat16))
        high, low = split_two(jnp.concatenate(sums, axis=1))
        right = jnp.concatenate(hots, axis=1)
        for part in (high, low):
            total = total + lax.dot_general(
                part, right, (((1,), (1,)), ((), ())), preferred_element_type=jnp.float32
            )
        return total

    return repeat_chunks(regions // CHUNK, add_up, jnp.zeros((options, groups), jnp.float32))


def middle_kernel(arrived_ref, lists_ref, shift_ref, picked_ref):
    regions = lists_ref.shape[0]
    rep = arrived_ref.shape[0] // regions
    applied = block_sums(arrived_ref, lists_ref, shift_ref.shape[2])
    dual = jnp.maximum(shift_ref[lax.axis_index("rep")] + DUAL_STEP * applied, 0.0)
    blocks = [dual[:, b * LANES : (b + 1) * LANES] for b in range(SUBLANES // 2)]

    def one(r, carry):
        found = pick_rows(blocks, lists_ref, r)
        for k in range(rep):
            picked_ref[r * rep + k] = found
        return carry

    each_region(regions, one)


def last_kernel(arrived_ref, lists_ref, base_ref, fresh_ref, dual_ref, primal_ref, flat_ref, sems):
    copy_primal = pltpu.make_async_copy(fresh_ref, primal_ref, sems.at[0])
    copy_primal.start()
    half = LANES // 2
    dual = jnp.maximum(base_ref[...] + block_sums(arrived_ref, lists_ref, base_ref.shape[1]), 0.0)
    lines = []
    for b in range(SUBLANES // 2):
        block = dual[:, b * LANES : (b + 1) * LANES]
        lines.append(block)
        lines.append(pltpu.roll(block, half, 1))
    flat_ref[...] = jnp.concatenate(lines, axis=0).T[: flat_ref.shape[0], :]
    copy_dual = pltpu.make_async_copy(flat_ref, dual_ref, sems.at[1])
    copy_dual.start()
    copy_primal.wait()
    copy_dual.wait()


def call(kernel, outs, scratch=(), ins=None):
    vmem = pl.BlockSpec(memory_space=pltpu.VMEM)
    hbm = pl.BlockSpec(memory_space=pltpu.HBM)
    params = {} if ins is None else {"in_specs": [hbm if far else vmem for far in ins]}
    return pl.pallas_call(
        kernel,
        out_shape=[jax.ShapeDtypeStruct(shape, kind) for shape, kind, _ in outs],
        out_specs=[hbm if far else vmem for _, _, far in outs],
        scratch_shapes=list(scratch),
        compiler_params=pltpu.CompilerParams(vmem_limit_bytes=48 * 1024 * 1024),
        **params,
    )


def local(unit_cost, start_primal, start_dual, quota_bound, person_slot, cell_lists):
    options, persons = unit_cost.shape
    regions = lax.axis_size("region")
    rep = lax.axis_size("rep")
    quarter = options // rep
    groups = quota_bound.shape[0] // options
    rows = persons // LANES
    halves = options // SUBLANES

    def to_tiles(x):
        x = x.reshape(halves, SUBLANES, rows, LANES).transpose(0, 2, 1, 3)
        return x.reshape(options * rows, LANES)

    def from_tiles(x):
        x = x.reshape(halves, rows, SUBLANES, LANES).transpose(0, 2, 1, 3)
        return x.reshape(options, persons)

    def array(*shape, kind=jnp.float32, far=False):
        return (shape, kind, far)

    flat = (groups * options // LANES, LANES)
    tiles = array(options * rows, LANES)
    scratch = (
        pltpu.VMEM(tiles[0], jnp.float32),
        pltpu.VMEM((2 * options, persons), jnp.bfloat16),
        pltpu.VMEM((LANES, persons), jnp.bfloat16),
    )
    quarters = array(regions * rep, quarter, LANES)

    picked, shift, base, lists, slots, cost, primal = call(
        functools.partial(first_kernel, options),
        (
            array(regions, options + SUBLANES, LANES),
            array(rep, quarter, groups),
            array(options, groups),
            array(regions, LANES, kind=jnp.int32),
            array(rows, LANES, kind=jnp.int32),
            tiles,
            tiles,
        ),
        (pltpu.VMEM(flat, jnp.float32), pltpu.VMEM(flat, jnp.float32), pltpu.SemaphoreType.DMA((6,))),
        (True,) * 6,
    )(
        *(
            pltpu.with_memory_space_constraint(x, pltpu.HBM)
            for x in (
                start_dual.reshape(flat),
                quota_bound.reshape(flat),
                cell_lists[0],
                person_slot.reshape(rows, LANES),
                to_tiles(unit_cost),
                to_tiles(start_primal),
            )
        )
    )
    first_prices = lax.all_to_all(picked, "region", split_axis=0, concat_axis=0, tiled=True)
    both = ("region", "rep")

    primal, sums = call(functools.partial(person_kernel, options, rep, False), (tiles, quarters), scratch)(
        first_prices, slots, cost, primal
    )
    arrived = lax.all_to_all(sums, both, split_axis=0, concat_axis=0, tiled=True)
    (picked,) = call(middle_kernel, (quarters,))(arrived, lists, shift)
    prices = lax.all_to_all(picked, both, split_axis=0, concat_axis=0, tiled=True)
    primal, sums = call(
        functools.partial(person_kernel, options, rep, True), (tiles, array(regions * rep, options, LANES)), scratch
    )(prices, first_prices, slots, cost, primal)
    arrived = lax.all_to_all(sums, both, split_axis=0, concat_axis=0, tiled=True)
    dual, primal = call(
        last_kernel,
        (array(*flat, far=True), array(options * rows, LANES, far=True)),
        (pltpu.VMEM(flat, jnp.float32), pltpu.SemaphoreType.DMA((2,))),
    )(arrived, lists, base, primal)
    return (from_tiles(primal), dual.reshape(-1))


def solution(mesh):
    placed = (
        P(None, ("region", "rep")),
        P(None, ("region", "rep")),
        P("region"),
        P("region"),
        P(("region", "rep")),
        P("region", None, None),
    )
    return jax.shard_map(
        local,
        mesh=mesh,
        in_specs=placed,
        out_specs=(P(None, ("region", "rep")), P("region")),
        check_vma=False,
    )
```

```python
import functools

import jax
import jax.numpy as jnp
from jax import lax
from jax.experimental import pallas as pl
from jax.experimental.pallas import tpu as pltpu
from jax.sharding import PartitionSpec as P

ITERS = 2
BISECT = 30
PRIMAL_STEP = 0.5
DUAL_STEP = 0.25
LANES = 128
SUBLANES = 8
CHUNK = 8
PACKED = 16
WIDE = 256
BLOCKS = 4
VMEM_LIMIT = 48 * 1024 * 1024


def sorting_network(count):
    pairs = []
    p = 1
    while p < count:
        k = p
        while k >= 1:
            for j in range(k % p, count - k, 2 * k):
                for i in range(min(k, count - j - k)):
                    if (i + j) // (2 * p) == (i + j + k) // (2 * p):
                        pairs.append((i + j, i + j + k))
            k //= 2
        p *= 2
    return pairs


def repeat_chunks(total, body, init):
    if total == 1:
        return body(0, init)
    return lax.fori_loop(0, total, body, init)


def simplex_theta(values):
    ranked = list(values)
    for a, b in sorting_network(len(values)):
        ranked[a], ranked[b] = jnp.maximum(ranked[a], ranked[b]), jnp.minimum(ranked[a], ranked[b])
    largest = ranked[0]
    total = jnp.zeros_like(largest)
    best = jnp.full_like(largest, -1.0)
    for k in range(1, len(values)):
        total = total + (ranked[k] - largest)
        best = jnp.maximum(best, (total - 1.0) * (1.0 / (k + 1)))
    cells = float(2**BISECT)
    step = jnp.maximum(jnp.ceil((best + 1.0) * cells), 1.0) - 0.5
    return (largest - 1.0) + step * (1.0 / cells)


def split_two(x):
    high = x.astype(jnp.bfloat16)
    low = (x - high.astype(jnp.float32)).astype(jnp.bfloat16)
    return high, low


def one_hot(index, count):
    wide = jnp.broadcast_to(index.astype(jnp.float32), (PACKED, index.shape[1])).astype(jnp.bfloat16)
    lines = []
    for first in range(0, count, PACKED):
        here = lax.broadcasted_iota(jnp.int32, wide.shape, 0) + first
        hit = wide == here.astype(jnp.float32).astype(jnp.bfloat16)
        lines.append(jnp.where(hit, jnp.bfloat16(1), jnp.bfloat16(0)))
    return jnp.concatenate(lines, axis=0)


def product(left, right):
    return lax.dot_general(left, right, (((1,), (1,)), ((), ())), preferred_element_type=jnp.float32)


def group_place(lists):
    return (lists & (SUBLANES - 1)) >> 1, (lists & 1) * (LANES // 2) + (lists >> 3)


def each_region(regions, body):
    if regions <= CHUNK:
        for r in range(regions):
            body(r, 0)
    else:
        lax.fori_loop(0, regions, body, 0)


def first_kernel(options, dual_far, lists_far, picked_ref, rows_ref, counts_ref, lists_ref, dual_ref, sems):
    copies = [
        pltpu.make_async_copy(dual_far, dual_ref, sems.at[0]),
        pltpu.make_async_copy(lists_far, lists_ref, sems.at[1]),
    ]
    for copy in copies:
        copy.start()
    for copy in copies:
        copy.wait()
    half = LANES // 2
    regions = lists_ref.shape[0]
    there = lax.broadcasted_iota(jnp.int32, (LANES, LANES), 0)
    which = lax.broadcasted_iota(jnp.int32, (SUBLANES, LANES), 0)

    def count_up(chunk, total):
        lefts, rights = [], []
        for i in range(CHUNK):
            block, lane = group_place(lists_ref[pl.ds(chunk * CHUNK + i, 1), :])
            lefts.append(jnp.where(block == which, 1.0, 0.0).astype(jnp.bfloat16))
            rights.append(jnp.where(lane == there, 1.0, 0.0).astype(jnp.bfloat16))
        return total + product(jnp.concatenate(lefts, axis=1), jnp.concatenate(rights, axis=1))

    counts = repeat_chunks(regions // CHUNK, count_up, jnp.zeros((SUBLANES, LANES), jnp.float32))
    counts_ref[...] = counts
    shares = 1.0 / jnp.maximum(counts, 1.0)

    flat = dual_ref[...]
    turned = jnp.concatenate([flat, flat], axis=0).T
    left = lax.broadcasted_iota(jnp.int32, (options, LANES), 1) < half
    duals = []
    for b in range(BLOCKS):
        even = turned[2 * b * options : (2 * b + 1) * options, :]
        odd = turned[(2 * b + 1) * options : (2 * b + 2) * options, :]
        dual = jnp.where(left, even, odd)
        rows_ref[b] = dual
        duals.append(dual)

    def one(r, carry):
        block, lane = group_place(lists_ref[pl.ds(r, 1), :])
        wide_block = jnp.broadcast_to(block, (options, LANES))
        wide_lane = jnp.broadcast_to(lane, (options, LANES))
        found = jnp.take_along_axis(duals[0], wide_lane, axis=1)
        for b in range(1, BLOCKS):
            found = jnp.where(wide_block == b, jnp.take_along_axis(duals[b], wide_lane, axis=1), found)
        picked_ref[r, 0:options, :] = found
        share = jnp.take_along_axis(shares, wide_lane[:SUBLANES], axis=1)
        share = jnp.sum(jnp.where(block == which, share, 0.0), axis=0, keepdims=True)
        picked_ref[r, options : options + SUBLANES, :] = jnp.broadcast_to(share, (SUBLANES, LANES))
        return carry

    each_region(regions, one)


def prepare_kernel(options, *refs):
    far, (rows_ref, counts_ref, lists_ref), outs, (quota_ref, sems) = refs[:4], refs[4:7], refs[7:16], refs[16:]
    slot_ref, cost_ref, primal_ref, shift_ref, base_ref, hot_ref, owner_ref, place_ref, block_ref = outs
    copies = [
        pltpu.make_async_copy(source, target, sems.at[i])
        for i, (source, target) in enumerate(zip(far, (slot_ref, quota_ref, cost_ref, primal_ref)))
    ]
    for copy in copies:
        copy.start()
    half = LANES // 2
    regions = lists_ref.shape[0]
    rows = slot_ref.shape[0]
    quarter = shift_ref.shape[1] // BLOCKS

    def lists_row(r, carry):
        block, lane = group_place(lists_ref[pl.ds(r, 1), :])
        place_ref[r] = one_hot(lane, LANES)
        block_ref[r] = jnp.broadcast_to(block, (SUBLANES, LANES))
        return carry

    each_region(regions, lists_row)
    copies[0].wait()
    for c in range(rows):
        span = slice(c * LANES, (c + 1) * LANES)
        slot = slot_ref[c : c + 1, :]
        hot_ref[:, span] = one_hot(slot & (WIDE - 1), WIDE)
        owner = jnp.broadcast_to((slot // WIDE).astype(jnp.float32), (PACKED, LANES))
        owner_ref[:, span] = owner.astype(jnp.bfloat16)
    copies[1].wait()
    flat = quota_ref[...]
    turned = jnp.concatenate([flat, flat], axis=0).T
    left = lax.broadcasted_iota(jnp.int32, (options, LANES), 1) < half
    for b in range(BLOCKS):
        even = turned[2 * b * options : (2 * b + 1) * options, :]
        odd = turned[(2 * b + 1) * options : (2 * b + 2) * options, :]
        pull = DUAL_STEP * jnp.where(left, even, odd)
        dual = rows_ref[b]
        shift = dual - pull
        for k in range(options // quarter):
            shift_ref[k, b * quarter : (b + 1) * quarter, :] = shift[k * quarter : (k + 1) * quarter, :]
        alone = dual
        for _ in range(ITERS - 1):
            alone = jnp.maximum(alone - pull, 0.0)
        named = jnp.broadcast_to(counts_ref[b : b + 1, :], alone.shape) > 0.0
        base_ref[b] = jnp.where(named, 0.0, alone) - pull
    for copy in copies[2:]:
        copy.wait()


def person_kernel(options, rep, last, *refs):
    if last:
        prices_ref, share_ref = refs[:2]
        regions = share_ref.shape[0]
    else:
        (prices_ref,) = refs[:1]
        regions = prices_ref.shape[0]
    slot_ref, cost_ref, primal_ref, hot_ref, owner_ref, fresh_ref, sums_ref, x_ref, parts_ref = refs[-9:]
    quarter = options // rep
    rows = slot_ref.shape[0]
    halves = options // SUBLANES
    chunks = regions // CHUNK
    blocks = CHUNK * LANES // WIDE
    groups = rows // SUBLANES
    stretch = SUBLANES * LANES

    def price(d, o):
        if last:
            return prices_ref[d * rep + o // quarter, o % quarter : o % quarter + 1, :]
        return prices_ref[d, o : o + 1, :]

    def partial_sums(chunk, g):
        span = slice(g * stretch, (g + 1) * stretch)
        owner = owner_ref[:, span]
        lines = []
        for part in range(2):
            x = parts_ref[part * options : (part + 1) * options, span]
            for e in range(blocks):
                number = jnp.asarray(chunk * blocks + e, jnp.float32).astype(jnp.bfloat16)
                lines.append(jnp.where(owner == number, x, jnp.bfloat16(0)))
        return product(jnp.concatenate(lines, axis=0), hot_ref[:, span])

    def hand_on(chunk, total):
        total = total[: blocks * options] + total[blocks * options :]
        for i in range(CHUNK):
            d = chunk * CHUNK + i
            e, h = divmod(i, WIDE // LANES)
            block = total[e * options : (e + 1) * options, h * LANES : (h + 1) * LANES]
            if last:
                share = jnp.where(lax.axis_index("rep") == 0, share_ref[d, options : options + SUBLANES, :], 0.0)
                held = jnp.concatenate([price(d, o) for o in range(options)], axis=0)
                block = DUAL_STEP * block + held * jnp.concatenate([share] * halves, axis=0)
            for k in range(rep):
                sums_ref[d * rep + k] = block if last else block[k * quarter : (k + 1) * quarter, :]

    total = None
    for g in range(groups):
        slot = slot_ref[g * SUBLANES : (g + 1) * SUBLANES, :]
        owner = slot // LANES
        within = slot - owner * LANES

        def pick(chunk, found):
            found = list(found)
            for d in range(CHUNK):
                mine = owner == chunk * CHUNK + d
                for o in range(options):
                    table = jnp.broadcast_to(price(chunk * CHUNK + d, o), (SUBLANES, LANES))
                    value = jnp.take_along_axis(table, within, axis=1)
                    found[o] = jnp.where(mine, value, found[o])
            return tuple(found)

        zero = jnp.zeros((SUBLANES, LANES), jnp.float32)
        adjoint = repeat_chunks(chunks, pick, (zero,) * options)
        places = []
        values = []
        for o in range(options):
            first = ((o // SUBLANES) * rows + g * SUBLANES) * SUBLANES + o % SUBLANES
            at = pl.ds(first, SUBLANES, stride=SUBLANES)
            places.append(at)
            values.append(primal_ref[at, :] - PRIMAL_STEP * (cost_ref[at, :] + adjoint[o]))
        theta = simplex_theta(values)
        for o in range(options):
            fresh = jnp.maximum(values[o] - theta, 0.0)
            fresh_ref[places[o], :] = fresh
            x_ref[places[o], :] = 2.0 * fresh - primal_ref[places[o], :]
        for c in range(g * SUBLANES, (g + 1) * SUBLANES):
            span = slice(c * LANES, (c + 1) * LANES)
            x = jnp.concatenate(
                [x_ref[(h * rows + c) * SUBLANES : (h * rows + c + 1) * SUBLANES, :] for h in range(halves)], axis=0
            )
            high, low = split_two(x)
            parts_ref[0:options, span] = high
            parts_ref[options : 2 * options, span] = low
        if chunks == 1:
            found = partial_sums(0, g)
            total = found if total is None else total + found

    if chunks == 1:
        hand_on(0, total)
    else:

        def add_up(chunk, carry):
            total = partial_sums(chunk, 0)
            for g in range(1, groups):
                total = total + partial_sums(chunk, g)
            hand_on(chunk, total)
            return carry

        lax.fori_loop(0, chunks, add_up, 0)


def block_sums(arrived_ref, place_ref, block_ref):
    regions = place_ref.shape[0]
    rep = arrived_ref.shape[0] // regions
    options = arrived_ref.shape[1]
    lines = BLOCKS * options
    copies = max(1, SUBLANES // options)
    tall = copies * options
    row = lax.broadcasted_iota(jnp.int32, (tall, CHUNK * LANES), 0) // options

    def add_up(chunk, total):
        sums, hots, numbers = [], [], []
        for i in range(CHUNK):
            r = chunk * CHUNK + i
            x = arrived_ref[r * rep]
            for k in range(1, rep):
                x = x + arrived_ref[r * rep + k]
            sums.append(jnp.concatenate([x] * copies, axis=0))
            hots.append(place_ref[r])
            numbers.append(jnp.concatenate([block_ref[r]] * (tall // SUBLANES), axis=0))
        x = jnp.concatenate(sums, axis=1)
        number = jnp.concatenate(numbers, axis=1) - row
        high = x.astype(jnp.bfloat16).astype(jnp.float32)
        left = [
            jnp.where(number == first, part, 0.0) for part in (high, x - high) for first in range(0, BLOCKS, copies)
        ]
        found = product(jnp.concatenate(left, axis=0).astype(jnp.bfloat16), jnp.concatenate(hots, axis=1))
        return total + found[:lines] + found[lines:]

    return repeat_chunks(regions // CHUNK, add_up, jnp.zeros((lines, LANES), jnp.float32))


def middle_kernel(arrived_ref, lists_ref, place_ref, block_ref, shift_ref, picked_ref):
    regions = lists_ref.shape[0]
    rep = arrived_ref.shape[0] // regions
    options = arrived_ref.shape[1]
    applied = block_sums(arrived_ref, place_ref, block_ref)
    dual = jnp.maximum(shift_ref[lax.axis_index("rep")] + DUAL_STEP * applied, 0.0)
    blocks = [dual[b * options : (b + 1) * options, :] for b in range(BLOCKS)]

    def one(r, carry):
        block, lane = group_place(lists_ref[pl.ds(r, 1), :])
        block = jnp.broadcast_to(block, (options, LANES))
        lane = jnp.broadcast_to(lane, (options, LANES))
        found = jnp.take_along_axis(blocks[0], lane, axis=1)
        for b in range(1, BLOCKS):
            found = jnp.where(block == b, jnp.take_along_axis(blocks[b], lane, axis=1), found)
        for k in range(rep):
            picked_ref[r * rep + k] = found
        return carry

    each_region(regions, one)


def last_kernel(arrived_ref, place_ref, block_ref, base_ref, dual_ref):
    options = base_ref.shape[1]
    sums = block_sums(arrived_ref, place_ref, block_ref)
    lines = []
    for b in range(BLOCKS):
        block = jnp.maximum(base_ref[b] + sums[b * options : (b + 1) * options, :], 0.0)
        lines.append(block)
        lines.append(pltpu.roll(block, LANES // 2, 1))
    dual_ref[...] = jnp.concatenate(lines, axis=0).T[: dual_ref.shape[0], :]


def write_kernel(fresh_ref, primal_far, sem):
    copy = pltpu.make_async_copy(fresh_ref, primal_far, sem)
    copy.start()
    copy.wait()


def call(kernel, outs, scratch=(), ins=None):
    vmem = pl.BlockSpec(memory_space=pltpu.VMEM)
    hbm = pl.BlockSpec(memory_space=pltpu.HBM)
    params = {} if ins is None else {"in_specs": [hbm if far else vmem for far in ins]}
    return pl.pallas_call(
        kernel,
        out_shape=[jax.ShapeDtypeStruct(shape, kind) for shape, kind, _ in outs],
        out_specs=[hbm if far else vmem for _, _, far in outs],
        scratch_shapes=list(scratch),
        compiler_params=pltpu.CompilerParams(vmem_limit_bytes=VMEM_LIMIT),
        **params,
    )


def far(x):
    return pltpu.with_memory_space_constraint(x, pltpu.HBM)


def local(unit_cost, start_primal, start_dual, quota_bound, person_slot, cell_lists):
    options, persons = unit_cost.shape
    regions = lax.axis_size("region")
    rep = lax.axis_size("rep")
    quarter = options // rep
    groups = quota_bound.shape[0] // options
    rows = persons // LANES
    halves = options // SUBLANES

    def to_tiles(x):
        x = x.reshape(halves, SUBLANES, rows, LANES).transpose(0, 2, 1, 3)
        return x.reshape(options * rows, LANES)

    def from_tiles(x):
        x = x.reshape(halves, rows, SUBLANES, LANES).transpose(0, 2, 1, 3)
        return x.reshape(options, persons)

    def array(*shape, kind=jnp.float32, far=False):
        return (shape, kind, far)

    flat = (groups * options // LANES, LANES)
    tiles = array(options * rows, LANES)
    block_rows = array(BLOCKS, options, LANES)
    quarters = array(regions * rep, quarter, LANES)
    wholes = array(regions * rep, options, LANES)
    both = ("region", "rep")
    exchange = functools.partial(lax.all_to_all, split_axis=0, concat_axis=0, tiled=True)

    picked, dual_rows, counts, lists = call(
        functools.partial(first_kernel, options),
        (
            array(regions, options + SUBLANES, LANES),
            block_rows,
            array(SUBLANES, LANES),
            array(regions, LANES, kind=jnp.int32),
        ),
        (pltpu.VMEM(flat, jnp.float32), pltpu.SemaphoreType.DMA((2,))),
        (True, True),
    )(far(start_dual.reshape(flat)), far(cell_lists[0]))
    first_prices = exchange(picked, "region")
    slots, cost, primal, shift, base, hot, owner, place, block = call(
        functools.partial(prepare_kernel, options),
        (
            array(rows, LANES, kind=jnp.int32),
            tiles,
            tiles,
            array(rep, BLOCKS * quarter, LANES),
            block_rows,
            array(WIDE, persons, kind=jnp.bfloat16),
            array(PACKED, persons, kind=jnp.bfloat16),
            array(regions, LANES, LANES, kind=jnp.bfloat16),
            array(regions, SUBLANES, LANES, kind=jnp.int32),
        ),
        (pltpu.VMEM(flat, jnp.float32), pltpu.SemaphoreType.DMA((4,))),
        (True,) * 4 + (False,) * 3,
    )(
        far(person_slot.reshape(rows, LANES)),
        far(quota_bound.reshape(flat)),
        far(to_tiles(unit_cost)),
        far(to_tiles(start_primal)),
        dual_rows,
        counts,
        lists,
    )
    scratch = (pltpu.VMEM(tiles[0], jnp.float32), pltpu.VMEM((2 * options, persons), jnp.bfloat16))

    primal, sums = call(functools.partial(person_kernel, options, rep, False), (tiles, quarters), scratch)(
        first_prices, slots, cost, primal, hot, owner
    )
    arrived = exchange(sums, both)
    (picked,) = call(middle_kernel, (quarters,))(arrived, lists, place, block, shift)
    prices = exchange(picked, both)
    primal, sums = call(functools.partial(person_kernel, options, rep, True), (tiles, wholes), scratch)(
        prices, first_prices, slots, cost, primal, hot, owner
    )
    arrived = exchange(sums, both)
    (primal,) = call(write_kernel, (array(*tiles[0], far=True),), (pltpu.SemaphoreType.DMA,))(primal)
    (dual,) = call(last_kernel, (array(*flat),))(arrived, place, block, base)
    return (from_tiles(primal), dual.reshape(-1))


def solution(mesh):
    placed = (
        P(None, ("region", "rep")),
        P(None, ("region", "rep")),
        P("region"),
        P("region"),
        P(("region", "rep")),
        P("region", None, None),
    )
    return jax.shard_map(
        local,
        mesh=mesh,
        in_specs=placed,
        out_specs=(P(None, ("region", "rep")), P("region")),
        check_vma=False,
    )
```

```python
import functools

import jax
import jax.numpy as jnp
from jax import lax
from jax.experimental import pallas as pl
from jax.experimental.pallas import tpu as pltpu
from jax.sharding import PartitionSpec as P

ITERS = 2
BISECT = 30
PRIMAL_STEP = 0.5
DUAL_STEP = 0.25
LANES = 128
SUBLANES = 8
CHUNK = 8
PACKED = 16
WIDE = 256
BLOCKS = 4
VMEM_LIMIT = 48 * 1024 * 1024


def sorting_network(count):
    pairs = []
    p = 1
    while p < count:
        k = p
        while k >= 1:
            for j in range(k % p, count - k, 2 * k):
                for i in range(min(k, count - j - k)):
                    if (i + j) // (2 * p) == (i + j + k) // (2 * p):
                        pairs.append((i + j, i + j + k))
            k //= 2
        p *= 2
    return pairs


def repeat_chunks(total, body, init):
    if total == 1:
        return body(0, init)
    return lax.fori_loop(0, total, body, init)


def simplex_theta(values):
    ranked = list(values)
    for a, b in sorting_network(len(values)):
        ranked[a], ranked[b] = jnp.maximum(ranked[a], ranked[b]), jnp.minimum(ranked[a], ranked[b])
    largest = ranked[0]
    total = jnp.zeros_like(largest)
    best = jnp.full_like(largest, -1.0)
    for k in range(1, len(values)):
        total = total + (ranked[k] - largest)
        best = jnp.maximum(best, (total - 1.0) * (1.0 / (k + 1)))
    cells = float(2**BISECT)
    step = jnp.maximum(jnp.ceil((best + 1.0) * cells), 1.0) - 0.5
    return (largest - 1.0) + step * (1.0 / cells)


def split_two(x):
    high = x.astype(jnp.bfloat16)
    low = (x - high.astype(jnp.float32)).astype(jnp.bfloat16)
    return high, low


def one_hot(index, count):
    wide = jnp.broadcast_to(index.astype(jnp.float32), (PACKED, index.shape[1])).astype(jnp.bfloat16)
    lines = []
    for first in range(0, count, PACKED):
        here = lax.broadcasted_iota(jnp.int32, wide.shape, 0) + first
        hit = wide == here.astype(jnp.float32).astype(jnp.bfloat16)
        lines.append(jnp.where(hit, jnp.bfloat16(1), jnp.bfloat16(0)))
    return jnp.concatenate(lines, axis=0)


def product(left, right):
    return lax.dot_general(left, right, (((1,), (1,)), ((), ())), preferred_element_type=jnp.float32)


def group_place(lists):
    return (lists & (SUBLANES - 1)) >> 1, (lists & 1) * (LANES // 2) + (lists >> 3)


def each_region(regions, body):
    if regions <= CHUNK:
        for r in range(regions):
            body(r, 0)
    else:
        lax.fori_loop(0, regions, body, 0)


def turn_rows(flat, options):
    turned = jnp.concatenate([flat, flat], axis=0).T
    left = lax.broadcasted_iota(jnp.int32, (options, LANES), 1) < LANES // 2
    pairs = [turned[i * options : (i + 1) * options, :] for i in range(2 * BLOCKS)]
    return [jnp.where(left, pairs[2 * b], pairs[2 * b + 1]) for b in range(BLOCKS)]


def first_kernel(options, *refs):
    far, outs, (dual_ref, quota_ref, sems) = refs[:6], refs[6:13], refs[13:]
    picked_ref, shift_ref, base_ref, lists_ref, slot_ref, cost_ref, primal_ref = outs
    targets = (lists_ref, dual_ref, quota_ref, slot_ref, cost_ref, primal_ref)
    copies = [
        pltpu.make_async_copy(source, target, sems.at[i]) for i, (source, target) in enumerate(zip(far, targets))
    ]
    for copy in copies:
        copy.start()
    regions = lists_ref.shape[0]
    quarter = shift_ref.shape[1] // BLOCKS
    there = lax.broadcasted_iota(jnp.int32, (LANES, LANES), 0)
    which = lax.broadcasted_iota(jnp.int32, (SUBLANES, LANES), 0)

    def count_up(chunk, total):
        lefts, rights = [], []
        for i in range(CHUNK):
            block, lane = group_place(lists_ref[pl.ds(chunk * CHUNK + i, 1), :])
            lefts.append(jnp.where(block == which, 1.0, 0.0).astype(jnp.bfloat16))
            rights.append(one_hot(lane, LANES))
        return total + product(jnp.concatenate(lefts, axis=1), jnp.concatenate(rights, axis=1))

    copies[0].wait()
    counts = repeat_chunks(regions // CHUNK, count_up, jnp.zeros((SUBLANES, LANES), jnp.float32))
    shares = 1.0 / jnp.maximum(counts, 1.0)
    copies[1].wait()
    duals = turn_rows(dual_ref[...], options)

    def one(r, carry):
        block, lane = group_place(lists_ref[pl.ds(r, 1), :])
        wide_block = jnp.broadcast_to(block, (options, LANES))
        wide_lane = jnp.broadcast_to(lane, (options, LANES))
        found = jnp.take_along_axis(duals[0], wide_lane, axis=1)
        for b in range(1, BLOCKS):
            found = jnp.where(wide_block == b, jnp.take_along_axis(duals[b], wide_lane, axis=1), found)
        picked_ref[r, 0:options, :] = found
        share = jnp.take_along_axis(shares, wide_lane[:SUBLANES], axis=1)
        share = jnp.sum(jnp.where(block == which, share, 0.0), axis=0, keepdims=True)
        picked_ref[r, options : options + SUBLANES, :] = jnp.broadcast_to(share, (SUBLANES, LANES))
        return carry

    each_region(regions, one)
    copies[2].wait()
    for b, quota in enumerate(turn_rows(quota_ref[...], options)):
        pull = DUAL_STEP * quota
        shift = duals[b] - pull
        for k in range(options // quarter):
            shift_ref[k, b * quarter : (b + 1) * quarter, :] = shift[k * quarter : (k + 1) * quarter, :]
        alone = duals[b]
        for _ in range(ITERS - 1):
            alone = jnp.maximum(alone - pull, 0.0)
        named = jnp.broadcast_to(counts[b : b + 1, :], alone.shape) > 0.0
        base_ref[b] = jnp.where(named, 0.0, alone) - pull
    for copy in copies[3:]:
        copy.wait()


def person_kernel(options, rep, last, *refs):
    if last:
        prices_ref, share_ref = refs[:2]
        regions = share_ref.shape[0]
    else:
        (prices_ref,) = refs[:1]
        regions = prices_ref.shape[0]
    slot_ref, cost_ref, primal_ref, fresh_ref, sums_ref, x_ref, parts_ref, hot_ref, owner_ref = refs[-9:]
    quarter = options // rep
    rows = slot_ref.shape[0]
    halves = options // SUBLANES
    chunks = regions // CHUNK
    blocks = CHUNK * LANES // WIDE
    groups = rows // SUBLANES
    stretch = SUBLANES * LANES

    def price(d, o):
        if last:
            return prices_ref[d * rep + o // quarter, o % quarter : o % quarter + 1, :]
        return prices_ref[d, o : o + 1, :]

    def partial_sums(chunk, g):
        span = slice(g * stretch, (g + 1) * stretch)
        owner = owner_ref[:, span]
        lines = []
        for part in range(2):
            x = parts_ref[part * options : (part + 1) * options, span]
            for e in range(blocks):
                number = jnp.asarray(chunk * blocks + e, jnp.float32).astype(jnp.bfloat16)
                lines.append(jnp.where(owner == number, x, jnp.bfloat16(0)))
        return product(jnp.concatenate(lines, axis=0), hot_ref[:, span])

    def hand_on(chunk, total):
        total = total[: blocks * options] + total[blocks * options :]
        for i in range(CHUNK):
            d = chunk * CHUNK + i
            e, h = divmod(i, WIDE // LANES)
            block = total[e * options : (e + 1) * options, h * LANES : (h + 1) * LANES]
            if last:
                share = jnp.where(lax.axis_index("rep") == 0, share_ref[d, options : options + SUBLANES, :], 0.0)
                held = jnp.concatenate([price(d, o) for o in range(options)], axis=0)
                block = DUAL_STEP * block + held * jnp.concatenate([share] * halves, axis=0)
            for k in range(rep):
                sums_ref[d * rep + k] = block if last else block[k * quarter : (k + 1) * quarter, :]

    total = None
    for g in range(groups):
        slot = slot_ref[g * SUBLANES : (g + 1) * SUBLANES, :]
        owner = slot // LANES
        within = slot - owner * LANES

        def pick(chunk, found):
            found = list(found)
            for d in range(CHUNK):
                mine = owner == chunk * CHUNK + d
                for o in range(options):
                    table = jnp.broadcast_to(price(chunk * CHUNK + d, o), (SUBLANES, LANES))
                    value = jnp.take_along_axis(table, within, axis=1)
                    found[o] = jnp.where(mine, value, found[o])
            return tuple(found)

        zero = jnp.zeros((SUBLANES, LANES), jnp.float32)
        adjoint = repeat_chunks(chunks, pick, (zero,) * options)
        places = []
        values = []
        for o in range(options):
            first = ((o // SUBLANES) * rows + g * SUBLANES) * SUBLANES + o % SUBLANES
            at = pl.ds(first, SUBLANES, stride=SUBLANES)
            places.append(at)
            values.append(primal_ref[at, :] - PRIMAL_STEP * (cost_ref[at, :] + adjoint[o]))
        theta = simplex_theta(values)
        for o in range(options):
            fresh = jnp.maximum(values[o] - theta, 0.0)
            fresh_ref[places[o], :] = fresh
            x_ref[places[o], :] = 2.0 * fresh - primal_ref[places[o], :]
        for c in range(g * SUBLANES, (g + 1) * SUBLANES):
            span = slice(c * LANES, (c + 1) * LANES)
            x = jnp.concatenate(
                [x_ref[(h * rows + c) * SUBLANES : (h * rows + c + 1) * SUBLANES, :] for h in range(halves)], axis=0
            )
            high, low = split_two(x)
            parts_ref[0:options, span] = high
            parts_ref[options : 2 * options, span] = low
            line = slot_ref[c : c + 1, :]
            hot_ref[:, span] = one_hot(line & (WIDE - 1), WIDE)
            number = jnp.broadcast_to((line // WIDE).astype(jnp.float32), (PACKED, LANES))
            owner_ref[:, span] = number.astype(jnp.bfloat16)
        if chunks == 1:
            found = partial_sums(0, g)
            total = found if total is None else total + found

    if chunks == 1:
        hand_on(0, total)
    else:

        def add_up(chunk, carry):
            total = partial_sums(chunk, 0)
            for g in range(1, groups):
                total = total + partial_sums(chunk, g)
            hand_on(chunk, total)
            return carry

        lax.fori_loop(0, chunks, add_up, 0)


def block_sums(arrived_ref, lists_ref):
    regions = lists_ref.shape[0]
    rep = arrived_ref.shape[0] // regions
    options = arrived_ref.shape[1]
    lines = BLOCKS * options
    copies = max(1, SUBLANES // options)
    tall = copies * options
    row = lax.broadcasted_iota(jnp.int32, (tall, CHUNK * LANES), 0) // options

    def add_up(chunk, total):
        sums, hots, numbers = [], [], []
        for i in range(CHUNK):
            r = chunk * CHUNK + i
            x = arrived_ref[r * rep]
            for k in range(1, rep):
                x = x + arrived_ref[r * rep + k]
            sums.append(jnp.concatenate([x] * copies, axis=0))
            block, lane = group_place(lists_ref[pl.ds(r, 1), :])
            hots.append(one_hot(lane, LANES))
            numbers.append(jnp.broadcast_to(block, (tall, LANES)))
        x = jnp.concatenate(sums, axis=1)
        number = jnp.concatenate(numbers, axis=1) - row
        high = x.astype(jnp.bfloat16).astype(jnp.float32)
        left = [
            jnp.where(number == first, part, 0.0) for part in (high, x - high) for first in range(0, BLOCKS, copies)
        ]
        found = product(jnp.concatenate(left, axis=0).astype(jnp.bfloat16), jnp.concatenate(hots, axis=1))
        return total + found[:lines] + found[lines:]

    return repeat_chunks(regions // CHUNK, add_up, jnp.zeros((lines, LANES), jnp.float32))


def middle_kernel(arrived_ref, lists_ref, shift_ref, picked_ref):
    regions = lists_ref.shape[0]
    rep = arrived_ref.shape[0] // regions
    options = arrived_ref.shape[1]
    applied = block_sums(arrived_ref, lists_ref)
    dual = jnp.maximum(shift_ref[lax.axis_index("rep")] + DUAL_STEP * applied, 0.0)
    blocks = [dual[b * options : (b + 1) * options, :] for b in range(BLOCKS)]

    def one(r, carry):
        block, lane = group_place(lists_ref[pl.ds(r, 1), :])
        block = jnp.broadcast_to(block, (options, LANES))
        lane = jnp.broadcast_to(lane, (options, LANES))
        found = jnp.take_along_axis(blocks[0], lane, axis=1)
        for b in range(1, BLOCKS):
            found = jnp.where(block == b, jnp.take_along_axis(blocks[b], lane, axis=1), found)
        for k in range(rep):
            picked_ref[r * rep + k] = found
        return carry

    each_region(regions, one)


def last_kernel(arrived_ref, lists_ref, base_ref, fresh_ref, dual_ref, primal_far, sem):
    copy = pltpu.make_async_copy(fresh_ref, primal_far, sem)
    copy.start()
    options = base_ref.shape[1]
    sums = block_sums(arrived_ref, lists_ref)
    lines = []
    for b in range(BLOCKS):
        block = jnp.maximum(base_ref[b] + sums[b * options : (b + 1) * options, :], 0.0)
        lines.append(block)
        lines.append(pltpu.roll(block, LANES // 2, 1))
    dual_ref[...] = jnp.concatenate(lines, axis=0).T[: dual_ref.shape[0], :]
    copy.wait()


def call(kernel, outs, scratch=(), ins=None):
    vmem = pl.BlockSpec(memory_space=pltpu.VMEM)
    hbm = pl.BlockSpec(memory_space=pltpu.HBM)
    params = {} if ins is None else {"in_specs": [hbm if far else vmem for far in ins]}
    return pl.pallas_call(
        kernel,
        out_shape=[jax.ShapeDtypeStruct(shape, kind) for shape, kind, _ in outs],
        out_specs=[hbm if far else vmem for _, _, far in outs],
        scratch_shapes=list(scratch),
        compiler_params=pltpu.CompilerParams(vmem_limit_bytes=VMEM_LIMIT),
        **params,
    )


def far(x):
    return pltpu.with_memory_space_constraint(x, pltpu.HBM)


def local(unit_cost, start_primal, start_dual, quota_bound, person_slot, cell_lists):
    options, persons = unit_cost.shape
    regions = lax.axis_size("region")
    rep = lax.axis_size("rep")
    quarter = options // rep
    groups = quota_bound.shape[0] // options
    rows = persons // LANES
    halves = options // SUBLANES

    def to_tiles(x):
        x = x.reshape(halves, SUBLANES, rows, LANES).transpose(0, 2, 1, 3)
        return x.reshape(options * rows, LANES)

    def from_tiles(x):
        x = x.reshape(halves, rows, SUBLANES, LANES).transpose(0, 2, 1, 3)
        return x.reshape(options, persons)

    def array(*shape, kind=jnp.float32, far=False):
        return (shape, kind, far)

    flat = (groups * options // LANES, LANES)
    tiles = array(options * rows, LANES)
    block_rows = array(BLOCKS, options, LANES)
    quarters = array(regions * rep, quarter, LANES)
    wholes = array(regions * rep, options, LANES)
    both = ("region", "rep")
    exchange = functools.partial(lax.all_to_all, split_axis=0, concat_axis=0, tiled=True)

    picked, shift, base, lists, slots, cost, primal = call(
        functools.partial(first_kernel, options),
        (
            array(regions, options + SUBLANES, LANES),
            array(rep, BLOCKS * quarter, LANES),
            block_rows,
            array(regions, LANES, kind=jnp.int32),
            array(rows, LANES, kind=jnp.int32),
            tiles,
            tiles,
        ),
        (pltpu.VMEM(flat, jnp.float32), pltpu.VMEM(flat, jnp.float32), pltpu.SemaphoreType.DMA((6,))),
        (True,) * 6,
    )(
        far(cell_lists[0]),
        far(start_dual.reshape(flat)),
        far(quota_bound.reshape(flat)),
        far(person_slot.reshape(rows, LANES)),
        far(to_tiles(unit_cost)),
        far(to_tiles(start_primal)),
    )
    first_prices = exchange(picked, "region")
    scratch = (
        pltpu.VMEM(tiles[0], jnp.float32),
        pltpu.VMEM((2 * options, persons), jnp.bfloat16),
        pltpu.VMEM((WIDE, persons), jnp.bfloat16),
        pltpu.VMEM((PACKED, persons), jnp.bfloat16),
    )
    primal, sums = call(functools.partial(person_kernel, options, rep, False), (tiles, quarters), scratch)(
        first_prices, slots, cost, primal
    )
    arrived = exchange(sums, both)
    (picked,) = call(middle_kernel, (quarters,))(arrived, lists, shift)
    prices = exchange(picked, both)
    primal, sums = call(functools.partial(person_kernel, options, rep, True), (tiles, wholes), scratch)(
        prices, first_prices, slots, cost, primal
    )
    arrived = exchange(sums, both)
    dual, primal = call(
        last_kernel, (array(*flat), array(*tiles[0], far=True)), (pltpu.SemaphoreType.DMA,)
    )(arrived, lists, base, primal)
    return (from_tiles(primal), dual.reshape(-1))


def solution(mesh):
    placed = (
        P(None, ("region", "rep")),
        P(None, ("region", "rep")),
        P("region"),
        P("region"),
        P(("region", "rep")),
        P("region", None, None),
    )
    return jax.shard_map(
        local,
        mesh=mesh,
        in_specs=placed,
        out_specs=(P(None, ("region", "rep")), P("region")),
        check_vma=False,
    )
```

```python
import functools

import jax
import jax.numpy as jnp
from jax import lax
from jax.experimental import pallas as pl
from jax.experimental.pallas import tpu as pltpu
from jax.sharding import PartitionSpec as P

ITERS = 2
BISECT = 30
PRIMAL_STEP = 0.5
DUAL_STEP = 0.25
LANES = 128
SUBLANES = 8
CHUNK = 8
PACKED = 16
WIDE = 256
BLOCKS = 4
VMEM_LIMIT = 48 * 1024 * 1024


def sorting_network(count):
    pairs = []
    p = 1
    while p < count:
        k = p
        while k >= 1:
            for j in range(k % p, count - k, 2 * k):
                for i in range(min(k, count - j - k)):
                    if (i + j) // (2 * p) == (i + j + k) // (2 * p):
                        pairs.append((i + j, i + j + k))
            k //= 2
        p *= 2
    return pairs


def repeat_chunks(total, body, init):
    if total == 1:
        return body(0, init)
    return lax.fori_loop(0, total, body, init)


def simplex_theta(values):
    ranked = list(values)
    for a, b in sorting_network(len(values)):
        ranked[a], ranked[b] = jnp.maximum(ranked[a], ranked[b]), jnp.minimum(ranked[a], ranked[b])
    largest = ranked[0]
    total = jnp.zeros_like(largest)
    best = jnp.full_like(largest, -1.0)
    for k in range(1, len(values)):
        total = total + (ranked[k] - largest)
        best = jnp.maximum(best, (total - 1.0) * (1.0 / (k + 1)))
    cells = float(2**BISECT)
    step = jnp.maximum(jnp.ceil((best + 1.0) * cells), 1.0) - 0.5
    return (largest - 1.0) + step * (1.0 / cells)


def split_two(x):
    high = x.astype(jnp.bfloat16)
    low = (x - high.astype(jnp.float32)).astype(jnp.bfloat16)
    return high, low


def one_hot(index, count):
    wide = jnp.broadcast_to(index.astype(jnp.float32), (PACKED, index.shape[1])).astype(jnp.bfloat16)
    lines = []
    for first in range(0, count, PACKED):
        here = lax.broadcasted_iota(jnp.int32, wide.shape, 0) + first
        hit = wide == here.astype(jnp.float32).astype(jnp.bfloat16)
        lines.append(jnp.where(hit, jnp.bfloat16(1), jnp.bfloat16(0)))
    return jnp.concatenate(lines, axis=0)


def product(left, right):
    return lax.dot_general(left, right, (((1,), (1,)), ((), ())), preferred_element_type=jnp.float32)


def group_place(lists):
    return (lists & (SUBLANES - 1)) >> 1, (lists & 1) * (LANES // 2) + (lists >> 3)


def each_region(regions, body):
    if regions <= CHUNK:
        for r in range(regions):
            body(r, 0)
    else:
        lax.fori_loop(0, regions, body, 0)


def turn_rows(flat, options):
    turned = jnp.concatenate([flat, flat], axis=0).T
    left = lax.broadcasted_iota(jnp.int32, (options, LANES), 1) < LANES // 2
    pairs = [turned[i * options : (i + 1) * options, :] for i in range(2 * BLOCKS)]
    return [jnp.where(left, pairs[2 * b], pairs[2 * b + 1]) for b in range(BLOCKS)]


def first_kernel(options, *refs):
    far, outs, (dual_ref, quota_ref, sems) = refs[:6], refs[6:13], refs[13:]
    picked_ref, shift_ref, base_ref, lists_ref, slot_ref, cost_ref, primal_ref = outs
    targets = (lists_ref, dual_ref, quota_ref, slot_ref, cost_ref, primal_ref)
    copies = [
        pltpu.make_async_copy(source, target, sems.at[i]) for i, (source, target) in enumerate(zip(far, targets))
    ]
    for copy in copies:
        copy.start()
    regions = lists_ref.shape[0]
    quarter = shift_ref.shape[1] // BLOCKS
    there = lax.broadcasted_iota(jnp.int32, (LANES, LANES), 0)
    which = lax.broadcasted_iota(jnp.int32, (SUBLANES, LANES), 0)

    def count_up(chunk, total):
        lefts, rights = [], []
        for i in range(CHUNK):
            block, lane = group_place(lists_ref[pl.ds(chunk * CHUNK + i, 1), :])
            lefts.append(jnp.where(block == which, 1.0, 0.0).astype(jnp.bfloat16))
            rights.append(one_hot(lane, LANES))
        return total + product(jnp.concatenate(lefts, axis=1), jnp.concatenate(rights, axis=1))

    copies[0].wait()
    counts = repeat_chunks(regions // CHUNK, count_up, jnp.zeros((SUBLANES, LANES), jnp.float32))
    shares = 1.0 / jnp.maximum(counts, 1.0)
    copies[1].wait()
    duals = turn_rows(dual_ref[...], options)

    def one(r, carry):
        block, lane = group_place(lists_ref[pl.ds(r, 1), :])
        wide_block = jnp.broadcast_to(block, (options, LANES))
        wide_lane = jnp.broadcast_to(lane, (options, LANES))
        found = jnp.take_along_axis(duals[0], wide_lane, axis=1)
        for b in range(1, BLOCKS):
            found = jnp.where(wide_block == b, jnp.take_along_axis(duals[b], wide_lane, axis=1), found)
        picked_ref[r, 0:options, :] = found
        share = jnp.take_along_axis(shares, wide_lane[:SUBLANES], axis=1)
        share = jnp.sum(jnp.where(block == which, share, 0.0), axis=0, keepdims=True)
        picked_ref[r, options : options + SUBLANES, :] = jnp.broadcast_to(share, (SUBLANES, LANES))
        return carry

    each_region(regions, one)
    copies[2].wait()
    for b, quota in enumerate(turn_rows(quota_ref[...], options)):
        pull = DUAL_STEP * quota
        shift = duals[b] - pull
        for k in range(options // quarter):
            shift_ref[k, b * quarter : (b + 1) * quarter, :] = shift[k * quarter : (k + 1) * quarter, :]
        alone = duals[b]
        for _ in range(ITERS - 1):
            alone = jnp.maximum(alone - pull, 0.0)
        named = jnp.broadcast_to(counts[b : b + 1, :], alone.shape) > 0.0
        base = jnp.where(named, 0.0, alone) - pull
        for h in range(base_ref.shape[0]):
            base_ref[h, b] = base[h * base_ref.shape[2] : (h + 1) * base_ref.shape[2], :]
    for copy in copies[3:]:
        copy.wait()


def person_kernel(options, rep, last, *refs):
    if last:
        prices_ref, share_ref, slot_ref, cost_ref, primal_ref, fresh_ref, sums_ref, x_ref, *kept_refs = refs
        regions = share_ref.shape[0]
    else:
        prices_ref, slot_ref, cost_ref, primal_ref, fresh_ref, sums_ref, x_ref, *kept_refs = refs
        regions = prices_ref.shape[0]
    quarter = options // rep
    rows = slot_ref.shape[0]
    halves = options // SUBLANES
    chunks = regions // CHUNK
    blocks = CHUNK * LANES // WIDE
    groups = rows // SUBLANES
    sent = sums_ref.shape[1]

    def price(d, o):
        if last:
            return prices_ref[d * rep + o // quarter, o % quarter : o % quarter + 1, :]
        return prices_ref[d, o : o + 1, :]

    def operands(c):
        x = [x_ref[(h * rows + c) * SUBLANES : (h * rows + c + 1) * SUBLANES, :] for h in range(halves)]
        high, low = split_two(jnp.concatenate(x, axis=0))
        line = slot_ref[c : c + 1, :]
        number = jnp.broadcast_to((line // WIDE).astype(jnp.float32), (PACKED, LANES)).astype(jnp.bfloat16)
        return high, low, one_hot(line & (WIDE - 1), WIDE), number

    def partial_sums(chunk, pieces):
        lines = []
        for part in range(2):
            for e in range(blocks):
                mine = jnp.asarray(chunk * blocks + e, jnp.float32).astype(jnp.bfloat16)
                kept = [jnp.where(piece[3] == mine, piece[part], jnp.bfloat16(0)) for piece in pieces]
                lines.append(jnp.concatenate(kept, axis=1))
        hot = jnp.concatenate([piece[2] for piece in pieces], axis=1)
        return product(jnp.concatenate(lines, axis=0), hot)

    def hand_on(chunk, total):
        total = total[: blocks * options] + total[blocks * options :]
        for i in range(CHUNK):
            d = chunk * CHUNK + i
            e, h = divmod(i, WIDE // LANES)
            block = total[e * options : (e + 1) * options, h * LANES : (h + 1) * LANES]
            if last:
                share = jnp.where(lax.axis_index("rep") == 0, share_ref[d, options : options + SUBLANES, :], 0.0)
                held = jnp.concatenate([price(d, o) for o in range(options)], axis=0)
                block = DUAL_STEP * block + held * jnp.concatenate([share] * halves, axis=0)
            for k in range(rep):
                first = k * sent % options
                sums_ref[d * rep + k] = block[first : first + sent, :]

    total = None
    for g in range(groups):
        slot = slot_ref[g * SUBLANES : (g + 1) * SUBLANES, :]
        owner = slot // LANES
        within = slot - owner * LANES

        def pick(chunk, found):
            found = list(found)
            for d in range(CHUNK):
                mine = owner == chunk * CHUNK + d
                for o in range(options):
                    table = jnp.broadcast_to(price(chunk * CHUNK + d, o), (SUBLANES, LANES))
                    value = jnp.take_along_axis(table, within, axis=1)
                    found[o] = jnp.where(mine, value, found[o])
            return tuple(found)

        zero = jnp.zeros((SUBLANES, LANES), jnp.float32)
        adjoint = repeat_chunks(chunks, pick, (zero,) * options)
        places = []
        values = []
        for o in range(options):
            first = ((o // SUBLANES) * rows + g * SUBLANES) * SUBLANES + o % SUBLANES
            at = pl.ds(first, SUBLANES, stride=SUBLANES)
            places.append(at)
            values.append(primal_ref[at, :] - PRIMAL_STEP * (cost_ref[at, :] + adjoint[o]))
        theta = simplex_theta(values)
        for o in range(options):
            fresh = jnp.maximum(values[o] - theta, 0.0)
            fresh_ref[places[o], :] = fresh
            x_ref[places[o], :] = 2.0 * fresh - primal_ref[places[o], :]
        pieces = [operands(c) for c in range(g * SUBLANES, (g + 1) * SUBLANES)]
        if chunks == 1:
            found = partial_sums(0, pieces)
            total = found if total is None else total + found
        else:
            for c, piece in zip(range(g * SUBLANES, (g + 1) * SUBLANES), pieces):
                for ref, value in zip(kept_refs, piece):
                    ref[:, c * LANES : (c + 1) * LANES] = value

    if chunks == 1:
        hand_on(0, total)
    else:

        def add_up(chunk, carry):
            hand_on(chunk, partial_sums(chunk, [[ref[...] for ref in kept_refs]]))
            return carry

        lax.fori_loop(0, chunks, add_up, 0)


def block_sums(arrived_ref, lists_ref):
    regions = lists_ref.shape[0]
    rep = arrived_ref.shape[0] // regions
    options = arrived_ref.shape[1]
    lines = BLOCKS * options
    copies = max(1, SUBLANES // options)
    tall = copies * options
    row = lax.broadcasted_iota(jnp.int32, (tall, CHUNK * LANES), 0) // options

    def add_up(chunk, total):
        sums, hots, numbers = [], [], []
        for i in range(CHUNK):
            r = chunk * CHUNK + i
            x = arrived_ref[r * rep]
            for k in range(1, rep):
                x = x + arrived_ref[r * rep + k]
            sums.append(jnp.concatenate([x] * copies, axis=0))
            block, lane = group_place(lists_ref[pl.ds(r, 1), :])
            hots.append(one_hot(lane, LANES))
            numbers.append(jnp.broadcast_to(block, (tall, LANES)))
        x = jnp.concatenate(sums, axis=1)
        number = jnp.concatenate(numbers, axis=1) - row
        high = x.astype(jnp.bfloat16).astype(jnp.float32)
        left = [
            jnp.where(number == first, part, 0.0) for part in (high, x - high) for first in range(0, BLOCKS, copies)
        ]
        found = product(jnp.concatenate(left, axis=0).astype(jnp.bfloat16), jnp.concatenate(hots, axis=1))
        return total + found[:lines] + found[lines:]

    return repeat_chunks(regions // CHUNK, add_up, jnp.zeros((lines, LANES), jnp.float32))


def middle_kernel(arrived_ref, lists_ref, shift_ref, picked_ref):
    regions = lists_ref.shape[0]
    rep = arrived_ref.shape[0] // regions
    options = arrived_ref.shape[1]
    applied = block_sums(arrived_ref, lists_ref)
    dual = jnp.maximum(shift_ref[lax.axis_index("rep")] + DUAL_STEP * applied, 0.0)
    blocks = [dual[b * options : (b + 1) * options, :] for b in range(BLOCKS)]

    def one(r, carry):
        block, lane = group_place(lists_ref[pl.ds(r, 1), :])
        block = jnp.broadcast_to(block, (options, LANES))
        lane = jnp.broadcast_to(lane, (options, LANES))
        found = jnp.take_along_axis(blocks[0], lane, axis=1)
        for b in range(1, BLOCKS):
            found = jnp.where(block == b, jnp.take_along_axis(blocks[b], lane, axis=1), found)
        for k in range(rep):
            picked_ref[r * rep + k] = found
        return carry

    each_region(regions, one)


def half_kernel(arrived_ref, lists_ref, base_ref, part_ref):
    sent = arrived_ref.shape[1]
    shares = base_ref.shape[0]
    mine = lax.axis_index("rep") % shares
    sums = block_sums(arrived_ref, lists_ref)
    lines = []
    for b in range(BLOCKS):
        block = jnp.maximum(base_ref[mine, b] + sums[b * sent : (b + 1) * sent, :], 0.0)
        whole = jnp.concatenate([jnp.where(mine == h, block, 0.0) for h in range(shares)], axis=0)
        lines.append(whole)
        lines.append(pltpu.roll(whole, LANES // 2, 1))
    part_ref[...] = jnp.concatenate(lines, axis=0).T[: part_ref.shape[0], :]


def last_kernel(mine_ref, other_ref, fresh_ref, dual_far, primal_far, sum_ref, sems):
    copy_primal = pltpu.make_async_copy(fresh_ref, primal_far, sems.at[0])
    copy_primal.start()
    sum_ref[...] = mine_ref[...] + other_ref[...]
    copy_dual = pltpu.make_async_copy(sum_ref, dual_far, sems.at[1])
    copy_dual.start()
    copy_primal.wait()
    copy_dual.wait()


def call(kernel, outs, scratch=(), ins=None):
    vmem = pl.BlockSpec(memory_space=pltpu.VMEM)
    hbm = pl.BlockSpec(memory_space=pltpu.HBM)
    params = {} if ins is None else {"in_specs": [hbm if far else vmem for far in ins]}
    return pl.pallas_call(
        kernel,
        out_shape=[jax.ShapeDtypeStruct(shape, kind) for shape, kind, _ in outs],
        out_specs=[hbm if far else vmem for _, _, far in outs],
        scratch_shapes=list(scratch),
        compiler_params=pltpu.CompilerParams(vmem_limit_bytes=VMEM_LIMIT),
        **params,
    )


def far(x):
    return pltpu.with_memory_space_constraint(x, pltpu.HBM)


def local(unit_cost, start_primal, start_dual, quota_bound, person_slot, cell_lists):
    options, persons = unit_cost.shape
    regions = lax.axis_size("region")
    rep = lax.axis_size("rep")
    quarter = options // rep
    groups = quota_bound.shape[0] // options
    rows = persons // LANES
    halves = options // SUBLANES

    def to_tiles(x):
        x = x.reshape(halves, SUBLANES, rows, LANES).transpose(0, 2, 1, 3)
        return x.reshape(options * rows, LANES)

    def from_tiles(x):
        x = x.reshape(halves, rows, SUBLANES, LANES).transpose(0, 2, 1, 3)
        return x.reshape(options, persons)

    def array(*shape, kind=jnp.float32, far=False):
        return (shape, kind, far)

    flat = (groups * options // LANES, LANES)
    tiles = array(options * rows, LANES)
    half = options // 2
    base_rows = array(2, BLOCKS, half, LANES)
    quarters = array(regions * rep, quarter, LANES)
    half_rows = array(regions * rep, half, LANES)
    both = ("region", "rep")
    exchange = functools.partial(lax.all_to_all, split_axis=0, concat_axis=0, tiled=True)

    picked, shift, base, lists, slots, cost, primal = call(
        functools.partial(first_kernel, options),
        (
            array(regions, options + SUBLANES, LANES),
            array(rep, BLOCKS * quarter, LANES),
            base_rows,
            array(regions, LANES, kind=jnp.int32),
            array(rows, LANES, kind=jnp.int32),
            tiles,
            tiles,
        ),
        (pltpu.VMEM(flat, jnp.float32), pltpu.VMEM(flat, jnp.float32), pltpu.SemaphoreType.DMA((6,))),
        (True,) * 6,
    )(
        far(cell_lists[0]),
        far(start_dual.reshape(flat)),
        far(quota_bound.reshape(flat)),
        far(person_slot.reshape(rows, LANES)),
        far(to_tiles(unit_cost)),
        far(to_tiles(start_primal)),
    )
    first_prices = exchange(picked, "region")
    scratch = (pltpu.VMEM(tiles[0], jnp.float32),)
    if regions > CHUNK:
        scratch += tuple(pltpu.VMEM((tall, persons), jnp.bfloat16) for tall in (options, options, WIDE, PACKED))
    primal, sums = call(functools.partial(person_kernel, options, rep, False), (tiles, quarters), scratch)(
        first_prices, slots, cost, primal
    )
    arrived = exchange(sums, both)
    (picked,) = call(middle_kernel, (quarters,))(arrived, lists, shift)
    prices = exchange(picked, both)
    primal, sums = call(functools.partial(person_kernel, options, rep, True), (tiles, half_rows), scratch)(
        prices, first_prices, slots, cost, primal
    )
    arrived = exchange(sums, both)
    (part,) = call(half_kernel, (array(*flat),))(arrived, lists, base)
    other = lax.ppermute(part, "rep", [(k, k ^ 1) for k in range(rep)])
    dual, primal = call(
        last_kernel,
        (array(*flat, far=True), array(*tiles[0], far=True)),
        (pltpu.VMEM(flat, jnp.float32), pltpu.SemaphoreType.DMA((2,))),
    )(part, other, primal)
    return (from_tiles(primal), dual.reshape(-1))


def solution(mesh):
    placed = (
        P(None, ("region", "rep")),
        P(None, ("region", "rep")),
        P("region"),
        P("region"),
        P(("region", "rep")),
        P("region", None, None),
    )
    return jax.shard_map(
        local,
        mesh=mesh,
        in_specs=placed,
        out_specs=(P(None, ("region", "rep")), P("region")),
        check_vma=False,
    )
```

```python
import functools

import jax
import jax.numpy as jnp
from jax import lax
from jax.experimental import pallas as pl
from jax.experimental.pallas import tpu as pltpu
from jax.sharding import PartitionSpec as P

ITERS = 2
BISECT = 30
PRIMAL_STEP = 0.5
DUAL_STEP = 0.25
LANES = 128
SUBLANES = 8
CHUNK = 8
PACKED = 16
WIDE = 256
LANE_BITS = LANES.bit_length() - 1
WIDE_BITS = WIDE.bit_length() - 1
BLOCKS = 4
VMEM_LIMIT = 48 * 1024 * 1024


def sorting_network(count):
    pairs = []
    p = 1
    while p < count:
        k = p
        while k >= 1:
            for j in range(k % p, count - k, 2 * k):
                for i in range(min(k, count - j - k)):
                    if (i + j) // (2 * p) == (i + j + k) // (2 * p):
                        pairs.append((i + j, i + j + k))
            k //= 2
        p *= 2
    return pairs


def repeat_chunks(total, body, init):
    if total == 1:
        return body(0, init)
    return lax.fori_loop(0, total, body, init)


def simplex_theta(values):
    ranked = list(values)
    for a, b in sorting_network(len(values)):
        ranked[a], ranked[b] = jnp.maximum(ranked[a], ranked[b]), jnp.minimum(ranked[a], ranked[b])
    largest = ranked[0]
    total = jnp.zeros_like(largest)
    best = jnp.full_like(largest, -1.0)
    for k in range(1, len(values)):
        total = total + (ranked[k] - largest)
        best = jnp.maximum(best, (total - 1.0) * (1.0 / (k + 1)))
    cells = float(2**BISECT)
    step = jnp.maximum(jnp.ceil((best + 1.0) * cells), 1.0) - 0.5
    return (largest - 1.0) + step * (1.0 / cells)


def split_two(x):
    high = x.astype(jnp.bfloat16)
    low = (x - high.astype(jnp.float32)).astype(jnp.bfloat16)
    return high, low


def one_hot(index, count):
    wide = jnp.broadcast_to(index.astype(jnp.float32), (PACKED, index.shape[1])).astype(jnp.bfloat16)
    lines = []
    for first in range(0, count, PACKED):
        here = lax.broadcasted_iota(jnp.int32, wide.shape, 0) + first
        hit = wide == here.astype(jnp.float32).astype(jnp.bfloat16)
        lines.append(jnp.where(hit, jnp.bfloat16(1), jnp.bfloat16(0)))
    return jnp.concatenate(lines, axis=0)


def product(left, right):
    return lax.dot_general(left, right, (((1,), (1,)), ((), ())), preferred_element_type=jnp.float32)


def group_place(lists):
    return (lists & (SUBLANES - 1)) >> 1, (lists & 1) * (LANES // 2) + (lists >> 3)


def each_region(regions, body):
    if regions <= CHUNK:
        for r in range(regions):
            body(r, 0)
    else:
        lax.fori_loop(0, regions, body, 0)


def turn_rows(flat, options):
    turned = jnp.concatenate([flat, flat], axis=0).T
    left = lax.broadcasted_iota(jnp.int32, (options, LANES), 1) < LANES // 2
    pairs = [turned[i * options : (i + 1) * options, :] for i in range(2 * BLOCKS)]
    return [jnp.where(left, pairs[2 * b], pairs[2 * b + 1]) for b in range(BLOCKS)]


def first_kernel(options, *refs):
    far, outs, (dual_ref, quota_ref, sems) = refs[:6], refs[6:13], refs[13:]
    picked_ref, shift_ref, base_ref, lists_ref, slot_ref, cost_ref, primal_ref = outs
    targets = (lists_ref, dual_ref, quota_ref, slot_ref, cost_ref, primal_ref)
    copies = [
        pltpu.make_async_copy(source, target, sems.at[i]) for i, (source, target) in enumerate(zip(far, targets))
    ]
    for copy in copies:
        copy.start()
    regions = lists_ref.shape[0]
    quarter = shift_ref.shape[1] // BLOCKS
    there = lax.broadcasted_iota(jnp.int32, (LANES, LANES), 0)
    which = lax.broadcasted_iota(jnp.int32, (SUBLANES, LANES), 0)

    def count_up(chunk, total):
        lefts, rights = [], []
        for i in range(CHUNK):
            block, lane = group_place(lists_ref[pl.ds(chunk * CHUNK + i, 1), :])
            lefts.append(jnp.where(block == which, 1.0, 0.0).astype(jnp.bfloat16))
            rights.append(one_hot(lane, LANES))
        return total + product(jnp.concatenate(lefts, axis=1), jnp.concatenate(rights, axis=1))

    for copy in copies[:3]:
        copy.wait()
    counts = repeat_chunks(regions // CHUNK, count_up, jnp.zeros((SUBLANES, LANES), jnp.float32))
    shares = 1.0 / jnp.maximum(counts, 1.0)
    duals = turn_rows(dual_ref[...], options)

    def one(r, carry):
        block, lane = group_place(lists_ref[pl.ds(r, 1), :])
        wide_block = jnp.broadcast_to(block, (options, LANES))
        wide_lane = jnp.broadcast_to(lane, (options, LANES))
        found = jnp.take_along_axis(duals[0], wide_lane, axis=1)
        for b in range(1, BLOCKS):
            found = jnp.where(wide_block == b, jnp.take_along_axis(duals[b], wide_lane, axis=1), found)
        picked_ref[r, 0:options, :] = found
        share = jnp.take_along_axis(shares, wide_lane[:SUBLANES], axis=1)
        share = jnp.sum(jnp.where(block == which, share, 0.0), axis=0, keepdims=True)
        picked_ref[r, options : options + SUBLANES, :] = jnp.broadcast_to(share, (SUBLANES, LANES))
        return carry

    each_region(regions, one)
    for b, quota in enumerate(turn_rows(quota_ref[...], options)):
        pull = DUAL_STEP * quota
        shift = duals[b] - pull
        for k in range(options // quarter):
            shift_ref[k, b * quarter : (b + 1) * quarter, :] = shift[k * quarter : (k + 1) * quarter, :]
        alone = duals[b]
        for _ in range(ITERS - 1):
            alone = jnp.maximum(alone - pull, 0.0)
        named = jnp.broadcast_to(counts[b : b + 1, :], alone.shape) > 0.0
        base = jnp.where(named, 0.0, alone) - pull
        for h in range(base_ref.shape[0]):
            base_ref[h, b] = base[h * base_ref.shape[2] : (h + 1) * base_ref.shape[2], :]
    for copy in copies[3:]:
        copy.wait()


def person_kernel(options, rep, last, *refs):
    if last:
        prices_ref, share_ref, turned_ref, slot_ref, cost_ref, primal_ref, fresh_ref, sums_ref, *kept_refs = refs
        regions = share_ref.shape[0]
    else:
        prices_ref, slot_ref, cost_ref, primal_ref, fresh_ref, sums_ref, turned_ref, *kept_refs = refs
        regions = prices_ref.shape[0]
    quarter = options // rep
    rows = slot_ref.shape[0]
    halves = options // SUBLANES
    chunks = regions // CHUNK
    blocks = CHUNK * LANES // WIDE
    groups = rows // SUBLANES
    sent = sums_ref.shape[1]

    def price(d, o):
        if last:
            return prices_ref[d * rep + o // quarter, o % quarter : o % quarter + 1, :]
        return prices_ref[d, o : o + 1, :]

    def operands(c):
        tiles = [slice((h * rows + c) * SUBLANES, (h * rows + c + 1) * SUBLANES) for h in range(halves)]
        x = jnp.concatenate([2.0 * fresh_ref[tile, :] - primal_ref[tile, :] for tile in tiles], axis=0)
        high, low = split_two(x)
        span = slice(c * LANES, (c + 1) * LANES)
        line = slot_ref[c : c + 1, :]
        if last:
            turned = turned_ref[span, :]
        else:
            within = jnp.broadcast_to((line & (WIDE - 1)).astype(jnp.float32), (LANES, LANES))
            turned = within.astype(jnp.bfloat16).T
            turned_ref[span, :] = turned
        turned = jnp.concatenate([turned] * (WIDE // LANES), axis=1)
        here = lax.broadcasted_iota(jnp.int32, (PACKED, WIDE), 1).astype(jnp.float32).astype(jnp.bfloat16)
        hot = [
            jnp.where(turned[first : first + PACKED] == here, jnp.bfloat16(1), jnp.bfloat16(0))
            for first in range(0, LANES, PACKED)
        ]
        number = jnp.broadcast_to((line >> WIDE_BITS).astype(jnp.float32), (PACKED, LANES)).astype(jnp.bfloat16)
        return high, low, number, jnp.concatenate(hot, axis=0)

    def partial_sums(chunk, pieces):
        lines = []
        for part in range(2):
            for e in range(blocks):
                mine = jnp.asarray(chunk * blocks + e, jnp.float32).astype(jnp.bfloat16)
                kept = [jnp.where(piece[2] == mine, piece[part], jnp.bfloat16(0)) for piece in pieces]
                lines.append(jnp.concatenate(kept, axis=1))
        hot = jnp.concatenate([piece[3] for piece in pieces], axis=0)
        return jnp.dot(jnp.concatenate(lines, axis=0), hot, preferred_element_type=jnp.float32)

    def hand_on(chunk, total):
        total = total[: blocks * options] + total[blocks * options :]
        for i in range(CHUNK):
            d = chunk * CHUNK + i
            e, h = divmod(i, WIDE // LANES)
            block = total[e * options : (e + 1) * options, h * LANES : (h + 1) * LANES]
            if last:
                share = jnp.where(lax.axis_index("rep") == 0, share_ref[d, options : options + SUBLANES, :], 0.0)
                held = jnp.concatenate([price(d, o) for o in range(options)], axis=0)
                block = DUAL_STEP * block + held * jnp.concatenate([share] * halves, axis=0)
            for k in range(rep):
                first = k * sent % options
                sums_ref[d * rep + k] = block[first : first + sent, :]

    for g in range(groups):
        slot = slot_ref[g * SUBLANES : (g + 1) * SUBLANES, :]
        owner = slot >> LANE_BITS
        within = slot & (LANES - 1)

        def pick(chunk, found):
            found = list(found)
            for d in range(CHUNK):
                mine = owner == chunk * CHUNK + d
                for o in range(options):
                    table = jnp.broadcast_to(price(chunk * CHUNK + d, o), (SUBLANES, LANES))
                    value = jnp.take_along_axis(table, within, axis=1)
                    found[o] = jnp.where(mine, value, found[o])
            return tuple(found)

        zero = jnp.zeros((SUBLANES, LANES), jnp.float32)
        adjoint = repeat_chunks(chunks, pick, (zero,) * options)
        places = []
        values = []
        for o in range(options):
            first = ((o // SUBLANES) * rows + g * SUBLANES) * SUBLANES + o % SUBLANES
            at = pl.ds(first, SUBLANES, stride=SUBLANES)
            places.append(at)
            values.append(primal_ref[at, :] - PRIMAL_STEP * (cost_ref[at, :] + adjoint[o]))
        theta = simplex_theta(values)
        for o in range(options):
            fresh_ref[places[o], :] = jnp.maximum(values[o] - theta, 0.0)

    pieces = [operands(c) for c in range(rows)]
    if chunks == 1:
        hand_on(0, partial_sums(0, pieces))
    else:
        for c, piece in enumerate(pieces):
            span = slice(c * LANES, (c + 1) * LANES)
            for ref, value in zip(kept_refs[:3], piece):
                ref[:, span] = value
            kept_refs[3][span, :] = piece[3]

        def add_up(chunk, carry):
            hand_on(chunk, partial_sums(chunk, [[ref[...] for ref in kept_refs]]))
            return carry

        lax.fori_loop(0, chunks, add_up, 0)


def block_sums(arrived_ref, lists_ref):
    regions = lists_ref.shape[0]
    rep = arrived_ref.shape[0] // regions
    options = arrived_ref.shape[1]
    lines = BLOCKS * options
    copies = max(1, SUBLANES // options)
    tall = copies * options
    row = lax.broadcasted_iota(jnp.int32, (tall, CHUNK * LANES), 0) // options

    def add_up(chunk, total):
        sums, hots, numbers = [], [], []
        for i in range(CHUNK):
            r = chunk * CHUNK + i
            x = arrived_ref[r * rep]
            for k in range(1, rep):
                x = x + arrived_ref[r * rep + k]
            sums.append(jnp.concatenate([x] * copies, axis=0))
            block, lane = group_place(lists_ref[pl.ds(r, 1), :])
            hots.append(one_hot(lane, LANES))
            numbers.append(jnp.broadcast_to(block, (tall, LANES)))
        x = jnp.concatenate(sums, axis=1)
        number = jnp.concatenate(numbers, axis=1) - row
        high = x.astype(jnp.bfloat16).astype(jnp.float32)
        left = [
            jnp.where(number == first, part, 0.0) for part in (high, x - high) for first in range(0, BLOCKS, copies)
        ]
        found = product(jnp.concatenate(left, axis=0).astype(jnp.bfloat16), jnp.concatenate(hots, axis=1))
        return total + found[:lines] + found[lines:]

    return repeat_chunks(regions // CHUNK, add_up, jnp.zeros((lines, LANES), jnp.float32))


def middle_kernel(arrived_ref, lists_ref, shift_ref, picked_ref):
    regions = lists_ref.shape[0]
    rep = arrived_ref.shape[0] // regions
    options = arrived_ref.shape[1]
    applied = block_sums(arrived_ref, lists_ref)
    dual = jnp.maximum(shift_ref[lax.axis_index("rep")] + DUAL_STEP * applied, 0.0)
    blocks = [dual[b * options : (b + 1) * options, :] for b in range(BLOCKS)]

    def one(r, carry):
        block, lane = group_place(lists_ref[pl.ds(r, 1), :])
        block = jnp.broadcast_to(block, (options, LANES))
        lane = jnp.broadcast_to(lane, (options, LANES))
        found = jnp.take_along_axis(blocks[0], lane, axis=1)
        for b in range(1, BLOCKS):
            found = jnp.where(block == b, jnp.take_along_axis(blocks[b], lane, axis=1), found)
        for k in range(rep):
            picked_ref[r * rep + k] = found
        return carry

    each_region(regions, one)


def half_kernel(arrived_ref, lists_ref, base_ref, part_ref):
    sent = arrived_ref.shape[1]
    shares = base_ref.shape[0]
    mine = lax.axis_index("rep") % shares
    sums = block_sums(arrived_ref, lists_ref)
    lines = []
    for b in range(BLOCKS):
        block = jnp.maximum(base_ref[mine, b] + sums[b * sent : (b + 1) * sent, :], 0.0)
        whole = jnp.concatenate([jnp.where(mine == h, block, 0.0) for h in range(shares)], axis=0)
        lines.append(whole)
        lines.append(pltpu.roll(whole, LANES // 2, 1))
    part_ref[...] = jnp.concatenate(lines, axis=0).T[: part_ref.shape[0], :]


def last_kernel(mine_ref, other_ref, fresh_ref, dual_far, primal_far, sum_ref, sems):
    copy_primal = pltpu.make_async_copy(fresh_ref, primal_far, sems.at[0])
    copy_primal.start()
    sum_ref[...] = mine_ref[...] + other_ref[...]
    copy_dual = pltpu.make_async_copy(sum_ref, dual_far, sems.at[1])
    copy_dual.start()
    copy_primal.wait()
    copy_dual.wait()


def call(kernel, outs, scratch=(), ins=None):
    vmem = pl.BlockSpec(memory_space=pltpu.VMEM)
    hbm = pl.BlockSpec(memory_space=pltpu.HBM)
    params = {} if ins is None else {"in_specs": [hbm if far else vmem for far in ins]}
    return pl.pallas_call(
        kernel,
        out_shape=[jax.ShapeDtypeStruct(shape, kind) for shape, kind, _ in outs],
        out_specs=[hbm if far else vmem for _, _, far in outs],
        scratch_shapes=list(scratch),
        compiler_params=pltpu.CompilerParams(vmem_limit_bytes=VMEM_LIMIT),
        **params,
    )


def far(x):
    return pltpu.with_memory_space_constraint(x, pltpu.HBM)


def local(unit_cost, start_primal, start_dual, quota_bound, person_slot, cell_lists):
    options, persons = unit_cost.shape
    regions = lax.axis_size("region")
    rep = lax.axis_size("rep")
    quarter = options // rep
    groups = quota_bound.shape[0] // options
    rows = persons // LANES
    halves = options // SUBLANES

    def to_tiles(x):
        x = x.reshape(halves, SUBLANES, rows, LANES).transpose(0, 2, 1, 3)
        return x.reshape(options * rows, LANES)

    def from_tiles(x):
        x = x.reshape(halves, rows, SUBLANES, LANES).transpose(0, 2, 1, 3)
        return x.reshape(options, persons)

    def array(*shape, kind=jnp.float32, far=False):
        return (shape, kind, far)

    flat = (groups * options // LANES, LANES)
    tiles = array(options * rows, LANES)
    half = options // 2
    base_rows = array(2, BLOCKS, half, LANES)
    quarters = array(regions * rep, quarter, LANES)
    half_rows = array(regions * rep, half, LANES)
    both = ("region", "rep")
    exchange = functools.partial(lax.all_to_all, split_axis=0, concat_axis=0, tiled=True)

    picked, shift, base, lists, slots, cost, primal = call(
        functools.partial(first_kernel, options),
        (
            array(regions, options + SUBLANES, LANES),
            array(rep, BLOCKS * quarter, LANES),
            base_rows,
            array(regions, LANES, kind=jnp.int32),
            array(rows, LANES, kind=jnp.int32),
            tiles,
            tiles,
        ),
        (pltpu.VMEM(flat, jnp.float32), pltpu.VMEM(flat, jnp.float32), pltpu.SemaphoreType.DMA((6,))),
        (True,) * 6,
    )(
        far(cell_lists[0]),
        far(start_dual.reshape(flat)),
        far(quota_bound.reshape(flat)),
        far(person_slot.reshape(rows, LANES)),
        far(to_tiles(unit_cost)),
        far(to_tiles(start_primal)),
    )
    first_prices = exchange(picked, "region")
    scratch = ()
    if regions > CHUNK:
        kept = ((options, persons), (options, persons), (PACKED, persons), (persons, WIDE))
        scratch = tuple(pltpu.VMEM(shape, jnp.bfloat16) for shape in kept)
    turned = array(persons, LANES, kind=jnp.bfloat16)
    primal, sums, turned = call(
        functools.partial(person_kernel, options, rep, False), (tiles, quarters, turned), scratch
    )(first_prices, slots, cost, primal)
    arrived = exchange(sums, both)
    (picked,) = call(middle_kernel, (quarters,))(arrived, lists, shift)
    prices = exchange(picked, both)
    primal, sums = call(functools.partial(person_kernel, options, rep, True), (tiles, half_rows), scratch)(
        prices, first_prices, turned, slots, cost, primal
    )
    arrived = exchange(sums, both)
    (part,) = call(half_kernel, (array(*flat),))(arrived, lists, base)
    other = lax.ppermute(part, "rep", [(k, k ^ 1) for k in range(rep)])
    dual, primal = call(
        last_kernel,
        (array(*flat, far=True), array(*tiles[0], far=True)),
        (pltpu.VMEM(flat, jnp.float32), pltpu.SemaphoreType.DMA((2,))),
    )(part, other, primal)
    return (from_tiles(primal), dual.reshape(-1))


def solution(mesh):
    placed = (
        P(None, ("region", "rep")),
        P(None, ("region", "rep")),
        P("region"),
        P("region"),
        P(("region", "rep")),
        P("region", None, None),
    )
    return jax.shard_map(
        local,
        mesh=mesh,
        in_specs=placed,
        out_specs=(P(None, ("region", "rep")), P("region")),
        check_vma=False,
    )
```

```python
import functools

import jax
import jax.numpy as jnp
from jax import lax
from jax.experimental import pallas as pl
from jax.experimental.pallas import tpu as pltpu
from jax.sharding import PartitionSpec as P

ITERS = 2
BISECT = 30
PRIMAL_STEP = 0.5
DUAL_STEP = 0.25
LANES = 128
SUBLANES = 8
CHUNK = 8
PACKED = 16
WIDE = 256
LANE_BITS = LANES.bit_length() - 1
WIDE_BITS = WIDE.bit_length() - 1
BLOCKS = 4
VMEM_LIMIT = 48 * 1024 * 1024


def sorting_network(count):
    pairs = []
    p = 1
    while p < count:
        k = p
        while k >= 1:
            for j in range(k % p, count - k, 2 * k):
                for i in range(min(k, count - j - k)):
                    if (i + j) // (2 * p) == (i + j + k) // (2 * p):
                        pairs.append((i + j, i + j + k))
            k //= 2
        p *= 2
    return pairs


def repeat_chunks(total, body, init):
    if total == 1:
        return body(0, init)
    return lax.fori_loop(0, total, body, init)


def simplex_theta(values):
    ranked = list(values)
    for a, b in sorting_network(len(values)):
        ranked[a], ranked[b] = jnp.maximum(ranked[a], ranked[b]), jnp.minimum(ranked[a], ranked[b])
    largest = ranked[0]
    total = jnp.zeros_like(largest)
    best = jnp.full_like(largest, -1.0)
    for k in range(1, len(values)):
        total = total + (ranked[k] - largest)
        best = jnp.maximum(best, (total - 1.0) * (1.0 / (k + 1)))
    cells = float(2**BISECT)
    step = jnp.maximum(jnp.ceil((best + 1.0) * cells), 1.0) - 0.5
    return (largest - 1.0) + step * (1.0 / cells)


def split_two(x):
    high = x.astype(jnp.bfloat16)
    low = (x - high.astype(jnp.float32)).astype(jnp.bfloat16)
    return high, low


def one_hot(index, count):
    wide = jnp.broadcast_to(index.astype(jnp.float32), (PACKED, index.shape[1])).astype(jnp.bfloat16)
    lines = []
    for first in range(0, count, PACKED):
        here = lax.broadcasted_iota(jnp.int32, wide.shape, 0) + first
        hit = wide == here.astype(jnp.float32).astype(jnp.bfloat16)
        lines.append(jnp.where(hit, jnp.bfloat16(1), jnp.bfloat16(0)))
    return jnp.concatenate(lines, axis=0)


def product(left, right):
    return lax.dot_general(left, right, (((1,), (1,)), ((), ())), preferred_element_type=jnp.float32)


def group_place(lists):
    return (lists & (SUBLANES - 1)) >> 1, (lists & 1) * (LANES // 2) + (lists >> 3)


def each_region(regions, body):
    if regions <= CHUNK:
        for r in range(regions):
            body(r, 0)
    else:
        lax.fori_loop(0, regions, body, 0)


def turn_rows(flat, options):
    turned = jnp.concatenate([flat, flat], axis=0).T
    left = lax.broadcasted_iota(jnp.int32, (options, LANES), 1) < LANES // 2
    pairs = [turned[i * options : (i + 1) * options, :] for i in range(2 * BLOCKS)]
    return [jnp.where(left, pairs[2 * b], pairs[2 * b + 1]) for b in range(BLOCKS)]


def first_kernel(options, *refs):
    far, outs, (dual_ref, quota_ref, sems) = refs[:6], refs[6:13], refs[13:]
    picked_ref, shift_ref, base_ref, lists_ref, slot_ref, cost_ref, primal_ref = outs
    targets = (lists_ref, dual_ref, quota_ref, slot_ref, cost_ref, primal_ref)
    copies = [
        pltpu.make_async_copy(source, target, sems.at[i]) for i, (source, target) in enumerate(zip(far, targets))
    ]
    for copy in copies:
        copy.start()
    regions = lists_ref.shape[0]
    quarter = shift_ref.shape[1] // BLOCKS
    there = lax.broadcasted_iota(jnp.int32, (LANES, LANES), 0)
    which = lax.broadcasted_iota(jnp.int32, (SUBLANES, LANES), 0)

    def count_up(chunk, total):
        lefts, rights = [], []
        for i in range(CHUNK):
            block, lane = group_place(lists_ref[pl.ds(chunk * CHUNK + i, 1), :])
            lefts.append(jnp.where(block == which, 1.0, 0.0).astype(jnp.bfloat16))
            rights.append(one_hot(lane, LANES))
        return total + product(jnp.concatenate(lefts, axis=1), jnp.concatenate(rights, axis=1))

    for copy in copies[:3]:
        copy.wait()
    counts = repeat_chunks(regions // CHUNK, count_up, jnp.zeros((SUBLANES, LANES), jnp.float32))
    shares = 1.0 / jnp.maximum(counts, 1.0)
    duals = turn_rows(dual_ref[...], options)

    def one(r, carry):
        block, lane = group_place(lists_ref[pl.ds(r, 1), :])
        wide_block = jnp.broadcast_to(block, (options, LANES))
        wide_lane = jnp.broadcast_to(lane, (options, LANES))
        found = jnp.take_along_axis(duals[0], wide_lane, axis=1)
        for b in range(1, BLOCKS):
            found = jnp.where(wide_block == b, jnp.take_along_axis(duals[b], wide_lane, axis=1), found)
        picked_ref[r, 0:options, :] = found
        share = jnp.take_along_axis(shares, wide_lane[:SUBLANES], axis=1)
        share = jnp.sum(jnp.where(block == which, share, 0.0), axis=0, keepdims=True)
        picked_ref[r, options : options + SUBLANES, :] = jnp.broadcast_to(share, (SUBLANES, LANES))
        return carry

    each_region(regions, one)
    for b, quota in enumerate(turn_rows(quota_ref[...], options)):
        pull = DUAL_STEP * quota
        shift = duals[b] - pull
        for k in range(options // quarter):
            shift_ref[k, b * quarter : (b + 1) * quarter, :] = shift[k * quarter : (k + 1) * quarter, :]
        alone = duals[b]
        for _ in range(ITERS - 1):
            alone = jnp.maximum(alone - pull, 0.0)
        named = jnp.broadcast_to(counts[b : b + 1, :], alone.shape) > 0.0
        base = jnp.where(named, 0.0, alone) - pull
        for h in range(base_ref.shape[0]):
            base_ref[h, b] = base[h * base_ref.shape[2] : (h + 1) * base_ref.shape[2], :]
    for copy in copies[3:]:
        copy.wait()


def person_kernel(options, rep, last, *refs):
    if last:
        prices_ref, share_ref, turned_ref, slot_ref, cost_ref, primal_ref, fresh_ref, sums_ref, *kept_refs = refs
        regions = share_ref.shape[0]
    else:
        prices_ref, slot_ref, cost_ref, primal_ref, fresh_ref, sums_ref, turned_ref, *kept_refs = refs
        regions = prices_ref.shape[0]
    quarter = options // rep
    rows = slot_ref.shape[0]
    halves = options // SUBLANES
    chunks = regions // CHUNK
    blocks = CHUNK * LANES // WIDE
    groups = rows // SUBLANES
    sent = sums_ref.shape[1]

    def price(d, o):
        if last:
            return prices_ref[d * rep + o // quarter, o % quarter : o % quarter + 1, :]
        return prices_ref[d, o : o + 1, :]

    def operands(c):
        tiles = [slice((h * rows + c) * SUBLANES, (h * rows + c + 1) * SUBLANES) for h in range(halves)]
        x = jnp.concatenate([2.0 * fresh_ref[tile, :] - primal_ref[tile, :] for tile in tiles], axis=0)
        high, low = split_two(x)
        span = slice(c * LANES, (c + 1) * LANES)
        line = slot_ref[c : c + 1, :]
        if last:
            turned = turned_ref[span, :]
        else:
            within = jnp.broadcast_to((line & (WIDE - 1)).astype(jnp.float32), (LANES, LANES))
            turned = within.astype(jnp.bfloat16).T
            turned_ref[span, :] = turned
        turned = jnp.concatenate([turned] * (WIDE // LANES), axis=1)
        here = lax.broadcasted_iota(jnp.int32, (PACKED, WIDE), 1).astype(jnp.float32).astype(jnp.bfloat16)
        hot = [
            jnp.where(turned[first : first + PACKED] == here, jnp.bfloat16(1), jnp.bfloat16(0))
            for first in range(0, LANES, PACKED)
        ]
        number = jnp.broadcast_to((line >> WIDE_BITS).astype(jnp.float32), (PACKED, LANES)).astype(jnp.bfloat16)
        return high, low, number, jnp.concatenate(hot, axis=0)

    def partial_sums(chunk, pieces):
        lines = []
        for part in range(2):
            for e in range(blocks):
                mine = jnp.asarray(chunk * blocks + e, jnp.float32).astype(jnp.bfloat16)
                kept = [jnp.where(piece[2] == mine, piece[part], jnp.bfloat16(0)) for piece in pieces]
                lines.append(jnp.concatenate(kept, axis=1))
        hot = jnp.concatenate([piece[3] for piece in pieces], axis=0)
        return jnp.dot(jnp.concatenate(lines, axis=0), hot, preferred_element_type=jnp.float32)

    def hand_on(chunk, total):
        total = total[: blocks * options] + total[blocks * options :]
        for i in range(CHUNK):
            d = chunk * CHUNK + i
            e, h = divmod(i, WIDE // LANES)
            block = total[e * options : (e + 1) * options, h * LANES : (h + 1) * LANES]
            if last:
                share = jnp.where(lax.axis_index("rep") == 0, share_ref[d, options : options + SUBLANES, :], 0.0)
                held = jnp.concatenate([price(d, o) for o in range(options)], axis=0)
                block = DUAL_STEP * block + held * jnp.concatenate([share] * halves, axis=0)
            for k in range(rep):
                first = k * sent % options
                sums_ref[d * rep + k] = block[first : first + sent, :]

    for g in range(groups):
        slot = slot_ref[g * SUBLANES : (g + 1) * SUBLANES, :]
        owner = slot >> LANE_BITS
        within = slot & (LANES - 1)

        def pick(chunk, found):
            near = owner - chunk * CHUNK
            here = (near >= 0) & (near < CHUNK)
            bits = [(near & (1 << i)) == 0 for i in range(CHUNK.bit_length() - 1)]
            picked = []
            for o in range(options):
                level = []
                for d in range(CHUNK):
                    table = jnp.broadcast_to(price(chunk * CHUNK + d, o), (SUBLANES, LANES))
                    level.append(jnp.take_along_axis(table, within, axis=1))
                for low in bits:
                    level = [jnp.where(low, a, b) for a, b in zip(level[::2], level[1::2])]
                picked.append(level[0] if chunks == 1 else jnp.where(here, level[0], found[o]))
            return tuple(picked)

        zero = jnp.zeros((SUBLANES, LANES), jnp.float32)
        adjoint = repeat_chunks(chunks, pick, (zero,) * options)
        places = []
        values = []
        for o in range(options):
            first = ((o // SUBLANES) * rows + g * SUBLANES) * SUBLANES + o % SUBLANES
            at = pl.ds(first, SUBLANES, stride=SUBLANES)
            places.append(at)
            values.append(primal_ref[at, :] - PRIMAL_STEP * (cost_ref[at, :] + adjoint[o]))
        theta = simplex_theta(values)
        for o in range(options):
            fresh_ref[places[o], :] = jnp.maximum(values[o] - theta, 0.0)

    pieces = [operands(c) for c in range(rows)]
    if chunks == 1:
        hand_on(0, partial_sums(0, pieces))
    else:
        for c, piece in enumerate(pieces):
            span = slice(c * LANES, (c + 1) * LANES)
            for ref, value in zip(kept_refs[:3], piece):
                ref[:, span] = value
            kept_refs[3][span, :] = piece[3]

        def add_up(chunk, carry):
            hand_on(chunk, partial_sums(chunk, [[ref[...] for ref in kept_refs]]))
            return carry

        lax.fori_loop(0, chunks, add_up, 0)


def block_sums(arrived_ref, lists_ref):
    regions = lists_ref.shape[0]
    rep = arrived_ref.shape[0] // regions
    options = arrived_ref.shape[1]
    lines = BLOCKS * options
    copies = max(1, SUBLANES // options)
    tall = copies * options
    row = lax.broadcasted_iota(jnp.int32, (tall, CHUNK * LANES), 0) // options

    def add_up(chunk, total):
        sums, hots, numbers = [], [], []
        for i in range(CHUNK):
            r = chunk * CHUNK + i
            x = arrived_ref[r * rep]
            for k in range(1, rep):
                x = x + arrived_ref[r * rep + k]
            sums.append(jnp.concatenate([x] * copies, axis=0))
            block, lane = group_place(lists_ref[pl.ds(r, 1), :])
            hots.append(one_hot(lane, LANES))
            numbers.append(jnp.broadcast_to(block, (tall, LANES)))
        x = jnp.concatenate(sums, axis=1)
        number = jnp.concatenate(numbers, axis=1) - row
        high = x.astype(jnp.bfloat16).astype(jnp.float32)
        left = [
            jnp.where(number == first, part, 0.0) for part in (high, x - high) for first in range(0, BLOCKS, copies)
        ]
        found = product(jnp.concatenate(left, axis=0).astype(jnp.bfloat16), jnp.concatenate(hots, axis=1))
        return total + found[:lines] + found[lines:]

    return repeat_chunks(regions // CHUNK, add_up, jnp.zeros((lines, LANES), jnp.float32))


def middle_kernel(arrived_ref, lists_ref, shift_ref, picked_ref):
    regions = lists_ref.shape[0]
    rep = arrived_ref.shape[0] // regions
    options = arrived_ref.shape[1]
    applied = block_sums(arrived_ref, lists_ref)
    dual = jnp.maximum(shift_ref[lax.axis_index("rep")] + DUAL_STEP * applied, 0.0)
    blocks = [dual[b * options : (b + 1) * options, :] for b in range(BLOCKS)]

    def one(r, carry):
        block, lane = group_place(lists_ref[pl.ds(r, 1), :])
        block = jnp.broadcast_to(block, (options, LANES))
        lane = jnp.broadcast_to(lane, (options, LANES))
        found = jnp.take_along_axis(blocks[0], lane, axis=1)
        for b in range(1, BLOCKS):
            found = jnp.where(block == b, jnp.take_along_axis(blocks[b], lane, axis=1), found)
        for k in range(rep):
            picked_ref[r * rep + k] = found
        return carry

    each_region(regions, one)


def half_kernel(arrived_ref, lists_ref, base_ref, part_ref):
    sent = arrived_ref.shape[1]
    shares = base_ref.shape[0]
    mine = lax.axis_index("rep") % shares
    sums = block_sums(arrived_ref, lists_ref)
    lines = []
    for b in range(BLOCKS):
        block = jnp.maximum(base_ref[mine, b] + sums[b * sent : (b + 1) * sent, :], 0.0)
        whole = jnp.concatenate([jnp.where(mine == h, block, 0.0) for h in range(shares)], axis=0)
        lines.append(whole)
        lines.append(pltpu.roll(whole, LANES // 2, 1))
    part_ref[...] = jnp.concatenate(lines, axis=0).T[: part_ref.shape[0], :]


def write_kernel(fresh_ref, primal_far, sem):
    copy = pltpu.make_async_copy(fresh_ref, primal_far, sem)
    copy.start()
    copy.wait()


def call(kernel, outs, scratch=(), ins=None):
    vmem = pl.BlockSpec(memory_space=pltpu.VMEM)
    hbm = pl.BlockSpec(memory_space=pltpu.HBM)
    params = {} if ins is None else {"in_specs": [hbm if far else vmem for far in ins]}
    return pl.pallas_call(
        kernel,
        out_shape=[jax.ShapeDtypeStruct(shape, kind) for shape, kind, _ in outs],
        out_specs=[hbm if far else vmem for _, _, far in outs],
        scratch_shapes=list(scratch),
        compiler_params=pltpu.CompilerParams(vmem_limit_bytes=VMEM_LIMIT),
        **params,
    )


def far(x):
    return pltpu.with_memory_space_constraint(x, pltpu.HBM)


def local(unit_cost, start_primal, start_dual, quota_bound, person_slot, cell_lists):
    options, persons = unit_cost.shape
    regions = lax.axis_size("region")
    rep = lax.axis_size("rep")
    quarter = options // rep
    groups = quota_bound.shape[0] // options
    rows = persons // LANES
    halves = options // SUBLANES

    def to_tiles(x):
        x = x.reshape(halves, SUBLANES, rows, LANES).transpose(0, 2, 1, 3)
        return x.reshape(options * rows, LANES)

    def from_tiles(x):
        x = x.reshape(halves, rows, SUBLANES, LANES).transpose(0, 2, 1, 3)
        return x.reshape(options, persons)

    def array(*shape, kind=jnp.float32, far=False):
        return (shape, kind, far)

    flat = (groups * options // LANES, LANES)
    tiles = array(options * rows, LANES)
    half = options // 2
    base_rows = array(2, BLOCKS, half, LANES)
    quarters = array(regions * rep, quarter, LANES)
    half_rows = array(regions * rep, half, LANES)
    both = ("region", "rep")
    exchange = functools.partial(lax.all_to_all, split_axis=0, concat_axis=0, tiled=True)

    picked, shift, base, lists, slots, cost, primal = call(
        functools.partial(first_kernel, options),
        (
            array(regions, options + SUBLANES, LANES),
            array(rep, BLOCKS * quarter, LANES),
            base_rows,
            array(regions, LANES, kind=jnp.int32),
            array(rows, LANES, kind=jnp.int32),
            tiles,
            tiles,
        ),
        (pltpu.VMEM(flat, jnp.float32), pltpu.VMEM(flat, jnp.float32), pltpu.SemaphoreType.DMA((6,))),
        (True,) * 6,
    )(
        far(cell_lists[0]),
        far(start_dual.reshape(flat)),
        far(quota_bound.reshape(flat)),
        far(person_slot.reshape(rows, LANES)),
        far(to_tiles(unit_cost)),
        far(to_tiles(start_primal)),
    )
    first_prices = exchange(picked, "region")
    scratch = ()
    if regions > CHUNK:
        kept = ((options, persons), (options, persons), (PACKED, persons), (persons, WIDE))
        scratch = tuple(pltpu.VMEM(shape, jnp.bfloat16) for shape in kept)
    turned = array(persons, LANES, kind=jnp.bfloat16)
    primal, sums, turned = call(
        functools.partial(person_kernel, options, rep, False), (tiles, quarters, turned), scratch
    )(first_prices, slots, cost, primal)
    arrived = exchange(sums, both)
    (picked,) = call(middle_kernel, (quarters,))(arrived, lists, shift)
    prices = exchange(picked, both)
    primal, sums = call(functools.partial(person_kernel, options, rep, True), (tiles, half_rows), scratch)(
        prices, first_prices, turned, slots, cost, primal
    )
    arrived = exchange(sums, both)
    (part,) = call(half_kernel, (array(*flat),))(arrived, lists, base)
    other = lax.ppermute(part, "rep", [(k, k ^ 1) for k in range(rep)])
    (primal,) = call(write_kernel, (array(*tiles[0], far=True),), (pltpu.SemaphoreType.DMA,))(primal)
    dual = part + other
    return (from_tiles(primal), dual.reshape(-1))


def solution(mesh):
    placed = (
        P(None, ("region", "rep")),
        P(None, ("region", "rep")),
        P("region"),
        P("region"),
        P(("region", "rep")),
        P("region", None, None),
    )
    return jax.shard_map(
        local,
        mesh=mesh,
        in_specs=placed,
        out_specs=(P(None, ("region", "rep")), P("region")),
        check_vma=False,
    )
```

```python
import functools

import jax
import jax.numpy as jnp
from jax import lax
from jax.experimental import pallas as pl
from jax.experimental.pallas import tpu as pltpu
from jax.sharding import PartitionSpec as P

ITERS = 2
BISECT = 30
PRIMAL_STEP = 0.5
DUAL_STEP = 0.25
LANES = 128
SUBLANES = 8
CHUNK = 8
PACKED = 16
WIDE = 256
LANE_BITS = LANES.bit_length() - 1
WIDE_BITS = WIDE.bit_length() - 1
BLOCKS = 4
VMEM_LIMIT = 48 * 1024 * 1024


def sorting_network(count):
    pairs = []
    p = 1
    while p < count:
        k = p
        while k >= 1:
            for j in range(k % p, count - k, 2 * k):
                for i in range(min(k, count - j - k)):
                    if (i + j) // (2 * p) == (i + j + k) // (2 * p):
                        pairs.append((i + j, i + j + k))
            k //= 2
        p *= 2
    return pairs


def repeat_chunks(total, body, init):
    if total == 1:
        return body(0, init)
    return lax.fori_loop(0, total, body, init)


def simplex_theta(values):
    ranked = list(values)
    for a, b in sorting_network(len(values)):
        ranked[a], ranked[b] = jnp.maximum(ranked[a], ranked[b]), jnp.minimum(ranked[a], ranked[b])
    largest = ranked[0]
    total = jnp.zeros_like(largest)
    best = jnp.full_like(largest, -1.0)
    for k in range(1, len(values)):
        total = total + (ranked[k] - largest)
        best = jnp.maximum(best, (total - 1.0) * (1.0 / (k + 1)))
    cells = float(2**BISECT)
    step = jnp.maximum(jnp.ceil((best + 1.0) * cells), 1.0) - 0.5
    return (largest - 1.0) + step * (1.0 / cells)


def split_two(x):
    high = x.astype(jnp.bfloat16)
    low = (x - high.astype(jnp.float32)).astype(jnp.bfloat16)
    return high, low


def one_hot(index, count):
    wide = jnp.broadcast_to(index.astype(jnp.float32), (PACKED, index.shape[1])).astype(jnp.bfloat16)
    lines = []
    for first in range(0, count, PACKED):
        here = lax.broadcasted_iota(jnp.int32, wide.shape, 0) + first
        hit = wide == here.astype(jnp.float32).astype(jnp.bfloat16)
        lines.append(jnp.where(hit, jnp.bfloat16(1), jnp.bfloat16(0)))
    return jnp.concatenate(lines, axis=0)


def product(left, right):
    return lax.dot_general(left, right, (((1,), (1,)), ((), ())), preferred_element_type=jnp.float32)


def group_place(lists):
    return (lists & (SUBLANES - 1)) >> 1, (lists & 1) * (LANES // 2) + (lists >> 3)


def each_region(regions, body):
    if regions <= CHUNK:
        for r in range(regions):
            body(r, 0)
    else:
        lax.fori_loop(0, regions, body, 0)


def turn_rows(flat, options):
    turned = jnp.concatenate([flat, flat], axis=0).T
    left = lax.broadcasted_iota(jnp.int32, (options, LANES), 1) < LANES // 2
    pairs = [turned[i * options : (i + 1) * options, :] for i in range(2 * BLOCKS)]
    return [jnp.where(left, pairs[2 * b], pairs[2 * b + 1]) for b in range(BLOCKS)]


def first_kernel(options, *refs):
    far, outs, (dual_ref, quota_ref, sems) = refs[:6], refs[6:13], refs[13:]
    picked_ref, shift_ref, base_ref, lists_ref, slot_ref, cost_ref, primal_ref = outs
    targets = (lists_ref, dual_ref, quota_ref, slot_ref, cost_ref, primal_ref)
    copies = [
        pltpu.make_async_copy(source, target, sems.at[i]) for i, (source, target) in enumerate(zip(far, targets))
    ]
    for copy in copies:
        copy.start()
    regions = lists_ref.shape[0]
    quarter = shift_ref.shape[1] // BLOCKS
    there = lax.broadcasted_iota(jnp.int32, (LANES, LANES), 0)
    which = lax.broadcasted_iota(jnp.int32, (SUBLANES, LANES), 0)

    def count_up(chunk, total):
        lefts, rights = [], []
        for i in range(CHUNK):
            block, lane = group_place(lists_ref[pl.ds(chunk * CHUNK + i, 1), :])
            lefts.append(jnp.where(block == which, 1.0, 0.0).astype(jnp.bfloat16))
            rights.append(one_hot(lane, LANES))
        return total + product(jnp.concatenate(lefts, axis=1), jnp.concatenate(rights, axis=1))

    for copy in copies[:3]:
        copy.wait()
    counts = repeat_chunks(regions // CHUNK, count_up, jnp.zeros((SUBLANES, LANES), jnp.float32))
    shares = 1.0 / jnp.maximum(counts, 1.0)
    duals = turn_rows(dual_ref[...], options)

    def one(r, carry):
        block, lane = group_place(lists_ref[pl.ds(r, 1), :])
        wide_block = jnp.broadcast_to(block, (options, LANES))
        wide_lane = jnp.broadcast_to(lane, (options, LANES))
        found = jnp.take_along_axis(duals[0], wide_lane, axis=1)
        for b in range(1, BLOCKS):
            found = jnp.where(wide_block == b, jnp.take_along_axis(duals[b], wide_lane, axis=1), found)
        picked_ref[r, 0:options, :] = found
        share = jnp.take_along_axis(shares, wide_lane[:SUBLANES], axis=1)
        share = jnp.sum(jnp.where(block == which, share, 0.0), axis=0, keepdims=True)
        picked_ref[r, options : options + SUBLANES, :] = jnp.broadcast_to(share, (SUBLANES, LANES))
        return carry

    each_region(regions, one)
    for b, quota in enumerate(turn_rows(quota_ref[...], options)):
        pull = DUAL_STEP * quota
        shift = duals[b] - pull
        for k in range(options // quarter):
            shift_ref[k, b * quarter : (b + 1) * quarter, :] = shift[k * quarter : (k + 1) * quarter, :]
        alone = duals[b]
        for _ in range(ITERS - 1):
            alone = jnp.maximum(alone - pull, 0.0)
        named = jnp.broadcast_to(counts[b : b + 1, :], alone.shape) > 0.0
        base = jnp.where(named, 0.0, alone) - pull
        for h in range(base_ref.shape[0]):
            base_ref[h, b] = base[h * base_ref.shape[2] : (h + 1) * base_ref.shape[2], :]
    for copy in copies[3:]:
        copy.wait()


def person_kernel(options, rep, last, *refs):
    if last:
        prices_ref, share_ref, turned_ref, slot_ref, cost_ref, primal_ref, fresh_ref, sums_ref, *kept_refs = refs
        regions = share_ref.shape[0]
    else:
        prices_ref, slot_ref, cost_ref, primal_ref, fresh_ref, sums_ref, turned_ref, *kept_refs = refs
        regions = prices_ref.shape[0]
    quarter = options // rep
    rows = slot_ref.shape[0]
    halves = options // SUBLANES
    chunks = regions // CHUNK
    blocks = CHUNK * LANES // WIDE
    groups = rows // SUBLANES
    sent = sums_ref.shape[1]

    def price(d, o):
        if last:
            return prices_ref[o // quarter * regions + d, o % quarter : o % quarter + 1, :]
        return prices_ref[d, o : o + 1, :]

    def operands(c):
        tiles = [slice((h * rows + c) * SUBLANES, (h * rows + c + 1) * SUBLANES) for h in range(halves)]
        x = jnp.concatenate([2.0 * fresh_ref[tile, :] - primal_ref[tile, :] for tile in tiles], axis=0)
        high, low = split_two(x)
        span = slice(c * LANES, (c + 1) * LANES)
        line = slot_ref[c : c + 1, :]
        if last:
            turned = turned_ref[span, :]
        else:
            within = jnp.broadcast_to((line & (WIDE - 1)).astype(jnp.float32), (LANES, LANES))
            turned = within.astype(jnp.bfloat16).T
            turned_ref[span, :] = turned
        turned = jnp.concatenate([turned] * (WIDE // LANES), axis=1)
        here = lax.broadcasted_iota(jnp.int32, (PACKED, WIDE), 1).astype(jnp.float32).astype(jnp.bfloat16)
        hot = [
            jnp.where(turned[first : first + PACKED] == here, jnp.bfloat16(1), jnp.bfloat16(0))
            for first in range(0, LANES, PACKED)
        ]
        number = jnp.broadcast_to((line >> WIDE_BITS).astype(jnp.float32), (PACKED, LANES)).astype(jnp.bfloat16)
        return high, low, number, jnp.concatenate(hot, axis=0)

    def partial_sums(chunk, pieces):
        lines = []
        for part in range(2):
            for e in range(blocks):
                mine = jnp.asarray(chunk * blocks + e, jnp.float32).astype(jnp.bfloat16)
                kept = [jnp.where(piece[2] == mine, piece[part], jnp.bfloat16(0)) for piece in pieces]
                lines.append(jnp.concatenate(kept, axis=1))
        hot = jnp.concatenate([piece[3] for piece in pieces], axis=0)
        return jnp.dot(jnp.concatenate(lines, axis=0), hot, preferred_element_type=jnp.float32)

    def hand_on(chunk, total):
        total = total[: blocks * options] + total[blocks * options :]
        for i in range(CHUNK):
            d = chunk * CHUNK + i
            e, h = divmod(i, WIDE // LANES)
            block = total[e * options : (e + 1) * options, h * LANES : (h + 1) * LANES]
            if last:
                share = jnp.where(lax.axis_index("rep") == 0, share_ref[d, options : options + SUBLANES, :], 0.0)
                held = jnp.concatenate([price(d, o) for o in range(options)], axis=0)
                block = DUAL_STEP * block + held * jnp.concatenate([share] * halves, axis=0)
            for k in range(rep):
                first = k * sent % options
                sums_ref[k * regions + d] = block[first : first + sent, :]

    for g in range(groups):
        slot = slot_ref[g * SUBLANES : (g + 1) * SUBLANES, :]
        owner = slot >> LANE_BITS
        within = slot & (LANES - 1)

        def pick(chunk, found):
            near = owner - chunk * CHUNK
            here = (near >= 0) & (near < CHUNK)
            bits = [(near & (1 << i)) == 0 for i in range(CHUNK.bit_length() - 1)]
            picked = []
            for o in range(options):
                level = []
                for d in range(CHUNK):
                    table = jnp.broadcast_to(price(chunk * CHUNK + d, o), (SUBLANES, LANES))
                    level.append(jnp.take_along_axis(table, within, axis=1))
                for low in bits:
                    level = [jnp.where(low, a, b) for a, b in zip(level[::2], level[1::2])]
                picked.append(level[0] if chunks == 1 else jnp.where(here, level[0], found[o]))
            return tuple(picked)

        zero = jnp.zeros((SUBLANES, LANES), jnp.float32)
        adjoint = repeat_chunks(chunks, pick, (zero,) * options)
        places = []
        values = []
        for o in range(options):
            first = ((o // SUBLANES) * rows + g * SUBLANES) * SUBLANES + o % SUBLANES
            at = pl.ds(first, SUBLANES, stride=SUBLANES)
            places.append(at)
            values.append(primal_ref[at, :] - PRIMAL_STEP * (cost_ref[at, :] + adjoint[o]))
        theta = simplex_theta(values)
        for o in range(options):
            fresh_ref[places[o], :] = jnp.maximum(values[o] - theta, 0.0)

    pieces = [operands(c) for c in range(rows)]
    if chunks == 1:
        hand_on(0, partial_sums(0, pieces))
    else:
        for c, piece in enumerate(pieces):
            span = slice(c * LANES, (c + 1) * LANES)
            for ref, value in zip(kept_refs[:3], piece):
                ref[:, span] = value
            kept_refs[3][span, :] = piece[3]

        def add_up(chunk, carry):
            hand_on(chunk, partial_sums(chunk, [[ref[...] for ref in kept_refs]]))
            return carry

        lax.fori_loop(0, chunks, add_up, 0)


def block_sums(arrived_ref, lists_ref):
    regions = lists_ref.shape[0]
    rep = arrived_ref.shape[0] // regions
    options = arrived_ref.shape[1]
    lines = BLOCKS * options
    copies = max(1, SUBLANES // options)
    tall = copies * options
    row = lax.broadcasted_iota(jnp.int32, (tall, CHUNK * LANES), 0) // options

    def add_up(chunk, total):
        sums, hots, numbers = [], [], []
        for i in range(CHUNK):
            r = chunk * CHUNK + i
            x = arrived_ref[r]
            for k in range(1, rep):
                x = x + arrived_ref[k * regions + r]
            sums.append(jnp.concatenate([x] * copies, axis=0))
            block, lane = group_place(lists_ref[pl.ds(r, 1), :])
            hots.append(one_hot(lane, LANES))
            numbers.append(jnp.broadcast_to(block, (tall, LANES)))
        x = jnp.concatenate(sums, axis=1)
        number = jnp.concatenate(numbers, axis=1) - row
        high = x.astype(jnp.bfloat16).astype(jnp.float32)
        left = [
            jnp.where(number == first, part, 0.0) for part in (high, x - high) for first in range(0, BLOCKS, copies)
        ]
        found = product(jnp.concatenate(left, axis=0).astype(jnp.bfloat16), jnp.concatenate(hots, axis=1))
        return total + found[:lines] + found[lines:]

    return repeat_chunks(regions // CHUNK, add_up, jnp.zeros((lines, LANES), jnp.float32))


def middle_kernel(arrived_ref, lists_ref, shift_ref, picked_ref):
    regions = lists_ref.shape[0]
    rep = arrived_ref.shape[0] // regions
    options = arrived_ref.shape[1]
    applied = block_sums(arrived_ref, lists_ref)
    dual = jnp.maximum(shift_ref[lax.axis_index("rep")] + DUAL_STEP * applied, 0.0)
    blocks = [dual[b * options : (b + 1) * options, :] for b in range(BLOCKS)]

    def one(r, carry):
        block, lane = group_place(lists_ref[pl.ds(r, 1), :])
        block = jnp.broadcast_to(block, (options, LANES))
        lane = jnp.broadcast_to(lane, (options, LANES))
        found = jnp.take_along_axis(blocks[0], lane, axis=1)
        for b in range(1, BLOCKS):
            found = jnp.where(block == b, jnp.take_along_axis(blocks[b], lane, axis=1), found)
        for k in range(rep):
            picked_ref[k * regions + r] = found
        return carry

    each_region(regions, one)


def half_kernel(arrived_ref, lists_ref, base_ref, part_ref):
    sent = arrived_ref.shape[1]
    shares = base_ref.shape[0]
    mine = lax.axis_index("rep") % shares
    sums = block_sums(arrived_ref, lists_ref)
    lines = []
    for b in range(BLOCKS):
        block = jnp.maximum(base_ref[mine, b] + sums[b * sent : (b + 1) * sent, :], 0.0)
        whole = jnp.concatenate([jnp.where(mine == h, block, 0.0) for h in range(shares)], axis=0)
        lines.append(whole)
        lines.append(pltpu.roll(whole, LANES // 2, 1))
    part_ref[...] = jnp.concatenate(lines, axis=0).T[: part_ref.shape[0], :]


def write_kernel(fresh_ref, primal_far, sem):
    copy = pltpu.make_async_copy(fresh_ref, primal_far, sem)
    copy.start()
    copy.wait()


def call(kernel, outs, scratch=(), ins=None):
    vmem = pl.BlockSpec(memory_space=pltpu.VMEM)
    hbm = pl.BlockSpec(memory_space=pltpu.HBM)
    params = {} if ins is None else {"in_specs": [hbm if far else vmem for far in ins]}
    return pl.pallas_call(
        kernel,
        out_shape=[jax.ShapeDtypeStruct(shape, kind) for shape, kind, _ in outs],
        out_specs=[hbm if far else vmem for _, _, far in outs],
        scratch_shapes=list(scratch),
        compiler_params=pltpu.CompilerParams(vmem_limit_bytes=VMEM_LIMIT),
        **params,
    )


def far(x):
    return pltpu.with_memory_space_constraint(x, pltpu.HBM)


def local(unit_cost, start_primal, start_dual, quota_bound, person_slot, cell_lists):
    options, persons = unit_cost.shape
    regions = lax.axis_size("region")
    rep = lax.axis_size("rep")
    quarter = options // rep
    groups = quota_bound.shape[0] // options
    rows = persons // LANES
    halves = options // SUBLANES

    def to_tiles(x):
        x = x.reshape(halves, SUBLANES, rows, LANES).transpose(0, 2, 1, 3)
        return x.reshape(options * rows, LANES)

    def from_tiles(x):
        x = x.reshape(halves, rows, SUBLANES, LANES).transpose(0, 2, 1, 3)
        return x.reshape(options, persons)

    def array(*shape, kind=jnp.float32, far=False):
        return (shape, kind, far)

    flat = (groups * options // LANES, LANES)
    tiles = array(options * rows, LANES)
    half = options // 2
    base_rows = array(2, BLOCKS, half, LANES)
    quarters = array(regions * rep, quarter, LANES)
    half_rows = array(regions * rep, half, LANES)
    both = ("rep", "region")
    exchange = functools.partial(lax.all_to_all, split_axis=0, concat_axis=0, tiled=True)

    picked, shift, base, lists, slots, cost, primal = call(
        functools.partial(first_kernel, options),
        (
            array(regions, options + SUBLANES, LANES),
            array(rep, BLOCKS * quarter, LANES),
            base_rows,
            array(regions, LANES, kind=jnp.int32),
            array(rows, LANES, kind=jnp.int32),
            tiles,
            tiles,
        ),
        (pltpu.VMEM(flat, jnp.float32), pltpu.VMEM(flat, jnp.float32), pltpu.SemaphoreType.DMA((6,))),
        (True,) * 6,
    )(
        far(cell_lists[0]),
        far(start_dual.reshape(flat)),
        far(quota_bound.reshape(flat)),
        far(person_slot.reshape(rows, LANES)),
        far(to_tiles(unit_cost)),
        far(to_tiles(start_primal)),
    )
    first_prices = exchange(picked, "region")
    scratch = ()
    if regions > CHUNK:
        kept = ((options, persons), (options, persons), (PACKED, persons), (persons, WIDE))
        scratch = tuple(pltpu.VMEM(shape, jnp.bfloat16) for shape in kept)
    turned = array(persons, LANES, kind=jnp.bfloat16)
    primal, sums, turned = call(
        functools.partial(person_kernel, options, rep, False), (tiles, quarters, turned), scratch
    )(first_prices, slots, cost, primal)
    arrived = exchange(sums, both)
    (picked,) = call(middle_kernel, (quarters,))(arrived, lists, shift)
    prices = exchange(picked, both)
    primal, sums = call(functools.partial(person_kernel, options, rep, True), (tiles, half_rows), scratch)(
        prices, first_prices, turned, slots, cost, primal
    )
    arrived = exchange(sums, both)
    (part,) = call(half_kernel, (array(*flat),))(arrived, lists, base)
    other = lax.ppermute(part, "rep", [(k, k ^ 1) for k in range(rep)])
    (primal,) = call(write_kernel, (array(*tiles[0], far=True),), (pltpu.SemaphoreType.DMA,))(primal)
    dual = part + other
    return (from_tiles(primal), dual.reshape(-1))


def solution(mesh):
    placed = (
        P(None, ("region", "rep")),
        P(None, ("region", "rep")),
        P("region"),
        P("region"),
        P(("region", "rep")),
        P("region", None, None),
    )
    return jax.shard_map(
        local,
        mesh=mesh,
        in_specs=placed,
        out_specs=(P(None, ("region", "rep")), P("region")),
        check_vma=False,
    )
```

```python
import functools

import jax
import jax.numpy as jnp
from jax import lax
from jax.experimental import pallas as pl
from jax.experimental.pallas import tpu as pltpu
from jax.sharding import PartitionSpec as P

ITERS = 2
BISECT = 30
PRIMAL_STEP = 0.5
DUAL_STEP = 0.25
LANES = 128
SUBLANES = 8
CHUNK = 8
PACKED = 16
WIDE = 256
LANE_BITS = LANES.bit_length() - 1
WIDE_BITS = WIDE.bit_length() - 1
BLOCKS = 4
VMEM_LIMIT = 48 * 1024 * 1024


def sorting_network(count):
    pairs = []
    p = 1
    while p < count:
        k = p
        while k >= 1:
            for j in range(k % p, count - k, 2 * k):
                for i in range(min(k, count - j - k)):
                    if (i + j) // (2 * p) == (i + j + k) // (2 * p):
                        pairs.append((i + j, i + j + k))
            k //= 2
        p *= 2
    return pairs


def repeat_chunks(total, body, init):
    if total == 1:
        return body(0, init)
    return lax.fori_loop(0, total, body, init)


def simplex_theta(values):
    ranked = list(values)
    for a, b in sorting_network(len(values)):
        ranked[a], ranked[b] = jnp.maximum(ranked[a], ranked[b]), jnp.minimum(ranked[a], ranked[b])
    largest = ranked[0]
    total = jnp.zeros_like(largest)
    best = jnp.full_like(largest, -1.0)
    for k in range(1, len(values)):
        total = total + (ranked[k] - largest)
        best = jnp.maximum(best, (total - 1.0) * (1.0 / (k + 1)))
    cells = float(2**BISECT)
    step = jnp.maximum(jnp.ceil((best + 1.0) * cells), 1.0) - 0.5
    return (largest - 1.0) + step * (1.0 / cells)


def split_two(x):
    high = x.astype(jnp.bfloat16)
    low = (x - high.astype(jnp.float32)).astype(jnp.bfloat16)
    return high, low


def one_hot(index, count):
    wide = jnp.broadcast_to(index.astype(jnp.float32), (PACKED, index.shape[1])).astype(jnp.bfloat16)
    lines = []
    for first in range(0, count, PACKED):
        here = lax.broadcasted_iota(jnp.int32, wide.shape, 0) + first
        hit = wide == here.astype(jnp.float32).astype(jnp.bfloat16)
        lines.append(jnp.where(hit, jnp.bfloat16(1), jnp.bfloat16(0)))
    return jnp.concatenate(lines, axis=0)


def product(left, right):
    return lax.dot_general(left, right, (((1,), (1,)), ((), ())), preferred_element_type=jnp.float32)


def group_place(lists):
    return (lists & (SUBLANES - 1)) >> 1, (lists & 1) * (LANES // 2) + (lists >> 3)


def each_region(regions, body):
    if regions <= CHUNK:
        for r in range(regions):
            body(r, 0)
    else:
        lax.fori_loop(0, regions, body, 0)


def turn_rows(flat, options):
    turned = jnp.concatenate([flat, flat], axis=0).T
    left = lax.broadcasted_iota(jnp.int32, (options, LANES), 1) < LANES // 2
    pairs = [turned[i * options : (i + 1) * options, :] for i in range(2 * BLOCKS)]
    return [jnp.where(left, pairs[2 * b], pairs[2 * b + 1]) for b in range(BLOCKS)]


def first_kernel(options, *refs):
    far, outs, (dual_ref, quota_ref, sems) = refs[:6], refs[6:14], refs[14:]
    picked_ref, shift_ref, base_ref, lists_ref, slot_ref, cost_ref, primal_ref, turned_ref = outs
    targets = (lists_ref, dual_ref, quota_ref, slot_ref, cost_ref, primal_ref)
    copies = [
        pltpu.make_async_copy(source, target, sems.at[i]) for i, (source, target) in enumerate(zip(far, targets))
    ]
    for copy in copies:
        copy.start()
    regions = lists_ref.shape[0]
    quarter = shift_ref.shape[1] // BLOCKS
    there = lax.broadcasted_iota(jnp.int32, (LANES, LANES), 0)
    which = lax.broadcasted_iota(jnp.int32, (SUBLANES, LANES), 0)

    def count_up(chunk, total):
        lefts, rights = [], []
        for i in range(CHUNK):
            block, lane = group_place(lists_ref[pl.ds(chunk * CHUNK + i, 1), :])
            lefts.append(jnp.where(block == which, 1.0, 0.0).astype(jnp.bfloat16))
            rights.append(one_hot(lane, LANES))
        return total + product(jnp.concatenate(lefts, axis=1), jnp.concatenate(rights, axis=1))

    for copy in copies[:4]:
        copy.wait()
    counts = repeat_chunks(regions // CHUNK, count_up, jnp.zeros((SUBLANES, LANES), jnp.float32))
    shares = 1.0 / jnp.maximum(counts, 1.0)
    duals = turn_rows(dual_ref[...], options)

    def one(r, carry):
        block, lane = group_place(lists_ref[pl.ds(r, 1), :])
        wide_block = jnp.broadcast_to(block, (options, LANES))
        wide_lane = jnp.broadcast_to(lane, (options, LANES))
        found = jnp.take_along_axis(duals[0], wide_lane, axis=1)
        for b in range(1, BLOCKS):
            found = jnp.where(wide_block == b, jnp.take_along_axis(duals[b], wide_lane, axis=1), found)
        picked_ref[r, 0:options, :] = found
        share = jnp.take_along_axis(shares, wide_lane[:SUBLANES], axis=1)
        share = jnp.sum(jnp.where(block == which, share, 0.0), axis=0, keepdims=True)
        picked_ref[r, options : options + SUBLANES, :] = jnp.broadcast_to(share, (SUBLANES, LANES))
        return carry

    each_region(regions, one)
    for b, quota in enumerate(turn_rows(quota_ref[...], options)):
        pull = DUAL_STEP * quota
        shift = duals[b] - pull
        for k in range(options // quarter):
            shift_ref[k, b * quarter : (b + 1) * quarter, :] = shift[k * quarter : (k + 1) * quarter, :]
        alone = duals[b]
        for _ in range(ITERS - 1):
            alone = jnp.maximum(alone - pull, 0.0)
        named = jnp.broadcast_to(counts[b : b + 1, :], alone.shape) > 0.0
        base = jnp.where(named, 0.0, alone) - pull
        for h in range(base_ref.shape[0]):
            base_ref[h, b] = base[h * base_ref.shape[2] : (h + 1) * base_ref.shape[2], :]
    for c in range(slot_ref.shape[0]):
        within = jnp.broadcast_to((slot_ref[c : c + 1, :] & (WIDE - 1)).astype(jnp.float32), (LANES, LANES))
        turned_ref[c * LANES : (c + 1) * LANES, :] = within.astype(jnp.bfloat16).T
    for copy in copies[4:]:
        copy.wait()


def person_kernel(options, rep, last, *refs):
    if last:
        prices_ref, share_ref, turned_ref, slot_ref, cost_ref, primal_ref, fresh_ref, sums_ref, *kept_refs = refs
        regions = share_ref.shape[0]
    else:
        prices_ref, turned_ref, slot_ref, cost_ref, primal_ref, fresh_ref, sums_ref, *kept_refs = refs
        regions = prices_ref.shape[0]
    quarter = options // rep
    rows = slot_ref.shape[0]
    halves = options // SUBLANES
    chunks = regions // CHUNK
    blocks = CHUNK * LANES // WIDE
    groups = rows // SUBLANES
    sent = sums_ref.shape[1]

    def price(d, o):
        if last:
            return prices_ref[o // quarter * regions + d, o % quarter : o % quarter + 1, :]
        return prices_ref[d, o : o + 1, :]

    def operands(c):
        tiles = [slice((h * rows + c) * SUBLANES, (h * rows + c + 1) * SUBLANES) for h in range(halves)]
        x = jnp.concatenate([2.0 * fresh_ref[tile, :] - primal_ref[tile, :] for tile in tiles], axis=0)
        high, low = split_two(x)
        span = slice(c * LANES, (c + 1) * LANES)
        line = slot_ref[c : c + 1, :]
        turned = turned_ref[span, :]
        turned = jnp.concatenate([turned] * (WIDE // LANES), axis=1)
        here = lax.broadcasted_iota(jnp.int32, (PACKED, WIDE), 1).astype(jnp.float32).astype(jnp.bfloat16)
        hot = [
            jnp.where(turned[first : first + PACKED] == here, jnp.bfloat16(1), jnp.bfloat16(0))
            for first in range(0, LANES, PACKED)
        ]
        number = jnp.broadcast_to((line >> WIDE_BITS).astype(jnp.float32), (PACKED, LANES)).astype(jnp.bfloat16)
        return high, low, number, jnp.concatenate(hot, axis=0)

    def partial_sums(chunk, pieces):
        lines = []
        for part in range(2):
            for e in range(blocks):
                mine = jnp.asarray(chunk * blocks + e, jnp.float32).astype(jnp.bfloat16)
                kept = [jnp.where(piece[2] == mine, piece[part], jnp.bfloat16(0)) for piece in pieces]
                lines.append(jnp.concatenate(kept, axis=1))
        hot = jnp.concatenate([piece[3] for piece in pieces], axis=0)
        return jnp.dot(jnp.concatenate(lines, axis=0), hot, preferred_element_type=jnp.float32)

    def hand_on(chunk, total):
        total = total[: blocks * options] + total[blocks * options :]
        for i in range(CHUNK):
            d = chunk * CHUNK + i
            e, h = divmod(i, WIDE // LANES)
            block = total[e * options : (e + 1) * options, h * LANES : (h + 1) * LANES]
            if last:
                share = jnp.where(lax.axis_index("rep") == 0, share_ref[d, options : options + SUBLANES, :], 0.0)
                held = jnp.concatenate([price(d, o) for o in range(options)], axis=0)
                block = DUAL_STEP * block + held * jnp.concatenate([share] * halves, axis=0)
            for k in range(rep):
                first = k * sent % options
                sums_ref[k * regions + d] = block[first : first + sent, :]

    for g in range(groups):
        slot = slot_ref[g * SUBLANES : (g + 1) * SUBLANES, :]
        owner = slot >> LANE_BITS
        within = slot & (LANES - 1)

        def pick(chunk, found):
            near = owner - chunk * CHUNK
            here = (near >= 0) & (near < CHUNK)
            bits = [(near & (1 << i)) == 0 for i in range(CHUNK.bit_length() - 1)]
            picked = []
            for o in range(options):
                level = []
                for d in range(CHUNK):
                    table = jnp.broadcast_to(price(chunk * CHUNK + d, o), (SUBLANES, LANES))
                    level.append(jnp.take_along_axis(table, within, axis=1))
                for low in bits:
                    level = [jnp.where(low, a, b) for a, b in zip(level[::2], level[1::2])]
                picked.append(level[0] if chunks == 1 else jnp.where(here, level[0], found[o]))
            return tuple(picked)

        zero = jnp.zeros((SUBLANES, LANES), jnp.float32)
        adjoint = repeat_chunks(chunks, pick, (zero,) * options)
        places = []
        values = []
        for o in range(options):
            first = ((o // SUBLANES) * rows + g * SUBLANES) * SUBLANES + o % SUBLANES
            at = pl.ds(first, SUBLANES, stride=SUBLANES)
            places.append(at)
            values.append(primal_ref[at, :] - PRIMAL_STEP * (cost_ref[at, :] + adjoint[o]))
        theta = simplex_theta(values)
        for o in range(options):
            fresh_ref[places[o], :] = jnp.maximum(values[o] - theta, 0.0)

    pieces = [operands(c) for c in range(rows)]
    if chunks == 1:
        hand_on(0, partial_sums(0, pieces))
    else:
        for c, piece in enumerate(pieces):
            span = slice(c * LANES, (c + 1) * LANES)
            for ref, value in zip(kept_refs[:3], piece):
                ref[:, span] = value
            kept_refs[3][span, :] = piece[3]

        def add_up(chunk, carry):
            hand_on(chunk, partial_sums(chunk, [[ref[...] for ref in kept_refs]]))
            return carry

        lax.fori_loop(0, chunks, add_up, 0)


def block_sums(arrived_ref, lists_ref):
    regions = lists_ref.shape[0]
    rep = arrived_ref.shape[0] // regions
    options = arrived_ref.shape[1]
    lines = BLOCKS * options
    copies = max(1, SUBLANES // options)
    tall = copies * options
    row = lax.broadcasted_iota(jnp.int32, (tall, CHUNK * LANES), 0) // options

    def add_up(chunk, total):
        sums, hots, numbers = [], [], []
        for i in range(CHUNK):
            r = chunk * CHUNK + i
            x = arrived_ref[r]
            for k in range(1, rep):
                x = x + arrived_ref[k * regions + r]
            sums.append(jnp.concatenate([x] * copies, axis=0))
            block, lane = group_place(lists_ref[pl.ds(r, 1), :])
            hots.append(one_hot(lane, LANES))
            numbers.append(jnp.broadcast_to(block, (tall, LANES)))
        x = jnp.concatenate(sums, axis=1)
        number = jnp.concatenate(numbers, axis=1) - row
        high = x.astype(jnp.bfloat16).astype(jnp.float32)
        left = [
            jnp.where(number == first, part, 0.0) for part in (high, x - high) for first in range(0, BLOCKS, copies)
        ]
        found = product(jnp.concatenate(left, axis=0).astype(jnp.bfloat16), jnp.concatenate(hots, axis=1))
        return total + found[:lines] + found[lines:]

    return repeat_chunks(regions // CHUNK, add_up, jnp.zeros((lines, LANES), jnp.float32))


def middle_kernel(arrived_ref, lists_ref, shift_ref, picked_ref):
    regions = lists_ref.shape[0]
    rep = arrived_ref.shape[0] // regions
    options = arrived_ref.shape[1]
    applied = block_sums(arrived_ref, lists_ref)
    dual = jnp.maximum(shift_ref[lax.axis_index("rep")] + DUAL_STEP * applied, 0.0)
    blocks = [dual[b * options : (b + 1) * options, :] for b in range(BLOCKS)]

    def one(r, carry):
        block, lane = group_place(lists_ref[pl.ds(r, 1), :])
        block = jnp.broadcast_to(block, (options, LANES))
        lane = jnp.broadcast_to(lane, (options, LANES))
        found = jnp.take_along_axis(blocks[0], lane, axis=1)
        for b in range(1, BLOCKS):
            found = jnp.where(block == b, jnp.take_along_axis(blocks[b], lane, axis=1), found)
        for k in range(rep):
            picked_ref[k * regions + r] = found
        return carry

    each_region(regions, one)


def half_kernel(arrived_ref, lists_ref, base_ref, part_ref):
    sent = arrived_ref.shape[1]
    shares = base_ref.shape[0]
    mine = lax.axis_index("rep") % shares
    sums = block_sums(arrived_ref, lists_ref)
    lines = []
    for b in range(BLOCKS):
        block = jnp.maximum(base_ref[mine, b] + sums[b * sent : (b + 1) * sent, :], 0.0)
        whole = jnp.concatenate([jnp.where(mine == h, block, 0.0) for h in range(shares)], axis=0)
        lines.append(whole)
        lines.append(pltpu.roll(whole, LANES // 2, 1))
    part_ref[...] = jnp.concatenate(lines, axis=0).T[: part_ref.shape[0], :]


def write_kernel(fresh_ref, primal_far, sem):
    copy = pltpu.make_async_copy(fresh_ref, primal_far, sem)
    copy.start()
    copy.wait()


def call(kernel, outs, scratch=(), ins=None):
    vmem = pl.BlockSpec(memory_space=pltpu.VMEM)
    hbm = pl.BlockSpec(memory_space=pltpu.HBM)
    params = {} if ins is None else {"in_specs": [hbm if far else vmem for far in ins]}
    return pl.pallas_call(
        kernel,
        out_shape=[jax.ShapeDtypeStruct(shape, kind) for shape, kind, _ in outs],
        out_specs=[hbm if far else vmem for _, _, far in outs],
        scratch_shapes=list(scratch),
        compiler_params=pltpu.CompilerParams(vmem_limit_bytes=VMEM_LIMIT),
        **params,
    )


def far(x):
    return pltpu.with_memory_space_constraint(x, pltpu.HBM)


def local(unit_cost, start_primal, start_dual, quota_bound, person_slot, cell_lists):
    options, persons = unit_cost.shape
    regions = lax.axis_size("region")
    rep = lax.axis_size("rep")
    quarter = options // rep
    groups = quota_bound.shape[0] // options
    rows = persons // LANES
    halves = options // SUBLANES

    def to_tiles(x):
        x = x.reshape(halves, SUBLANES, rows, LANES).transpose(0, 2, 1, 3)
        return x.reshape(options * rows, LANES)

    def from_tiles(x):
        x = x.reshape(halves, rows, SUBLANES, LANES).transpose(0, 2, 1, 3)
        return x.reshape(options, persons)

    def array(*shape, kind=jnp.float32, far=False):
        return (shape, kind, far)

    flat = (groups * options // LANES, LANES)
    tiles = array(options * rows, LANES)
    half = options // 2
    base_rows = array(2, BLOCKS, half, LANES)
    quarters = array(regions * rep, quarter, LANES)
    half_rows = array(regions * rep, half, LANES)
    both = ("rep", "region")
    exchange = functools.partial(lax.all_to_all, split_axis=0, concat_axis=0, tiled=True)

    picked, shift, base, lists, slots, cost, primal, turned = call(
        functools.partial(first_kernel, options),
        (
            array(regions, options + SUBLANES, LANES),
            array(rep, BLOCKS * quarter, LANES),
            base_rows,
            array(regions, LANES, kind=jnp.int32),
            array(rows, LANES, kind=jnp.int32),
            tiles,
            tiles,
            array(persons, LANES, kind=jnp.bfloat16),
        ),
        (pltpu.VMEM(flat, jnp.float32), pltpu.VMEM(flat, jnp.float32), pltpu.SemaphoreType.DMA((6,))),
        (True,) * 6,
    )(
        far(cell_lists[0]),
        far(start_dual.reshape(flat)),
        far(quota_bound.reshape(flat)),
        far(person_slot.reshape(rows, LANES)),
        far(to_tiles(unit_cost)),
        far(to_tiles(start_primal)),
    )
    first_prices = exchange(picked, "region")
    scratch = ()
    if regions > CHUNK:
        kept = ((options, persons), (options, persons), (PACKED, persons), (persons, WIDE))
        scratch = tuple(pltpu.VMEM(shape, jnp.bfloat16) for shape in kept)
    primal, sums = call(functools.partial(person_kernel, options, rep, False), (tiles, quarters), scratch)(
        first_prices, turned, slots, cost, primal
    )
    arrived = exchange(sums, both)
    (picked,) = call(middle_kernel, (quarters,))(arrived, lists, shift)
    prices = exchange(picked, both)
    primal, sums = call(functools.partial(person_kernel, options, rep, True), (tiles, half_rows), scratch)(
        prices, first_prices, turned, slots, cost, primal
    )
    arrived = exchange(sums, both)
    (part,) = call(half_kernel, (array(*flat),))(arrived, lists, base)
    other = lax.ppermute(part, "rep", [(k, k ^ 1) for k in range(rep)])
    (primal,) = call(write_kernel, (array(*tiles[0], far=True),), (pltpu.SemaphoreType.DMA,))(primal)
    dual = part + other
    return (from_tiles(primal), dual.reshape(-1))


def solution(mesh):
    placed = (
        P(None, ("region", "rep")),
        P(None, ("region", "rep")),
        P("region"),
        P("region"),
        P(("region", "rep")),
        P("region", None, None),
    )
    return jax.shard_map(
        local,
        mesh=mesh,
        in_specs=placed,
        out_specs=(P(None, ("region", "rep")), P("region")),
        check_vma=False,
    )
```

```python
import functools

import jax
import jax.numpy as jnp
from jax import lax
from jax.experimental import pallas as pl
from jax.experimental.pallas import tpu as pltpu
from jax.sharding import PartitionSpec as P

ITERS = 2
BISECT = 30
PRIMAL_STEP = 0.5
DUAL_STEP = 0.25
LANES = 128
SUBLANES = 8
CHUNK = 8
PACKED = 16
WIDE = 256
LANE_BITS = LANES.bit_length() - 1
WIDE_BITS = WIDE.bit_length() - 1
BLOCKS = 4
VMEM_LIMIT = 48 * 1024 * 1024


def sorting_network(count):
    pairs = []
    p = 1
    while p < count:
        k = p
        while k >= 1:
            for j in range(k % p, count - k, 2 * k):
                for i in range(min(k, count - j - k)):
                    if (i + j) // (2 * p) == (i + j + k) // (2 * p):
                        pairs.append((i + j, i + j + k))
            k //= 2
        p *= 2
    return pairs


def repeat_chunks(total, body, init):
    if total == 1:
        return body(0, init)
    return lax.fori_loop(0, total, body, init)


def simplex_theta(values):
    ranked = list(values)
    for a, b in sorting_network(len(values)):
        ranked[a], ranked[b] = jnp.maximum(ranked[a], ranked[b]), jnp.minimum(ranked[a], ranked[b])
    largest = ranked[0]
    total = jnp.zeros_like(largest)
    best = jnp.full_like(largest, -1.0)
    for k in range(1, len(values)):
        total = total + (ranked[k] - largest)
        best = jnp.maximum(best, (total - 1.0) * (1.0 / (k + 1)))
    cells = float(2**BISECT)
    step = jnp.maximum(jnp.ceil((best + 1.0) * cells), 1.0) - 0.5
    return (largest - 1.0) + step * (1.0 / cells)


def split_two(x):
    high = x.astype(jnp.bfloat16)
    low = (x - high.astype(jnp.float32)).astype(jnp.bfloat16)
    return high, low


def one_hot(index, count):
    wide = jnp.broadcast_to(index.astype(jnp.float32), (PACKED, index.shape[1])).astype(jnp.bfloat16)
    lines = []
    for first in range(0, count, PACKED):
        here = lax.broadcasted_iota(jnp.int32, wide.shape, 0) + first
        hit = wide == here.astype(jnp.float32).astype(jnp.bfloat16)
        lines.append(jnp.where(hit, jnp.bfloat16(1), jnp.bfloat16(0)))
    return jnp.concatenate(lines, axis=0)


def product(left, right):
    return lax.dot_general(left, right, (((1,), (1,)), ((), ())), preferred_element_type=jnp.float32)


def group_place(lists):
    return (lists & (SUBLANES - 1)) >> 1, (lists & 1) * (LANES // 2) + (lists >> 3)


def each_region(regions, body):
    if regions <= CHUNK:
        for r in range(regions):
            body(r, 0)
    else:
        lax.fori_loop(0, regions, body, 0)


def turn_rows(flat, options):
    turned = jnp.concatenate([flat, flat], axis=0).T
    left = lax.broadcasted_iota(jnp.int32, (options, LANES), 1) < LANES // 2
    pairs = [turned[i * options : (i + 1) * options, :] for i in range(2 * BLOCKS)]
    return [jnp.where(left, pairs[2 * b], pairs[2 * b + 1]) for b in range(BLOCKS)]


def first_kernel(options, *refs):
    far, outs, (dual_ref, quota_ref, sems) = refs[:6], refs[6:15], refs[15:]
    picked_ref, shift_ref, base_ref, lists_ref, slot_ref, cost_ref, primal_ref, turned_ref, lanes_ref = outs
    targets = (lists_ref, dual_ref, quota_ref, slot_ref, cost_ref, primal_ref)
    copies = [
        pltpu.make_async_copy(source, target, sems.at[i]) for i, (source, target) in enumerate(zip(far, targets))
    ]
    for copy in copies:
        copy.start()
    regions = lists_ref.shape[0]
    quarter = shift_ref.shape[1] // BLOCKS
    there = lax.broadcasted_iota(jnp.int32, (LANES, LANES), 0)
    which = lax.broadcasted_iota(jnp.int32, (SUBLANES, LANES), 0)

    def count_up(chunk, total):
        lefts, rights = [], []
        for i in range(CHUNK):
            block, lane = group_place(lists_ref[pl.ds(chunk * CHUNK + i, 1), :])
            lefts.append(jnp.where(block == which, 1.0, 0.0).astype(jnp.bfloat16))
            rights.append(one_hot(lane, LANES))
        return total + product(jnp.concatenate(lefts, axis=1), jnp.concatenate(rights, axis=1))

    for copy in copies[:4]:
        copy.wait()
    counts = repeat_chunks(regions // CHUNK, count_up, jnp.zeros((SUBLANES, LANES), jnp.float32))
    shares = 1.0 / jnp.maximum(counts, 1.0)
    duals = turn_rows(dual_ref[...], options)

    def one(r, carry):
        block, lane = group_place(lists_ref[pl.ds(r, 1), :])
        wide_block = jnp.broadcast_to(block, (options, LANES))
        wide_lane = jnp.broadcast_to(lane, (options, LANES))
        found = jnp.take_along_axis(duals[0], wide_lane, axis=1)
        for b in range(1, BLOCKS):
            found = jnp.where(wide_block == b, jnp.take_along_axis(duals[b], wide_lane, axis=1), found)
        picked_ref[r, 0:options, :] = found
        share = jnp.take_along_axis(shares, wide_lane[:SUBLANES], axis=1)
        share = jnp.sum(jnp.where(block == which, share, 0.0), axis=0, keepdims=True)
        picked_ref[r, options : options + SUBLANES, :] = jnp.broadcast_to(share, (SUBLANES, LANES))
        lanes_ref[r] = jnp.broadcast_to(lane.astype(jnp.float32), (LANES, LANES)).astype(jnp.bfloat16).T
        return carry

    each_region(regions, one)
    for b, quota in enumerate(turn_rows(quota_ref[...], options)):
        pull = DUAL_STEP * quota
        shift = duals[b] - pull
        for k in range(options // quarter):
            shift_ref[k, b * quarter : (b + 1) * quarter, :] = shift[k * quarter : (k + 1) * quarter, :]
        alone = duals[b]
        for _ in range(ITERS - 1):
            alone = jnp.maximum(alone - pull, 0.0)
        named = jnp.broadcast_to(counts[b : b + 1, :], alone.shape) > 0.0
        base = jnp.where(named, 0.0, alone) - pull
        for h in range(base_ref.shape[0]):
            base_ref[h, b] = base[h * base_ref.shape[2] : (h + 1) * base_ref.shape[2], :]
    for c in range(slot_ref.shape[0]):
        within = jnp.broadcast_to((slot_ref[c : c + 1, :] & (WIDE - 1)).astype(jnp.float32), (LANES, LANES))
        turned_ref[c * LANES : (c + 1) * LANES, :] = within.astype(jnp.bfloat16).T
    for copy in copies[4:]:
        copy.wait()


def person_kernel(options, rep, last, *refs):
    if last:
        prices_ref, share_ref, turned_ref, slot_ref, cost_ref, primal_ref, fresh_ref, sums_ref, *kept_refs = refs
        regions = share_ref.shape[0]
    else:
        prices_ref, turned_ref, slot_ref, cost_ref, primal_ref, fresh_ref, sums_ref, *kept_refs = refs
        regions = prices_ref.shape[0]
    quarter = options // rep
    rows = slot_ref.shape[0]
    halves = options // SUBLANES
    chunks = regions // CHUNK
    blocks = CHUNK * LANES // WIDE
    groups = rows // SUBLANES
    sent = sums_ref.shape[1]

    def price(d, o):
        if last:
            return prices_ref[o // quarter * regions + d, o % quarter : o % quarter + 1, :]
        return prices_ref[d, o : o + 1, :]

    def operands(c):
        tiles = [slice((h * rows + c) * SUBLANES, (h * rows + c + 1) * SUBLANES) for h in range(halves)]
        x = jnp.concatenate([2.0 * fresh_ref[tile, :] - primal_ref[tile, :] for tile in tiles], axis=0)
        high, low = split_two(x)
        span = slice(c * LANES, (c + 1) * LANES)
        line = slot_ref[c : c + 1, :]
        turned = turned_ref[span, :]
        turned = jnp.concatenate([turned] * (WIDE // LANES), axis=1)
        here = lax.broadcasted_iota(jnp.int32, (PACKED, WIDE), 1).astype(jnp.float32).astype(jnp.bfloat16)
        hot = [
            jnp.where(turned[first : first + PACKED] == here, jnp.bfloat16(1), jnp.bfloat16(0))
            for first in range(0, LANES, PACKED)
        ]
        number = jnp.broadcast_to((line >> WIDE_BITS).astype(jnp.float32), (PACKED, LANES)).astype(jnp.bfloat16)
        return high, low, number, jnp.concatenate(hot, axis=0)

    def partial_sums(chunk, pieces):
        lines = []
        for part in range(2):
            for e in range(blocks):
                mine = jnp.asarray(chunk * blocks + e, jnp.float32).astype(jnp.bfloat16)
                kept = [jnp.where(piece[2] == mine, piece[part], jnp.bfloat16(0)) for piece in pieces]
                lines.append(jnp.concatenate(kept, axis=1))
        hot = jnp.concatenate([piece[3] for piece in pieces], axis=0)
        return jnp.dot(jnp.concatenate(lines, axis=0), hot, preferred_element_type=jnp.float32)

    def hand_on(chunk, total):
        total = total[: blocks * options] + total[blocks * options :]
        for i in range(CHUNK):
            d = chunk * CHUNK + i
            e, h = divmod(i, WIDE // LANES)
            block = total[e * options : (e + 1) * options, h * LANES : (h + 1) * LANES]
            if last:
                share = jnp.where(lax.axis_index("rep") == 0, share_ref[d, options : options + SUBLANES, :], 0.0)
                held = jnp.concatenate([price(d, o) for o in range(options)], axis=0)
                block = DUAL_STEP * block + held * jnp.concatenate([share] * halves, axis=0)
            for k in range(rep):
                first = k * sent % options
                sums_ref[k * regions + d] = block[first : first + sent, :]

    for g in range(groups):
        slot = slot_ref[g * SUBLANES : (g + 1) * SUBLANES, :]
        owner = slot >> LANE_BITS
        within = slot & (LANES - 1)

        def pick(chunk, found):
            near = owner - chunk * CHUNK
            here = (near >= 0) & (near < CHUNK)
            bits = [(near & (1 << i)) == 0 for i in range(CHUNK.bit_length() - 1)]
            picked = []
            for o in range(options):
                level = []
                for d in range(CHUNK):
                    table = jnp.broadcast_to(price(chunk * CHUNK + d, o), (SUBLANES, LANES))
                    level.append(jnp.take_along_axis(table, within, axis=1))
                for low in bits:
                    level = [jnp.where(low, a, b) for a, b in zip(level[::2], level[1::2])]
                picked.append(level[0] if chunks == 1 else jnp.where(here, level[0], found[o]))
            return tuple(picked)

        zero = jnp.zeros((SUBLANES, LANES), jnp.float32)
        adjoint = repeat_chunks(chunks, pick, (zero,) * options)
        places = []
        values = []
        for o in range(options):
            first = ((o // SUBLANES) * rows + g * SUBLANES) * SUBLANES + o % SUBLANES
            at = pl.ds(first, SUBLANES, stride=SUBLANES)
            places.append(at)
            values.append(primal_ref[at, :] - PRIMAL_STEP * (cost_ref[at, :] + adjoint[o]))
        theta = simplex_theta(values)
        for o in range(options):
            fresh_ref[places[o], :] = jnp.maximum(values[o] - theta, 0.0)

    pieces = [operands(c) for c in range(rows)]
    if chunks == 1:
        hand_on(0, partial_sums(0, pieces))
    else:
        for c, piece in enumerate(pieces):
            span = slice(c * LANES, (c + 1) * LANES)
            for ref, value in zip(kept_refs[:3], piece):
                ref[:, span] = value
            kept_refs[3][span, :] = piece[3]

        def add_up(chunk, carry):
            hand_on(chunk, partial_sums(chunk, [[ref[...] for ref in kept_refs]]))
            return carry

        lax.fori_loop(0, chunks, add_up, 0)


def block_sums(arrived_ref, lists_ref, lanes_ref):
    regions = lists_ref.shape[0]
    rep = arrived_ref.shape[0] // regions
    options = arrived_ref.shape[1]
    lines = BLOCKS * options
    copies = max(1, SUBLANES // options)
    tall = copies * options
    row = lax.broadcasted_iota(jnp.int32, (tall, CHUNK * LANES), 0) // options

    here = lax.broadcasted_iota(jnp.int32, (PACKED, LANES), 1).astype(jnp.float32).astype(jnp.bfloat16)

    def add_up(chunk, total):
        sums, hots, numbers = [], [], []
        for i in range(CHUNK):
            r = chunk * CHUNK + i
            x = arrived_ref[r]
            for k in range(1, rep):
                x = x + arrived_ref[k * regions + r]
            sums.append(jnp.concatenate([x] * copies, axis=0))
            block, _ = group_place(lists_ref[pl.ds(r, 1), :])
            turned = lanes_ref[r]
            for first in range(0, LANES, PACKED):
                hit = turned[first : first + PACKED] == here
                hots.append(jnp.where(hit, jnp.bfloat16(1), jnp.bfloat16(0)))
            numbers.append(jnp.broadcast_to(block, (tall, LANES)))
        x = jnp.concatenate(sums, axis=1)
        number = jnp.concatenate(numbers, axis=1) - row
        high = x.astype(jnp.bfloat16).astype(jnp.float32)
        left = [
            jnp.where(number == first, part, 0.0) for part in (high, x - high) for first in range(0, BLOCKS, copies)
        ]
        left = jnp.concatenate(left, axis=0).astype(jnp.bfloat16)
        found = jnp.dot(left, jnp.concatenate(hots, axis=0), preferred_element_type=jnp.float32)
        return total + found[:lines] + found[lines:]

    return repeat_chunks(regions // CHUNK, add_up, jnp.zeros((lines, LANES), jnp.float32))


def middle_kernel(arrived_ref, lists_ref, lanes_ref, shift_ref, picked_ref):
    regions = lists_ref.shape[0]
    rep = arrived_ref.shape[0] // regions
    options = arrived_ref.shape[1]
    applied = block_sums(arrived_ref, lists_ref, lanes_ref)
    dual = jnp.maximum(shift_ref[lax.axis_index("rep")] + DUAL_STEP * applied, 0.0)
    blocks = [dual[b * options : (b + 1) * options, :] for b in range(BLOCKS)]

    def one(r, carry):
        block, lane = group_place(lists_ref[pl.ds(r, 1), :])
        block = jnp.broadcast_to(block, (options, LANES))
        lane = jnp.broadcast_to(lane, (options, LANES))
        found = jnp.take_along_axis(blocks[0], lane, axis=1)
        for b in range(1, BLOCKS):
            found = jnp.where(block == b, jnp.take_along_axis(blocks[b], lane, axis=1), found)
        for k in range(rep):
            picked_ref[k * regions + r] = found
        return carry

    each_region(regions, one)


def half_kernel(arrived_ref, lists_ref, lanes_ref, base_ref, part_ref):
    sent = arrived_ref.shape[1]
    shares = base_ref.shape[0]
    mine = lax.axis_index("rep") % shares
    sums = block_sums(arrived_ref, lists_ref, lanes_ref)
    lines = []
    for b in range(BLOCKS):
        block = jnp.maximum(base_ref[mine, b] + sums[b * sent : (b + 1) * sent, :], 0.0)
        whole = jnp.concatenate([jnp.where(mine == h, block, 0.0) for h in range(shares)], axis=0)
        lines.append(whole)
        lines.append(pltpu.roll(whole, LANES // 2, 1))
    part_ref[...] = jnp.concatenate(lines, axis=0).T[: part_ref.shape[0], :]


def write_kernel(fresh_ref, primal_far, sem):
    copy = pltpu.make_async_copy(fresh_ref, primal_far, sem)
    copy.start()
    copy.wait()


def call(kernel, outs, scratch=(), ins=None):
    vmem = pl.BlockSpec(memory_space=pltpu.VMEM)
    hbm = pl.BlockSpec(memory_space=pltpu.HBM)
    params = {} if ins is None else {"in_specs": [hbm if far else vmem for far in ins]}
    return pl.pallas_call(
        kernel,
        out_shape=[jax.ShapeDtypeStruct(shape, kind) for shape, kind, _ in outs],
        out_specs=[hbm if far else vmem for _, _, far in outs],
        scratch_shapes=list(scratch),
        compiler_params=pltpu.CompilerParams(vmem_limit_bytes=VMEM_LIMIT),
        **params,
    )


def far(x):
    return pltpu.with_memory_space_constraint(x, pltpu.HBM)


def local(unit_cost, start_primal, start_dual, quota_bound, person_slot, cell_lists):
    options, persons = unit_cost.shape
    regions = lax.axis_size("region")
    rep = lax.axis_size("rep")
    quarter = options // rep
    groups = quota_bound.shape[0] // options
    rows = persons // LANES
    halves = options // SUBLANES

    def to_tiles(x):
        x = x.reshape(halves, SUBLANES, rows, LANES).transpose(0, 2, 1, 3)
        return x.reshape(options * rows, LANES)

    def from_tiles(x):
        x = x.reshape(halves, rows, SUBLANES, LANES).transpose(0, 2, 1, 3)
        return x.reshape(options, persons)

    def array(*shape, kind=jnp.float32, far=False):
        return (shape, kind, far)

    flat = (groups * options // LANES, LANES)
    tiles = array(options * rows, LANES)
    half = options // 2
    base_rows = array(2, BLOCKS, half, LANES)
    quarters = array(regions * rep, quarter, LANES)
    half_rows = array(regions * rep, half, LANES)
    both = ("rep", "region")
    exchange = functools.partial(lax.all_to_all, split_axis=0, concat_axis=0, tiled=True)

    picked, shift, base, lists, slots, cost, primal, turned, lanes = call(
        functools.partial(first_kernel, options),
        (
            array(regions, options + SUBLANES, LANES),
            array(rep, BLOCKS * quarter, LANES),
            base_rows,
            array(regions, LANES, kind=jnp.int32),
            array(rows, LANES, kind=jnp.int32),
            tiles,
            tiles,
            array(persons, LANES, kind=jnp.bfloat16),
            array(regions, LANES, LANES, kind=jnp.bfloat16),
        ),
        (pltpu.VMEM(flat, jnp.float32), pltpu.VMEM(flat, jnp.float32), pltpu.SemaphoreType.DMA((6,))),
        (True,) * 6,
    )(
        far(cell_lists[0]),
        far(start_dual.reshape(flat)),
        far(quota_bound.reshape(flat)),
        far(person_slot.reshape(rows, LANES)),
        far(to_tiles(unit_cost)),
        far(to_tiles(start_primal)),
    )
    first_prices = exchange(picked, "region")
    scratch = ()
    if regions > CHUNK:
        kept = ((options, persons), (options, persons), (PACKED, persons), (persons, WIDE))
        scratch = tuple(pltpu.VMEM(shape, jnp.bfloat16) for shape in kept)
    primal, sums = call(functools.partial(person_kernel, options, rep, False), (tiles, quarters), scratch)(
        first_prices, turned, slots, cost, primal
    )
    arrived = exchange(sums, both)
    (picked,) = call(middle_kernel, (quarters,))(arrived, lists, lanes, shift)
    prices = exchange(picked, both)
    primal, sums = call(functools.partial(person_kernel, options, rep, True), (tiles, half_rows), scratch)(
        prices, first_prices, turned, slots, cost, primal
    )
    arrived = exchange(sums, both)
    (part,) = call(half_kernel, (array(*flat),))(arrived, lists, lanes, base)
    other = lax.ppermute(part, "rep", [(k, k ^ 1) for k in range(rep)])
    (primal,) = call(write_kernel, (array(*tiles[0], far=True),), (pltpu.SemaphoreType.DMA,))(primal)
    dual = part + other
    return (from_tiles(primal), dual.reshape(-1))


def solution(mesh):
    placed = (
        P(None, ("region", "rep")),
        P(None, ("region", "rep")),
        P("region"),
        P("region"),
        P(("region", "rep")),
        P("region", None, None),
    )
    return jax.shard_map(
        local,
        mesh=mesh,
        in_specs=placed,
        out_specs=(P(None, ("region", "rep")), P("region")),
        check_vma=False,
    )
```
